128 devices in a mesh: section: 2 (over z_lo), dp: 32 (over x, y, core), tensor: 2 (over z_hi).
Axes of the slice: x: 4, y: 4, z: 4 (z_hi: 2, z_lo: 2; z = z_hi * 2 + z_lo), core: 2. Of those that a mesh axis runs over, the one named last changes fastest.
Arguments:
- ends: bfloat16 [2, 2, 32, 192, 1024], P('section', None, 'dp'), may hold values from -6 to 6
- lengths: int32 [2, 32], P(None, 'dp'), may hold values from 48 to 192
- w_qkv: bfloat16 [2, 1024, 3, 1024], P('section', 'dp', None, 'tensor'), may hold values from -0.1875 to 0.1875
- w_out: bfloat16 [2, 1024, 1024], P('section', 'tensor', 'dp'), may hold values from -2 to 2
- w_up: bfloat16 [2, 1024, 4096], P('section', 'dp', 'tensor'), may hold values from -0.1875 to 0.1875
- w_down: bfloat16 [2, 4096, 1024], P('section', 'tensor', 'dp'), may hold values from -0.09375 to 0.09375
- gains: bfloat16 [2, 2, 1024], P('section', None, 'dp'), may hold values from 0.5 to 1.5
- shifts: bfloat16 [2, 4, 1024], P('section', None, 'dp'), may hold values from -1.796875 to 1.796875
- b_qv: bfloat16 [2, 2, 2, 512], P('section', None, 'tensor', 'dp'), may hold values from -1.796875 to 1.796875
- b_ff: bfloat16 [2, 2, 2048], P('section', 'tensor', 'dp'), may hold values from -1.796875 to 1.796875
Outputs:
- ends_out: bfloat16 [2, 2, 32, 192, 1024], P('section', None, 'dp')
- grad_qkv: float32 [2, 1024, 3, 1024], P('section', 'dp', None, 'tensor')
- grad_out: float32 [2, 1024, 1024], P('section', 'tensor', 'dp')
- grad_up: float32 [2, 1024, 4096], P('section', 'dp', 'tensor')
- grad_down: float32 [2, 4096, 1024], P('section', 'tensor', 'dp')
- grad_gains: float32 [2, 2, 1024], P('section', None, 'dp')
- grad_shifts: float32 [2, 4, 1024], P('section', None, 'dp')
- grad_bqv: float32 [2, 2, 2, 512], P('section', None, 'tensor', 'dp')
- grad_bff: float32 [2, 2, 2048], P('section', 'tensor', 'dp')
The draws below stay inside these ranges and needn't reach their ends.
All inputs are finite; a program needn't handle non-finite values.
Results may differ from the reference program's by a relative error of at most 0.025.
Values may be sent and summed in bfloat16 or wider, within the bound.
A program may use at most 192 MiB of HBM per device.

```python
import jax
import jax.numpy as jnp
from jax import lax

D = 1024
H = 16
HD = 64
FF = 4096
SEQ = 192
MB = 2
SEQS = 32
N_TENSOR = 2


def set_ends(array, key, smallest, top_value):
    shape = array.shape
    place = [jax.random.randint(jax.random.fold_in(key, axis), (), 0, shape[axis]) for axis in range(len(shape))]
    array = array.at[tuple(place)].set(smallest)
    longest = shape.index(max(shape))
    place[longest] = (place[longest] + 1) % shape[longest]
    return array.at[tuple(place)].set(top_value)


def steps_of(key, shape, split, low, largest):
    def one(dim, shards_of):
        steps = jax.random.uniform(jax.random.fold_in(jax.random.fold_in(key, 6), dim), (shards_of,), jnp.float32, low / len(split), largest / len(split))
        return jnp.repeat(jnp.exp(steps), shape[dim] // shards_of).reshape((-1,) + (1,) * (len(shape) - dim - 1))

    loudness = one(*split[0])
    for cut in split[1:]:
        loudness = loudness * one(*cut)
    return loudness


def bell_draw(stream_key, dims, width, reach, cuts=(), kind=jnp.bfloat16):
    drawn = jax.random.normal(stream_key, dims, jnp.float32) * width
    if len(cuts) > 0:
        drawn = steps_of(stream_key, dims, cuts, -0.22, 0.18) * drawn
    return jnp.clip(drawn, min=-reach, max=reach).astype(kind)


def setup_inputs(seed: int = 0) -> dict:
    key_list = jax.random.split(jax.random.key(seed), 11)
    ends = bell_draw(key_list[0], (2, MB, SEQS, SEQ, D), 1.0, 6.0, ((0, 2), (2, 32)))
    lengths = set_ends(jax.random.randint(key_list[1], (MB, SEQS), SEQ // 4, SEQ + 1), jax.random.fold_in(key_list[1], 1), SEQ // 4, SEQ).astype(jnp.int32)
    w_qkv = bell_draw(key_list[2], (2, D, 3, D), D ** -0.5, 0.1875, ((0, 2), (1, 32), (3, 2)))
    w_out = bell_draw(key_list[3], (2, D, D), (max(2 * D // SEQ, 1)) ** -0.5, 2.0, ((0, 2), (1, 2), (2, 32)))
    w_up = bell_draw(key_list[4], (2, D, FF), D ** -0.5, 0.1875, ((0, 2), (1, 32), (2, 2)))
    w_down = bell_draw(key_list[5], (2, FF, D), FF ** -0.5, 0.09375, ((0, 2), (1, 2), (2, 32)))
    gains = jnp.clip(1.0 + 0.1 * jax.random.normal(key_list[6], (2, 2, D), jnp.float32), 0.5, 1.5).astype(jnp.bfloat16)
    shifts = bell_draw(key_list[7], (2, 4, D), 0.3, 1.796875, ((0, 2), (2, 32)))
    b_qv = bell_draw(key_list[8], (2, 2, N_TENSOR, D // N_TENSOR), 0.3, 1.796875, ((0, 2), (2, 2), (3, 32)))
    b_ff = bell_draw(key_list[9], (2, N_TENSOR, FF // N_TENSOR), 0.3, 1.796875, ((0, 2), (1, 2), (2, 32)))
    return dict(ends=ends, lengths=lengths, w_qkv=w_qkv, w_out=w_out, w_up=w_up, w_down=w_down, gains=gains, shifts=shifts, b_qv=b_qv, b_ff=b_ff)


epsilon = 1e-05
highest = lax.Precision.HIGHEST

@jax.custom_vjp
def low(v):
    return lax.optimization_barrier(v.astype(jnp.bfloat16)).astype(jnp.float32)

@jax.custom_vjp
def low_back(v):
    return v

def low_keep(v):
    return (low(v), None)

def low_pass(kept, grad):
    return (grad,)

def back_keep(v):
    return (v, None)

def back_low(kept, grad):
    return (low(grad),)
low.defvjp(low_keep, low_pass)
low_back.defvjp(back_keep, back_low)

def normalize_ref(values, gain, shift):
    centred = values - lax.optimization_barrier(jnp.mean(values, -1, keepdims=True))
    variance = lax.optimization_barrier(jnp.mean(centred * centred, -1, keepdims=True))
    return centred * lax.rsqrt(variance + epsilon) * gain + shift

def softmax_rows(scores):
    row_max = lax.optimization_barrier(jnp.max(scores, -1, keepdims=True))
    powers = jnp.exp(scores - row_max)
    return powers / lax.optimization_barrier(jnp.sum(powers, -1, keepdims=True))

def encoder_layer(layer_in, weights, valid):
    w_qkv, w_out, w_up, w_down, gains, shifts, b_qv, b_ff = weights
    batch_rows, seq_len = (layer_in.shape[0], layer_in.shape[1])
    head_shape = (batch_rows, seq_len, H, HD)
    projected = jnp.einsum('bsd,dkh->bskh', layer_in, w_qkv, precision=highest)
    queries = low(low_back(projected[:, :, 0] + b_qv[0]))
    keys_rows = low(low_back(projected[:, :, 1]))
    values = low(low_back(projected[:, :, 2] + b_qv[1]))
    scores = jnp.einsum('bqhe,bkhe->bhqk', queries.reshape(head_shape), keys_rows.reshape(head_shape), precision=highest) * HD ** (-0.5)
    scores = jnp.where(valid[:, None, None, :], low_back(scores), -1000000000.0)
    probs = low(softmax_rows(scores))
    context = jnp.einsum('bhqk,bkhe->bqhe', probs, values.reshape(head_shape), precision=highest)
    context = low(low_back(context.reshape(batch_rows, seq_len, D)))
    attended = low_back(jnp.einsum('bsh,hd->bsd', context, w_out, precision=highest)) + shifts[0]
    hidden_in = normalize_ref(layer_in + attended, gains[0], shifts[1])
    upward = low_back(jnp.einsum('bsd,df->bsf', low(hidden_in), w_up, precision=highest) + b_ff)
    activated = low(jax.nn.gelu(upward, approximate=False))
    downward = low_back(jnp.einsum('bsf,fd->bsd', activated, w_down, precision=highest)) + shifts[2]
    result = normalize_ref(hidden_in + downward, gains[1], shifts[3])
    return low(low_back(result))

def reference(ends, lengths, w_qkv, w_out, w_up, w_down, gains, shifts, b_qv, b_ff):
    weights = (w_qkv.astype(jnp.float32), w_out.astype(jnp.float32), w_up.astype(jnp.float32), w_down.astype(jnp.float32), gains.astype(jnp.float32), shifts.astype(jnp.float32), b_qv.astype(jnp.float32).reshape(2, 2, D), b_ff.astype(jnp.float32).reshape(2, FF))
    positions = jnp.arange(SEQ, dtype=jnp.int32)

    def step(totals, item):
        inputs_mb, cotangent, length_mb = item
        valid = positions[None, :] < length_mb[:, None]

        def stacked(layer_in, weights_in):
            for section_num in range(2):
                layer_in = encoder_layer(layer_in, tuple((w[section_num] for w in weights_in)), valid)
            return layer_in
        result, backward = jax.vjp(stacked, inputs_mb.astype(jnp.float32), weights)
        grad_in, grad_weights = backward(cotangent.astype(jnp.float32))
        totals = jax.tree.map(jnp.add, totals, grad_weights)
        return (totals, (grad_in.astype(jnp.bfloat16), result.astype(jnp.bfloat16)))
    zeros = jax.tree.map(jnp.zeros_like, weights)
    totals, (grads_in, results) = lax.scan(step, zeros, (ends[0], ends[1], lengths))
    ends_out = jnp.stack([grads_in, results])
    return (ends_out, totals[0], totals[1], totals[2], totals[3], totals[4], totals[5], totals[6].reshape(2, 2, N_TENSOR, D // N_TENSOR), totals[7].reshape(2, N_TENSOR, FF // N_TENSOR))
```

```python
from functools import partial

import jax
import jax.numpy as jnp
from jax import lax
from jax.experimental import pallas as pl
from jax.experimental.pallas import tpu as pltpu
from jax.sharding import PartitionSpec as P

HD = 64
epsilon = 1e-05

HALF_A = 3200
OFFSETS = (0, 3, 1, 2)
MESH = pl.DeviceIdType.MESH


def place():
    d = lax.axis_index("dp")
    return lax.div(d, 8), lax.rem(lax.div(d, 2), 4), lax.rem(d, 2), lax.axis_index("tensor")


def dp_at(x, y, c):
    return (x * 4 + y) * 2 + c


def beside(h, phase, step, x, y, c):
    if (h == 0) == (phase == 1):
        return {"dp": dp_at(lax.rem(x + step, 4), y, c)}
    return {"dp": dp_at(x, lax.rem(y + step, 4), c)}


def meet(x, y, c, t):
    barrier = pltpu.get_barrier_semaphore()
    partners = [
        {"dp": dp_at(lax.rem(x + 1, 4), y, c)},
        {"dp": dp_at(lax.rem(x + 3, 4), y, c)},
        {"dp": dp_at(x, lax.rem(y + 1, 4), c)},
        {"dp": dp_at(x, lax.rem(y + 3, 4), c)},
        {"dp": dp_at(x, y, 1 - c)},
        {"tensor": 1 - t},
    ]
    for partner in partners:
        pl.semaphore_signal(barrier, inc=1, device_id=partner, device_id_type=MESH)
    pl.semaphore_wait(barrier, len(partners))


class Sender:
    def __init__(self, send_sems, recv_sems):
        self.send_sems, self.recv_sems, self.copies = send_sems, recv_sems, []

    def __call__(self, src, dst, where):
        i = len(self.copies)
        copy = pltpu.make_async_remote_copy(
            src_ref=src,
            dst_ref=dst,
            send_sem=self.send_sems.at[i],
            recv_sem=self.recv_sems.at[i],
            device_id=where,
            device_id_type=MESH,
        )
        copy.start()
        self.copies.append(copy)
        return copy

    def finish(self):
        for copy in self.copies:
            copy.wait_send()


N_GATHER = 143


def gather_kernel(shard, out, local_sem, send_sems, recv_sems):
    x, y, c, t = place()
    cols = shard.shape[-1]
    part_a, part_b = pl.ds(0, HALF_A), pl.ds(HALF_A, cols - HALF_A)
    meet(x, y, c, t)
    send = Sender(send_sems, recv_sems)
    sibling = {"dp": dp_at(x, y, 1 - c)}
    own = out.at[t, x, y, c]
    local = pltpu.make_async_copy(shard, own, local_sem)
    local.start()
    from_partner = send(shard, own, {"tensor": 1 - t})
    to_sibling = [send(shard, own, sibling)]

    def block(k, h, ja, jb):
        a, b = OFFSETS[ja], OFFSETS[jb]
        dx, dy = (a, b) if h == 0 else (b, a)
        return out.at[t if k == 0 else 1 - t, lax.rem(x + dx, 4), lax.rem(y + dy, 4), c, h]

    def both(k, h, phase, ja):
        dst = block(k, h, ja, 0)
        src = shard.at[h] if (k == 0 and ja == 0) else dst
        return (
            send(src, dst, beside(h, phase, 1, x, y, c)),
            send(src, dst, beside(h, phase, 3, x, y, c)),
        )

    def take(k, h, phase, ja, pair):
        onward = []
        for copy, j, part, step in ((pair[0], 1, part_a, 1), (pair[1], 2, part_b, 3)):
            copy.wait_recv()
            here = block(k, h, *((j, 0) if phase == 1 else (ja, j)))
            onward.append(send(here.at[:, part], here.at[:, part], beside(h, phase, step, x, y, c)))
            to_sibling.append(send(here, here, sibling))
        return onward

    first, second = {}, {}

    def begin(k):
        for h in (0, 1):
            first[k, h] = both(k, h, 1, 0)
        for h in (0, 1):
            second[k, h, 0] = both(k, h, 2, 0)

    begin(0)
    from_partner.wait_recv()
    begin(1)
    mate = out.at[1 - t, x, y, c]
    to_sibling.append(send(mate, mate, sibling))
    for k in (0, 1):
        onward = {}
        for h in (0, 1):
            onward[h] = take(k, h, 1, 0, first[k, h])
        for h in (0, 1):
            for ja in (1, 2):
                second[k, h, ja] = both(k, h, 2, ja)
        for h in (0, 1):
            for copy in onward[h]:
                copy.wait_recv()
            second[k, h, 3] = both(k, h, 2, 3)
            here = block(k, h, 3, 0)
            to_sibling.append(send(here, here, sibling))
        last = []
        for ja in (0, 1, 2, 3):
            for h in (0, 1):
                last.append((h, ja, take(k, h, 2, ja, second[k, h, ja])))
        for h, ja, pair in last:
            for copy in pair:
                copy.wait_recv()
            here = block(k, h, ja, 3)
            to_sibling.append(send(here, here, sibling))
    local.wait()
    for copy in to_sibling:
        copy.wait_recv()
    send.finish()


def gather_weights(shard):
    rows, cols = shard.shape
    out = pl.pallas_call(
        gather_kernel,
        out_shape=jax.ShapeDtypeStruct((2, 4, 4, 2, 2, 16, cols), jnp.bfloat16),
        in_specs=[pl.BlockSpec(memory_space=pl.ANY)],
        out_specs=pl.BlockSpec(memory_space=pl.ANY),
        scratch_shapes=[
            pltpu.SemaphoreType.DMA,
            pltpu.SemaphoreType.DMA((N_GATHER,)),
            pltpu.SemaphoreType.DMA((N_GATHER,)),
        ],
        compiler_params=pltpu.CompilerParams(collective_id=0, has_side_effects=True),
        name="gather_weights",
    )(shard.reshape(2, 16, cols))
    return out.reshape(2, 32 * rows, cols)


N_SCATTER = 49


def scatter_kernel(
    grads, out, kept, given, pass_a, pass_b, near_p, near_m, q_a, q_b, q_p, q_m, mine, mate,
    local_sems, send_sems, recv_sems,
):
    x, y, c, t = place()
    cols = grads.shape[-1]
    part_a, part_b = pl.ds(0, HALF_A), pl.ds(HALF_A, cols - HALF_A)
    meet(x, y, c, t)
    send = Sender(send_sems, recv_sems)
    sibling = {"dp": dp_at(x, y, 1 - c)}
    f32 = jnp.float32

    def add(dst, *others):
        dst[...] = sum((o[...].astype(f32) for o in others), dst[...].astype(f32)).astype(dst.dtype)

    def half_of(p, h, j, core):
        tt = 1 - t if p == 0 else t
        if h == 0:
            return grads.at[tt, lax.rem(x + OFFSETS[j], 4), :, core, 0]
        return grads.at[tt, :, lax.rem(y + OFFSETS[j], 4), core, 1]

    loads, swaps = {}, {}
    for p in (0, 1):
        for j in (3, 1, 2, 0):
            for h in (0, 1):
                swaps[p, h, j] = send(half_of(p, h, j, 1 - c), given.at[p, h, j], sibling)
                load = pltpu.make_async_copy(
                    half_of(p, h, j, c), kept.at[p, h, j], local_sems.at[len(loads)]
                )
                load.start()
                loads[p, h, j] = load

    def settle(p, h, j):
        loads[p, h, j].wait()
        swaps[p, h, j].wait_recv()

    def each(body):
        lax.fori_loop(0, 4, lambda i, z: (body(i), z)[1], 0)

    far, near, q_far, q_near = {}, {}, {}, {}

    def start_far(p):
        for h in (0, 1):
            settle(p, h, 3)
            each(lambda i: add(kept.at[p, h, 3, i], given.at[p, h, 3, i]))
            far[p, h] = (
                send(kept.at[p, h, 3, :, :, part_a], pass_a.at[p, h], beside(h, 1, 1, x, y, c)),
                send(kept.at[p, h, 3, :, :, part_b], pass_b.at[p, h], beside(h, 1, 3, x, y, c)),
            )

    def start_near(p):
        for h in (0, 1):
            settle(p, h, 2)
            settle(p, h, 1)
            far[p, h][0].wait_recv()

            def plus(i):
                add(kept.at[p, h, 2, i, :, part_a], given.at[p, h, 2, i, :, part_a], pass_a.at[p, h, i])
                add(kept.at[p, h, 2, i, :, part_b], given.at[p, h, 2, i, :, part_b])

            each(plus)
            up = send(kept.at[p, h, 2], near_p.at[p, h], beside(h, 1, 1, x, y, c))
            far[p, h][1].wait_recv()

            def minus(i):
                add(kept.at[p, h, 1, i, :, part_b], given.at[p, h, 1, i, :, part_b], pass_b.at[p, h, i])
                add(kept.at[p, h, 1, i, :, part_a], given.at[p, h, 1, i, :, part_a])

            each(minus)
            near[p, h] = (up, send(kept.at[p, h, 1], near_m.at[p, h], beside(h, 1, 3, x, y, c)))

    def line(p, h, j):
        return kept.at[p, h, 0, lax.rem((y if h == 0 else x) + OFFSETS[j], 4)]

    def end_first(p):
        for h in (0, 1):
            settle(p, h, 0)
            for copy in near[p, h]:
                copy.wait_recv()
            each(
                lambda i: add(
                    kept.at[p, h, 0, i], given.at[p, h, 0, i], near_p.at[p, h, i], near_m.at[p, h, i]
                )
            )
            src = line(p, h, 3)
            q_far[p, h] = (
                send(src.at[:, part_a], q_a.at[p, h], beside(h, 2, 1, x, y, c)),
                send(src.at[:, part_b], q_b.at[p, h], beside(h, 2, 3, x, y, c)),
            )

    def mid_second(p):
        for h in (0, 1):
            q_far[p, h][0].wait_recv()
            src = line(p, h, 2)
            add(src.at[:, part_a], q_a.at[p, h])
            up = send(src, q_p.at[p, h], beside(h, 2, 1, x, y, c))
            q_far[p, h][1].wait_recv()
            src = line(p, h, 1)
            add(src.at[:, part_b], q_b.at[p, h])
            q_near[p, h] = (up, send(src, q_m.at[p, h], beside(h, 2, 3, x, y, c)))

    def end_second(p, dst, *more):
        for h in (0, 1):
            for copy in q_near[p, h]:
                copy.wait_recv()
            terms = [line(p, h, 0), q_p.at[p, h], q_m.at[p, h]] + [m.at[h] for m in more]
            dst[h] = sum((o[...].astype(f32) for o in terms[1:]), terms[0][...].astype(f32)).astype(dst.dtype)

    start_far(0)
    start_near(0)
    start_far(1)
    end_first(0)
    start_near(1)
    mid_second(0)
    end_first(1)
    end_second(0, mine)
    across = send(mine, mate, {"tensor": 1 - t})
    mid_second(1)
    across.wait_recv()
    end_second(1, out, mate)
    send.finish()


def scatter_grads(grads):
    cols = grads.shape[-1]
    bf = jnp.bfloat16
    rest = cols - HALF_A
    vmem = pltpu.VMEM
    out = pl.pallas_call(
        scatter_kernel,
        out_shape=jax.ShapeDtypeStruct((2, 16, cols), jnp.float32),
        in_specs=[pl.BlockSpec(memory_space=pl.ANY)],
        out_specs=pl.BlockSpec(memory_space=vmem),
        scratch_shapes=[
            vmem((2, 2, 4, 4, 16, cols), bf),
            vmem((2, 2, 4, 4, 16, cols), bf),
            vmem((2, 2, 4, 16, HALF_A), bf),
            vmem((2, 2, 4, 16, rest), bf),
            vmem((2, 2, 4, 16, cols), bf),
            vmem((2, 2, 4, 16, cols), bf),
            vmem((2, 2, 16, HALF_A), bf),
            vmem((2, 2, 16, rest), bf),
            vmem((2, 2, 16, cols), bf),
            vmem((2, 2, 16, cols), bf),
            vmem((2, 16, cols), bf),
            vmem((2, 16, cols), bf),
            pltpu.SemaphoreType.DMA((16,)),
            pltpu.SemaphoreType.DMA((N_SCATTER,)),
            pltpu.SemaphoreType.DMA((N_SCATTER,)),
        ],
        compiler_params=pltpu.CompilerParams(
            collective_id=1, has_side_effects=True, vmem_limit_bytes=52 * 2**20
        ),
        name="scatter_grads",
    )(grads.reshape(2, 4, 4, 2, 2, 16, cols))
    return out.reshape(32, cols)


def normalize(values):
    centred = values - jnp.mean(values, -1, keepdims=True)
    inverse_std = lax.rsqrt(jnp.mean(centred * centred, -1, keepdims=True) + epsilon)
    return (centred * inverse_std, inverse_std)


def norm_backward(grad_norm, normed, inverse_std):
    return inverse_std * (
        grad_norm
        - jnp.mean(grad_norm, -1, keepdims=True)
        - normed * jnp.mean(grad_norm * normed, -1, keepdims=True)
    )


def layer_forward(layer_in, key_mask, params):
    w_qkv, w_out, w_up, w_down, gains, shifts, b_qv, b_ff = params
    batch_rows, seq_len = (layer_in.shape[0], layer_in.shape[1])
    local_width = w_out.shape[0]
    head_shape = (batch_rows, seq_len, local_width // HD, HD)
    score_scale = HD ** (-0.5)
    projected = jnp.einsum("bsd,dkh->bskh", layer_in, w_qkv, preferred_element_type=jnp.float32)
    queries = (projected[:, :, 0] + b_qv[0]).astype(jnp.bfloat16).reshape(head_shape)
    keys_rows = projected[:, :, 1].astype(jnp.bfloat16).reshape(head_shape)
    values = (projected[:, :, 2] + b_qv[1]).astype(jnp.bfloat16).reshape(head_shape)
    scores = (
        jnp.einsum("bqhe,bkhe->bhqk", queries, keys_rows, preferred_element_type=jnp.float32)
        * score_scale
    )
    scores = jnp.where(key_mask[:, None, None, :], scores, -1000000000.0)
    row_max = jnp.max(scores, -1, keepdims=True)
    powers = jnp.exp(scores - row_max)
    probs = powers / jnp.sum(powers, -1, keepdims=True)
    probs_low = probs.astype(jnp.bfloat16)
    context = jnp.einsum("bhqk,bkhe->bqhe", probs_low, values, preferred_element_type=jnp.float32)
    context = context.reshape(batch_rows, seq_len, local_width).astype(jnp.bfloat16)
    attended = (
        jnp.einsum("bsh,hd->bsd", context, w_out, preferred_element_type=jnp.float32)
        + shifts[0]
    )
    normed_one, inverse_one = normalize(layer_in.astype(jnp.float32) + attended)
    hidden_in = normed_one * gains[0] + shifts[1]
    hidden_low = hidden_in.astype(jnp.bfloat16)
    upward = jnp.einsum("bsd,df->bsf", hidden_low, w_up, preferred_element_type=jnp.float32) + b_ff
    activated = jax.nn.gelu(upward, approximate=False).astype(jnp.bfloat16)
    downward = (
        jnp.einsum("bsf,fd->bsd", activated, w_down, preferred_element_type=jnp.float32)
        + shifts[2]
    )
    normed_two, inverse_two = normalize(hidden_in + downward)
    result = (normed_two * gains[1] + shifts[3]).astype(jnp.bfloat16)
    saved = (
        layer_in,
        queries,
        keys_rows,
        values,
        probs,
        probs_low,
        context,
        normed_one,
        inverse_one,
        hidden_low,
        upward,
        activated,
        normed_two,
        inverse_two,
    )
    return (result, saved)


def layer_backward(grad_out, saved, params):
    w_qkv, w_out, w_up, w_down, gains, shifts, b_qv, b_ff = params
    (
        layer_in,
        queries,
        keys_rows,
        values,
        probs,
        probs_low,
        context,
        normed_one,
        inverse_one,
        hidden_low,
        upward,
        activated,
        normed_two,
        inverse_two,
    ) = saved
    batch_rows, seq_len = (layer_in.shape[0], layer_in.shape[1])
    local_width = w_out.shape[0]
    score_scale = HD ** (-0.5)
    grad_gain_two = jnp.sum(grad_out * normed_two, axis=(0, 1))
    grad_shift_three = jnp.sum(grad_out, axis=(0, 1))
    grad_sum_two = norm_backward(grad_out * gains[1], normed_two, inverse_two)
    grad_shift_two = jnp.sum(grad_sum_two, axis=(0, 1))
    grad_sum_low = grad_sum_two.astype(jnp.bfloat16)
    grad_w_down = jnp.einsum(
        "bsf,bsd->fd", activated, grad_sum_low, preferred_element_type=jnp.float32
    )
    grad_act = jnp.einsum("bsd,fd->bsf", grad_sum_low, w_down, preferred_element_type=jnp.float32)
    grad_up = jax.vjp(partial(jax.nn.gelu, approximate=False), upward)[1](grad_act)[0]
    grad_up_low = grad_up.astype(jnp.bfloat16)
    grad_b_ff = jnp.sum(grad_up_low.astype(jnp.float32), axis=(0, 1))
    grad_w_up = jnp.einsum(
        "bsd,bsf->df", hidden_low, grad_up_low, preferred_element_type=jnp.float32
    )
    grad_hidden = grad_sum_two + jnp.einsum("bsf,df->bsd", grad_up_low, w_up, preferred_element_type=jnp.float32)
    grad_gain_one = jnp.sum(grad_hidden * normed_one, axis=(0, 1))
    grad_shift_one = jnp.sum(grad_hidden, axis=(0, 1))
    grad_sum_one = norm_backward(grad_hidden * gains[0], normed_one, inverse_one)
    grad_shift_zero = jnp.sum(grad_sum_one, axis=(0, 1))
    grad_one_low = grad_sum_one.astype(jnp.bfloat16)
    grad_w_out = jnp.einsum(
        "bsh,bsd->hd", context, grad_one_low, preferred_element_type=jnp.float32
    )
    grad_context = jnp.einsum(
        "bsd,hd->bsh", grad_one_low, w_out, preferred_element_type=jnp.float32
    )
    grad_context = grad_context.astype(jnp.bfloat16).reshape(queries.shape)
    grad_probs = jnp.einsum(
        "bqhe,bkhe->bhqk", grad_context, values, preferred_element_type=jnp.float32
    )
    grad_values = jnp.einsum(
        "bhqk,bqhe->bkhe", probs_low, grad_context, preferred_element_type=jnp.float32
    )
    grad_scores = probs * (grad_probs - jnp.sum(probs * grad_probs, -1, keepdims=True))
    grad_scores = grad_scores.astype(jnp.bfloat16)
    grad_queries = (
        jnp.einsum("bhqk,bkhe->bqhe", grad_scores, keys_rows, preferred_element_type=jnp.float32)
        * score_scale
    )
    grad_keys = (
        jnp.einsum("bhqk,bqhe->bkhe", grad_scores, queries, preferred_element_type=jnp.float32)
        * score_scale
    )
    flat_shape = (batch_rows, seq_len, local_width)
    grad_q_low = grad_queries.reshape(flat_shape).astype(jnp.bfloat16)
    grad_k_low = grad_keys.reshape(flat_shape).astype(jnp.bfloat16)
    grad_v_low = grad_values.reshape(flat_shape).astype(jnp.bfloat16)
    grad_b_qv = jnp.stack(
        [
            jnp.sum(grad_q_low.astype(jnp.float32), axis=(0, 1)),
            jnp.sum(grad_v_low.astype(jnp.float32), axis=(0, 1)),
        ]
    )
    grad_proj = jnp.stack([grad_q_low, grad_k_low, grad_v_low], axis=2)
    grad_w_qkv = jnp.einsum(
        "bsd,bskh->dkh", layer_in, grad_proj, preferred_element_type=jnp.float32
    )
    grad_in = grad_sum_one + jnp.einsum("bskh,dkh->bsd", grad_proj, w_qkv, preferred_element_type=jnp.float32)
    terms = (
        grad_w_qkv,
        grad_w_out,
        grad_w_up,
        grad_w_down,
        jnp.stack([grad_gain_one, grad_gain_two]),
        jnp.stack([grad_shift_zero, grad_shift_one, grad_shift_two, grad_shift_three]),
        grad_b_qv,
        grad_b_ff,
    )
    return (grad_in, terms)


COLS = 6272


def pack_shard(w_qkv, w_out, w_up, w_down, gains, shifts, b_qv, b_ff):
    extra = jnp.concatenate(
        [gains[0].T, shifts[0].T, b_qv[0, :, 0].reshape(32, 1), b_ff[0, 0].reshape(2, 32).T], axis=1
    )
    return jnp.concatenate(
        [
            w_qkv[0].reshape(32, 1536),
            w_out[0].T,
            w_up[0],
            w_down[0].T,
            jnp.pad(extra, ((0, 0), (0, 119))),
        ],
        axis=1,
    )


def unpack_extra(extra):
    extra = extra.astype(jnp.float32)
    gains = extra[0, :, 0:2].T
    shifts = extra[0, :, 2:6].T
    b_qv = extra[:, :, 6].reshape(2, 32, 2, 16).transpose(2, 0, 1, 3).reshape(2, 1024)
    b_ff = extra[:, :, 7:9].reshape(2, 32, 32, 2).transpose(0, 1, 3, 2).reshape(4096)
    return gains, shifts, b_qv, b_ff


def unpack_full(full):
    w_qkv = full[:, :, :1536].reshape(2, 1024, 3, 512).transpose(1, 2, 0, 3).reshape(1024, 3, 1024)
    w_out = full[:, :, 1536:2048].transpose(0, 2, 1).reshape(1024, 1024)
    w_up = full[:, :, 2048:4096].transpose(1, 0, 2).reshape(1024, 4096)
    w_down = full[:, :, 4096:6144].transpose(0, 2, 1).reshape(4096, 1024)
    return (w_qkv, w_out, w_up, w_down) + unpack_extra(full[:, :, 6144:])


def pack_extra(gains, shifts, b_qv, b_ff):
    common = jnp.concatenate([gains, shifts], axis=0).T
    return jnp.concatenate(
        [
            jnp.broadcast_to(common, (2, 1024, 6)),
            b_qv.reshape(2, 2, 32, 16).transpose(1, 2, 0, 3).reshape(2, 1024, 1),
            b_ff.reshape(2, 32, 2, 32).transpose(0, 1, 3, 2).reshape(2, 1024, 2),
            jnp.zeros((2, 1024, 119), gains.dtype),
        ],
        axis=2,
    )


def pack_full(terms):
    w_qkv, w_out, w_up, w_down = (term.astype(jnp.bfloat16) for term in terms[:4])
    return jnp.concatenate(
        [
            w_qkv.reshape(1024, 3, 2, 512).transpose(2, 0, 1, 3).reshape(2, 1024, 1536),
            w_out.reshape(2, 512, 1024).transpose(0, 2, 1),
            w_up.reshape(1024, 2, 2048).transpose(1, 0, 2),
            w_down.reshape(2, 2048, 1024).transpose(0, 2, 1),
            pack_extra(*terms[4:]).astype(jnp.bfloat16),
        ],
        axis=2,
    )


def unpack_shard(got):
    extra = got[:, 6144:]
    return (
        got[:, :1536].reshape(1, 32, 3, 512),
        got[:, 1536:2048].T[None],
        got[:, 2048:4096][None],
        got[:, 4096:6144].T[None],
        extra[:, 0:2].T[None],
        extra[:, 2:6].T[None],
        extra[:, 6].reshape(1, 2, 1, 16),
        extra[:, 7:9].T.reshape(1, 1, 64),
    )


def body(ends, lengths, w_qkv, w_out, w_up, w_down, gains, shifts, b_qv, b_ff):
    section_at = lax.axis_index("section")
    tensor_at = lax.axis_index("tensor")
    own = lax.dynamic_index_in_dim(ends[0], tensor_at, 0, keepdims=False)
    length = lax.dynamic_index_in_dim(lengths, tensor_at, 0, keepdims=False)
    key_mask = lax.broadcasted_iota(jnp.int32, (1, own.shape[1]), 1) < length[:, None]
    full = gather_weights(pack_shard(w_qkv, w_out, w_up, w_down, gains, shifts, b_qv, b_ff))
    params = unpack_full(full)
    first_out, _ = layer_forward(own, key_mask, params)
    arrived = lax.ppermute(first_out, "section", [(0, 1)])
    entry = jnp.where(section_at == 0, own, arrived)
    layer_out, saved = layer_forward(entry, key_mask, params)
    grad_in, _ = layer_backward(own.astype(jnp.float32), saved, params)
    inbound = lax.ppermute(grad_in.astype(jnp.bfloat16), "section", [(1, 0)])
    grad_out = jnp.where(section_at == 1, own, inbound).astype(jnp.float32)
    grad_in, terms = layer_backward(grad_out, saved, params)
    kept = jnp.where(section_at == 0, grad_in.astype(jnp.bfloat16), layer_out)
    other = lax.ppermute(kept, "tensor", [(0, 1), (1, 0)])
    ends_out = jnp.where(tensor_at == 0, jnp.stack([kept, other]), jnp.stack([other, kept]))[None]
    return (ends_out,) + unpack_shard(scatter_grads(pack_full(terms)))


def solution(mesh):
    in_specs = (
        P("section", None, "dp", None, None),
        P(None, "dp"),
        P("section", "dp", None, "tensor"),
        P("section", "tensor", "dp"),
        P("section", "dp", "tensor"),
        P("section", "tensor", "dp"),
        P("section", None, "dp"),
        P("section", None, "dp"),
        P("section", None, "tensor", "dp"),
        P("section", "tensor", "dp"),
    )
    out_specs = (
        P("section", None, "dp", None, None),
        P("section", "dp", None, "tensor"),
        P("section", "tensor", "dp"),
        P("section", "dp", "tensor"),
        P("section", "tensor", "dp"),
        P("section", None, "dp"),
        P("section", None, "dp"),
        P("section", None, "tensor", "dp"),
        P("section", "tensor", "dp"),
    )
    return jax.shard_map(body, mesh=mesh, in_specs=in_specs, out_specs=out_specs, check_vma=False)
```

```python
import jax
import jax.numpy as jnp
from jax import lax
from jax.experimental import pallas as pl
from jax.experimental.pallas import tpu as pltpu
from jax.sharding import PartitionSpec as P

HD = 64
epsilon = 1e-05

COLS = 6272
MAIN = 6144
ROWS = 192
BLOCK = 512
CHUNKS = ((0, 1536), (1536, 512), (2048, 2048), (4096, 2048))


HALF_A = 3200
OFFSETS = (0, 3, 1, 2)
MESH = pl.DeviceIdType.MESH


def place():
    d = lax.axis_index("dp")
    return lax.div(d, 8), lax.rem(lax.div(d, 2), 4), lax.rem(d, 2), lax.axis_index("tensor")


def dp_at(x, y, c):
    return (x * 4 + y) * 2 + c


def beside(h, phase, step, x, y, c):
    if (h == 0) == (phase == 1):
        return {"dp": dp_at(lax.rem(x + step, 4), y, c)}
    return {"dp": dp_at(x, lax.rem(y + step, 4), c)}


def meet(x, y, c, t):
    barrier = pltpu.get_barrier_semaphore()
    partners = [
        {"dp": dp_at(lax.rem(x + 1, 4), y, c)},
        {"dp": dp_at(lax.rem(x + 3, 4), y, c)},
        {"dp": dp_at(x, lax.rem(y + 1, 4), c)},
        {"dp": dp_at(x, lax.rem(y + 3, 4), c)},
        {"dp": dp_at(x, y, 1 - c)},
        {"tensor": 1 - t},
    ]
    for partner in partners:
        pl.semaphore_signal(barrier, inc=1, device_id=partner, device_id_type=MESH)
    pl.semaphore_wait(barrier, len(partners))


class Sender:
    def __init__(self, send_sems, recv_sems):
        self.send_sems, self.recv_sems, self.copies = send_sems, recv_sems, []

    def __call__(self, src, dst, where):
        i = len(self.copies)
        copy = pltpu.make_async_remote_copy(
            src_ref=src,
            dst_ref=dst,
            send_sem=self.send_sems.at[i],
            recv_sem=self.recv_sems.at[i],
            device_id=where,
            device_id_type=MESH,
        )
        copy.start()
        self.copies.append(copy)
        return copy

    def finish(self):
        for copy in self.copies:
            copy.wait_send()


N_GATHER = 143


def gather_kernel(shard, out, local_sem, send_sems, recv_sems):
    x, y, c, t = place()
    cols = shard.shape[-1]
    part_a, part_b = pl.ds(0, HALF_A), pl.ds(HALF_A, cols - HALF_A)
    meet(x, y, c, t)
    send = Sender(send_sems, recv_sems)
    sibling = {"dp": dp_at(x, y, 1 - c)}
    own = out.at[t, x, y, c]
    local = pltpu.make_async_copy(shard, own, local_sem)
    local.start()
    from_partner = send(shard, own, {"tensor": 1 - t})
    to_sibling = [send(shard, own, sibling)]

    def block(k, h, ja, jb):
        a, b = OFFSETS[ja], OFFSETS[jb]
        dx, dy = (a, b) if h == 0 else (b, a)
        return out.at[t if k == 0 else 1 - t, lax.rem(x + dx, 4), lax.rem(y + dy, 4), c, h]

    def both(k, h, phase, ja):
        dst = block(k, h, ja, 0)
        src = shard.at[h] if (k == 0 and ja == 0) else dst
        return (
            send(src, dst, beside(h, phase, 1, x, y, c)),
            send(src, dst, beside(h, phase, 3, x, y, c)),
        )

    def take(k, h, phase, ja, pair):
        onward = []
        for copy, j, part, step in ((pair[0], 1, part_a, 1), (pair[1], 2, part_b, 3)):
            copy.wait_recv()
            here = block(k, h, *((j, 0) if phase == 1 else (ja, j)))
            onward.append(send(here.at[:, part], here.at[:, part], beside(h, phase, step, x, y, c)))
            to_sibling.append(send(here, here, sibling))
        return onward

    first, second = {}, {}

    def begin(k):
        for h in (0, 1):
            first[k, h] = both(k, h, 1, 0)
        for h in (0, 1):
            second[k, h, 0] = both(k, h, 2, 0)

    begin(0)
    from_partner.wait_recv()
    begin(1)
    mate = out.at[1 - t, x, y, c]
    to_sibling.append(send(mate, mate, sibling))
    for k in (0, 1):
        onward = {}
        for h in (0, 1):
            onward[h] = take(k, h, 1, 0, first[k, h])
        for h in (0, 1):
            for ja in (1, 2):
                second[k, h, ja] = both(k, h, 2, ja)
        for h in (0, 1):
            for copy in onward[h]:
                copy.wait_recv()
            second[k, h, 3] = both(k, h, 2, 3)
            here = block(k, h, 3, 0)
            to_sibling.append(send(here, here, sibling))
        last = []
        for ja in (0, 1, 2, 3):
            for h in (0, 1):
                last.append((h, ja, take(k, h, 2, ja, second[k, h, ja])))
        for h, ja, pair in last:
            for copy in pair:
                copy.wait_recv()
            here = block(k, h, ja, 3)
            to_sibling.append(send(here, here, sibling))
    local.wait()
    for copy in to_sibling:
        copy.wait_recv()
    send.finish()


def gather_weights(shard):
    rows, cols = shard.shape
    out = pl.pallas_call(
        gather_kernel,
        out_shape=jax.ShapeDtypeStruct((2, 4, 4, 2, 2, 16, cols), jnp.bfloat16),
        in_specs=[pl.BlockSpec(memory_space=pl.ANY)],
        out_specs=pl.BlockSpec(memory_space=pl.ANY),
        scratch_shapes=[
            pltpu.SemaphoreType.DMA,
            pltpu.SemaphoreType.DMA((N_GATHER,)),
            pltpu.SemaphoreType.DMA((N_GATHER,)),
        ],
        compiler_params=pltpu.CompilerParams(collective_id=0, has_side_effects=True),
        name="gather_weights",
    )(shard.reshape(2, 16, cols))
    return out.reshape(2, 32 * rows, cols)


N_SCATTER = 65


def scatter_kernel(
    main, extra, out, kept, given, pass_a, pass_b, near_p, near_m, q_a, q_b, q_p, q_m, mine, mate,
    local_sems, send_sems, recv_sems,
):
    x, y, c, t = place()
    cols = kept.shape[-1]
    whole = (pl.ds(0, MAIN), pl.ds(MAIN, cols - MAIN))
    part_a, part_b = pl.ds(0, HALF_A), pl.ds(HALF_A, cols - HALF_A)
    meet(x, y, c, t)
    send = Sender(send_sems, recv_sems)
    sibling = {"dp": dp_at(x, y, 1 - c)}
    f32 = jnp.float32

    def add(dst, *others):
        dst[...] = sum((o[...].astype(f32) for o in others), dst[...].astype(f32)).astype(dst.dtype)

    def half_of(grads, p, h, j, core):
        tt = 1 - t if p == 0 else t
        if h == 0:
            return grads.at[tt, lax.rem(x + OFFSETS[j], 4), :, core, 0]
        return grads.at[tt, :, lax.rem(y + OFFSETS[j], 4), core, 1]

    loads, swaps = {}, {}
    for p in (0, 1):
        for j in (3, 1, 2, 0):
            for h in (0, 1):
                swaps[p, h, j], loads[p, h, j] = [], []
                for grads, part in ((main, whole[0]), (extra, whole[1])):
                    swaps[p, h, j].append(
                        send(half_of(grads, p, h, j, 1 - c), given.at[p, h, j, :, :, part], sibling)
                    )
                    load = pltpu.make_async_copy(
                        half_of(grads, p, h, j, c),
                        kept.at[p, h, j, :, :, part],
                        local_sems.at[len(swaps) * 2 + len(loads[p, h, j]) - 2],
                    )
                    load.start()
                    loads[p, h, j].append(load)

    def settle(p, h, j):
        for load in loads[p, h, j]:
            load.wait()
        for swap in swaps[p, h, j]:
            swap.wait_recv()

    def each(body):
        lax.fori_loop(0, 4, lambda i, z: (body(i), z)[1], 0)

    far, near, q_far, q_near = {}, {}, {}, {}

    def start_far(p):
        for h in (0, 1):
            settle(p, h, 3)
            each(lambda i: add(kept.at[p, h, 3, i], given.at[p, h, 3, i]))
            far[p, h] = (
                send(kept.at[p, h, 3, :, :, part_a], pass_a.at[p, h], beside(h, 1, 1, x, y, c)),
                send(kept.at[p, h, 3, :, :, part_b], pass_b.at[p, h], beside(h, 1, 3, x, y, c)),
            )

    def start_near(p):
        for h in (0, 1):
            settle(p, h, 2)
            settle(p, h, 1)
            far[p, h][0].wait_recv()

            def plus(i):
                add(kept.at[p, h, 2, i, :, part_a], given.at[p, h, 2, i, :, part_a], pass_a.at[p, h, i])
                add(kept.at[p, h, 2, i, :, part_b], given.at[p, h, 2, i, :, part_b])

            each(plus)
            up = send(kept.at[p, h, 2], near_p.at[p, h], beside(h, 1, 1, x, y, c))
            far[p, h][1].wait_recv()

            def minus(i):
                add(kept.at[p, h, 1, i, :, part_b], given.at[p, h, 1, i, :, part_b], pass_b.at[p, h, i])
                add(kept.at[p, h, 1, i, :, part_a], given.at[p, h, 1, i, :, part_a])

            each(minus)
            near[p, h] = (up, send(kept.at[p, h, 1], near_m.at[p, h], beside(h, 1, 3, x, y, c)))

    def line(p, h, j):
        return kept.at[p, h, 0, lax.rem((y if h == 0 else x) + OFFSETS[j], 4)]

    def end_first(p):
        for h in (0, 1):
            settle(p, h, 0)
            for copy in near[p, h]:
                copy.wait_recv()
            each(
                lambda i: add(
                    kept.at[p, h, 0, i], given.at[p, h, 0, i], near_p.at[p, h, i], near_m.at[p, h, i]
                )
            )
            src = line(p, h, 3)
            q_far[p, h] = (
                send(src.at[:, part_a], q_a.at[p, h], beside(h, 2, 1, x, y, c)),
                send(src.at[:, part_b], q_b.at[p, h], beside(h, 2, 3, x, y, c)),
            )

    def mid_second(p):
        for h in (0, 1):
            q_far[p, h][0].wait_recv()
            src = line(p, h, 2)
            add(src.at[:, part_a], q_a.at[p, h])
            up = send(src, q_p.at[p, h], beside(h, 2, 1, x, y, c))
            q_far[p, h][1].wait_recv()
            src = line(p, h, 1)
            add(src.at[:, part_b], q_b.at[p, h])
            q_near[p, h] = (up, send(src, q_m.at[p, h], beside(h, 2, 3, x, y, c)))

    def end_second(p, dst, *more):
        for h in (0, 1):
            for copy in q_near[p, h]:
                copy.wait_recv()
            terms = [line(p, h, 0), q_p.at[p, h], q_m.at[p, h]] + [m.at[h] for m in more]
            dst[h] = sum((o[...].astype(f32) for o in terms[1:]), terms[0][...].astype(f32)).astype(dst.dtype)

    start_far(0)
    start_near(0)
    start_far(1)
    end_first(0)
    start_near(1)
    mid_second(0)
    end_first(1)
    end_second(0, mine)
    across = send(mine, mate, {"tensor": 1 - t})
    mid_second(1)
    across.wait_recv()
    end_second(1, out, mate)
    send.finish()


def scatter_grads(main, extra):
    cols = COLS
    bf = jnp.bfloat16
    rest = cols - HALF_A
    vmem = pltpu.VMEM
    out = pl.pallas_call(
        scatter_kernel,
        out_shape=jax.ShapeDtypeStruct((2, 16, cols), jnp.float32),
        in_specs=[pl.BlockSpec(memory_space=pl.ANY)] * 2,
        out_specs=pl.BlockSpec(memory_space=vmem),
        scratch_shapes=[
            vmem((2, 2, 4, 4, 16, cols), bf),
            vmem((2, 2, 4, 4, 16, cols), bf),
            vmem((2, 2, 4, 16, HALF_A), bf),
            vmem((2, 2, 4, 16, rest), bf),
            vmem((2, 2, 4, 16, cols), bf),
            vmem((2, 2, 4, 16, cols), bf),
            vmem((2, 2, 16, HALF_A), bf),
            vmem((2, 2, 16, rest), bf),
            vmem((2, 2, 16, cols), bf),
            vmem((2, 2, 16, cols), bf),
            vmem((2, 16, cols), bf),
            vmem((2, 16, cols), bf),
            pltpu.SemaphoreType.DMA((32,)),
            pltpu.SemaphoreType.DMA((N_SCATTER,)),
            pltpu.SemaphoreType.DMA((N_SCATTER,)),
        ],
        compiler_params=pltpu.CompilerParams(
            collective_id=1, has_side_effects=True, vmem_limit_bytes=52 * 2**20
        ),
        name="scatter_grads",
    )(main.reshape(2, 4, 4, 2, 2, 16, MAIN), extra.reshape(2, 4, 4, 2, 2, 16, cols - MAIN))
    return out.reshape(32, cols)


def dot(a, b):
    return lax.dot_general(a, b, (((1,), (0,)), ((), ())), preferred_element_type=jnp.float32)


def dot_nt(a, b):
    return lax.dot_general(a, b, (((1,), (1,)), ((), ())), preferred_element_type=jnp.float32)


def dot_tn(a, b):
    return lax.dot_general(a, b, (((0,), (0,)), ((), ())), preferred_element_type=jnp.float32)


def low(v):
    return v.astype(jnp.bfloat16)


def high(v):
    return v.astype(jnp.float32)


def columns(start, size):
    return pl.ds(pl.multiple_of(start, 128), size)


def each(count, work):
    lax.fori_loop(0, count, lambda i, z: (work(i), z)[1], 0)


def total(v):
    return jnp.sum(v, axis=0, keepdims=True)


def normalize(values):
    centred = values - jnp.mean(values, -1, keepdims=True)
    inverse_std = lax.rsqrt(jnp.mean(centred * centred, -1, keepdims=True) + epsilon)
    return centred * inverse_std, inverse_std


def norm_backward(grad_norm, normed, inverse_std):
    return inverse_std * (
        grad_norm
        - jnp.mean(grad_norm, -1, keepdims=True)
        - normed * jnp.mean(grad_norm * normed, -1, keepdims=True)
    )


def layers_kernel(
    lengths, ends, full, gains, shifts, b_qv, b_ff,
    ends_out, grads, d_gains, d_shifts, d_bqv, d_bff,
    w, x_own, x_in, relay, q, k, v, o, probs, n1, n2, i1, i2, res, hid, act, slope, d_act, d_qkv,
    acc, d_low, a_low, kept, stage,
    load_sems, io_sems, stage_sems, send_sems, recv_sems,
):
    s, t = lax.axis_index("section"), lax.axis_index("tensor")
    loads = {}
    own_load = pltpu.make_async_copy(ends.at[t], x_own, io_sems.at[0])
    own_load.start()
    for n, (start, size) in enumerate(CHUNKS):
        for half in (0, 1):
            part = pl.ds(start, size)
            load = pltpu.make_async_copy(
                full.at[half, :, part], w.at[half, :, part], load_sems.at[2 * n + half]
            )
            load.start()
            loads[n, half] = load

    barrier = pltpu.get_barrier_semaphore()
    pl.semaphore_signal(barrier, inc=1, device_id={"section": 1 - s}, device_id_type=MESH)
    pl.semaphore_signal(barrier, inc=1, device_id={"tensor": 1 - t}, device_id_type=MESH)
    pl.semaphore_wait(barrier, 2)

    def ready(n):
        for half in (0, 1):
            if (n, half) in loads:
                loads.pop((n, half)).wait()

    length = lengths[t, 0]
    first_half = lax.broadcasted_iota(jnp.int32, (ROWS, 128), 1) < HD
    valid = lax.broadcasted_iota(jnp.int32, (ROWS, ROWS), 1) < length
    scale = HD**-0.5

    def pick(e, value):
        return jnp.where(first_half == (e == 0), value, jnp.zeros_like(value))

    def forward(x):
        ready(0)

        def project(i):
            half, j = lax.div(i, 3), lax.rem(i, 3)
            p = dot(x[...], w[half, :, columns(j * BLOCK, BLOCK)])
            at = columns(half * BLOCK, BLOCK)

            @pl.when(j == 0)
            def _():
                q[:, at] = low(p + b_qv[0:1, at])

            @pl.when(j == 1)
            def _():
                k[:, at] = low(p)

            @pl.when(j == 2)
            def _():
                v[:, at] = low(p + b_qv[1:2, at])

        each(6, project)

        def heads(i):
            at = columns(i * 128, 128)
            kp, vp, qp = k[:, at], v[:, at], q[:, at]
            outs = []
            for e in (0, 1):
                scores = dot_nt(pick(e, qp), kp) * scale
                scores = jnp.where(valid, scores, -1e9)
                powers = jnp.exp(scores - jnp.max(scores, -1, keepdims=True))
                p = powers / jnp.sum(powers, -1, keepdims=True)
                probs[2 * i + e] = p
                outs.append(dot(low(p), vp))
            o[:, at] = low(jnp.where(first_half, outs[0], outs[1]))

        each(8, heads)
        ready(1)
        attended = dot_nt(o[:, 0:512], w[0, :, 1536:2048]) + dot_nt(o[:, 512:1024], w[1, :, 1536:2048])
        normed, inverse = normalize(high(x[...]) + attended + shifts[0:1])
        n1[...], i1[...] = normed, inverse
        hidden = normed * gains[0:1] + shifts[1:2]
        res[...] = hidden
        hid[...] = low(hidden)
        ready(2)

        def widen(i):
            half, j = lax.div(i, 4), lax.rem(i, 4)
            at = columns(i * BLOCK, BLOCK)
            u = dot(hid[...], w[half, :, columns(2048 + j * BLOCK, BLOCK)]) + b_ff[:, at]
            phi = 0.5 + 0.5 * lax.erf(u * 0.7071067811865476)
            act[:, at] = low(u * phi)
            slope[:, at] = phi + u * (jnp.exp(u * u * -0.5) * 0.3989422804014327)

        each(8, widen)
        ready(3)

        def narrow(i):
            at = columns(i * 256, 256)
            rows = pl.ds(pl.multiple_of(i * 256, 256), 256)
            acc[:, at] = dot_nt(act[:, 0:2048], w[0, rows, 4096:6144]) + dot_nt(
                act[:, 2048:4096], w[1, rows, 4096:6144]
            )

        each(4, narrow)
        normed, inverse = normalize(res[...] + acc[...] + shifts[2:3])
        n2[...], i2[...] = normed, inverse
        return low(normed * gains[1:2] + shifts[3:4])

    def backward(grad_out):
        normed = n2[...]
        d_gains[1:2] = total(grad_out * normed)
        d_shifts[3:4] = total(grad_out)
        d_sum = norm_backward(grad_out * gains[1:2], normed, i2[...])
        d_shifts[2:3] = total(d_sum)
        res[...] = d_sum
        d_low[...] = low(d_sum)

        def widen(i):
            half, j = lax.div(i, 4), lax.rem(i, 4)
            at = columns(i * BLOCK, BLOCK)
            d = low(dot(d_low[...], w[half, :, columns(4096 + j * BLOCK, BLOCK)]) * slope[:, at])
            d_act[:, at] = d
            d_bff[:, at] = total(high(d))

        each(8, widen)

        def narrow(i):
            at = columns(i * 256, 256)
            rows = pl.ds(pl.multiple_of(i * 256, 256), 256)
            acc[:, at] = dot_nt(d_act[:, 0:2048], w[0, rows, 2048:4096]) + dot_nt(
                d_act[:, 2048:4096], w[1, rows, 2048:4096]
            )

        each(4, narrow)
        d_hidden = res[...] + acc[...]
        normed = n1[...]
        d_gains[0:1] = total(d_hidden * normed)
        d_shifts[1:2] = total(d_hidden)
        d_sum = norm_backward(d_hidden * gains[0:1], normed, i1[...])
        d_shifts[0:1] = total(d_sum)
        res[...] = d_sum
        a_low[...] = low(d_sum)

        def heads(i):
            at = columns(i * 128, 128)
            half = lax.div(i, 4)
            d_o = low(dot(a_low[...], w[half, :, columns(1536 + lax.rem(i, 4) * 128, 128)]))
            kp, vp, qp = k[:, at], v[:, at], q[:, at]
            parts = []
            for e in (0, 1):
                p = probs[2 * i + e]
                d_p = dot_nt(pick(e, d_o), vp)
                d_s = low(p * (d_p - jnp.sum(p * d_p, -1, keepdims=True)))
                parts.append((dot(d_s, kp) * scale, dot_tn(d_s, qp) * scale, dot_tn(low(p), d_o)))
            d_q, d_k, d_v = (low(jnp.where(first_half, a, b)) for a, b in zip(*parts))
            d_qkv[0, :, at] = d_q
            d_qkv[1, :, at] = d_k
            d_qkv[2, :, at] = d_v
            d_bqv[0:1, at] = total(high(d_q))
            d_bqv[1:2, at] = total(high(d_v))

        each(8, heads)

        def narrow_in(i):
            at = columns(i * 256, 256)
            rows = pl.ds(pl.multiple_of(i * 256, 256), 256)
            acc[:, at] = sum(
                dot_nt(d_qkv[j, :, 512 * half : 512 * half + 512], w[half, rows, 512 * j : 512 * j + 512])
                for half in (0, 1)
                for j in (0, 1, 2)
            )

        each(4, narrow_in)
        return low(res[...] + acc[...])

    def weight_grads(x):
        def block(i, half, start, left, right):
            slot = lax.rem(i, 4)
            copy = pltpu.make_async_copy(
                stage.at[slot], grads.at[half, :, columns(start, BLOCK)], stage_sems.at[slot]
            )

            @pl.when(i >= 4)
            def _():
                copy.wait()

            stage[slot] = low(dot_tn(left, right))
            copy.start()

        def narrow(i):
            block(i, lax.div(i, 4), 4096 + lax.rem(i, 4) * BLOCK, d_low[...], act[:, columns(i * BLOCK, BLOCK)])

        def widen(i):
            block(i + 8, lax.div(i, 4), 2048 + lax.rem(i, 4) * BLOCK, hid[...], d_act[:, columns(i * BLOCK, BLOCK)])

        def attend(i):
            block(i + 16, i, 1536, a_low[...], o[:, columns(i * BLOCK, BLOCK)])

        def project(i):
            half, j = lax.div(i, 3), lax.rem(i, 3)
            block(i + 18, half, j * BLOCK, x[...], d_qkv[j, :, columns(half * BLOCK, BLOCK)])

        each(8, narrow)
        each(8, widen)
        each(2, attend)
        each(6, project)
        for slot in range(4):
            pltpu.make_async_copy(
                stage.at[slot], grads.at[0, :, pl.ds(0, BLOCK)], stage_sems.at[slot]
            ).wait()

    def exchange(n):
        copy = pltpu.make_async_remote_copy(
            src_ref=kept.at[n],
            dst_ref=relay.at[n],
            send_sem=send_sems.at[n],
            recv_sem=recv_sems.at[n],
            device_id={"section": 1 - s},
            device_id_type=MESH,
        )
        copy.start()
        copy.wait()
        return relay[n]

    own_load.wait()
    kept[0] = forward(x_own)
    x_in[...] = jnp.where(s == 0, x_own[...], exchange(0))
    result = forward(x_in)
    kept[2] = result
    kept[1] = backward(high(x_own[...]))
    grad_out = jnp.where(s == 1, x_own[...], exchange(1))
    d_x = backward(high(grad_out))
    kept[2] = jnp.where(s == 0, d_x, kept[2])
    across = pltpu.make_async_remote_copy(
        src_ref=kept.at[2],
        dst_ref=ends_out.at[t],
        send_sem=send_sems.at[2],
        recv_sem=recv_sems.at[2],
        device_id={"tensor": 1 - t},
        device_id_type=MESH,
    )
    across.start()
    here = pltpu.make_async_copy(kept.at[2], ends_out.at[t], io_sems.at[1])
    here.start()
    weight_grads(x_in)
    here.wait()
    across.wait()


def run_layers(lengths, ends, full, gains, shifts, b_qv, b_ff):
    vmem = pltpu.VMEM
    bf, f32 = jnp.bfloat16, jnp.float32
    hbm = pl.BlockSpec(memory_space=pl.ANY)
    near = pl.BlockSpec(memory_space=vmem)
    sem = pltpu.SemaphoreType.DMA
    shape = jax.ShapeDtypeStruct
    return pl.pallas_call(
        layers_kernel,
        out_shape=(
            shape((2, ROWS, 1024), bf),
            shape((2, 1024, MAIN), bf),
            shape((2, 1024), f32),
            shape((4, 1024), f32),
            shape((2, 1024), f32),
            shape((1, 4096), f32),
        ),
        in_specs=[pl.BlockSpec(memory_space=pltpu.SMEM), hbm, hbm, near, near, near, near],
        out_specs=(hbm, hbm, near, near, near, near),
        scratch_shapes=[
            vmem((2, 1024, MAIN), bf),
            vmem((ROWS, 1024), bf),
            vmem((ROWS, 1024), bf),
            vmem((2, ROWS, 1024), bf),
            vmem((ROWS, 1024), bf),
            vmem((ROWS, 1024), bf),
            vmem((ROWS, 1024), bf),
            vmem((ROWS, 1024), bf),
            vmem((16, ROWS, ROWS), f32),
            vmem((ROWS, 1024), f32),
            vmem((ROWS, 1024), f32),
            vmem((ROWS, 1), f32),
            vmem((ROWS, 1), f32),
            vmem((ROWS, 1024), f32),
            vmem((ROWS, 1024), bf),
            vmem((ROWS, 4096), bf),
            vmem((ROWS, 4096), f32),
            vmem((ROWS, 4096), bf),
            vmem((3, ROWS, 1024), bf),
            vmem((ROWS, 1024), f32),
            vmem((ROWS, 1024), bf),
            vmem((ROWS, 1024), bf),
            vmem((3, ROWS, 1024), bf),
            vmem((4, 1024, BLOCK), bf),
            sem((8,)),
            sem((2,)),
            sem((4,)),
            sem((3,)),
            sem((3,)),
        ],
        compiler_params=pltpu.CompilerParams(
            collective_id=2, has_side_effects=True, vmem_limit_bytes=58 * 2**20
        ),
        name="run_layers",
    )(lengths, ends, full, gains, shifts, b_qv, b_ff)


def pack_shard(w_qkv, w_out, w_up, w_down, gains, shifts, b_qv, b_ff):
    extra = jnp.concatenate(
        [gains[0].T, shifts[0].T, b_qv[0, :, 0].reshape(32, 1), b_ff[0, 0].reshape(2, 32).T], axis=1
    )
    return jnp.concatenate(
        [
            w_qkv[0].reshape(32, 1536),
            w_out[0].T,
            w_up[0],
            w_down[0].T,
            jnp.pad(extra, ((0, 0), (0, 119))),
        ],
        axis=1,
    )


def unpack_extra(extra):
    extra = extra.astype(jnp.float32)
    gains = extra[0, :, 0:2].T
    shifts = extra[0, :, 2:6].T
    b_qv = extra[:, :, 6].reshape(2, 32, 2, 16).transpose(2, 0, 1, 3).reshape(2, 1024)
    b_ff = extra[:, :, 7:9].reshape(2, 32, 32, 2).transpose(0, 1, 3, 2).reshape(4096)
    return gains, shifts, b_qv, b_ff


def pack_extra(gains, shifts, b_qv, b_ff):
    common = jnp.concatenate([gains, shifts], axis=0).T
    return jnp.concatenate(
        [
            jnp.broadcast_to(common, (2, 1024, 6)),
            b_qv.reshape(2, 2, 32, 16).transpose(1, 2, 0, 3).reshape(2, 1024, 1),
            b_ff.reshape(2, 32, 2, 32).transpose(0, 1, 3, 2).reshape(2, 1024, 2),
            jnp.zeros((2, 1024, 119), gains.dtype),
        ],
        axis=2,
    )


def unpack_shard(got):
    extra = got[:, 6144:]
    return (
        got[:, :1536].reshape(1, 32, 3, 512),
        got[:, 1536:2048].T[None],
        got[:, 2048:4096][None],
        got[:, 4096:6144].T[None],
        extra[:, 0:2].T[None],
        extra[:, 2:6].T[None],
        extra[:, 6].reshape(1, 2, 1, 16),
        extra[:, 7:9].T.reshape(1, 1, 64),
    )


def body(ends, lengths, w_qkv, w_out, w_up, w_down, gains, shifts, b_qv, b_ff):
    full = gather_weights(pack_shard(w_qkv, w_out, w_up, w_down, gains, shifts, b_qv, b_ff))
    gains, shifts, b_qv, b_ff = unpack_extra(full[:, :, MAIN:])
    ends_out, main, d_gains, d_shifts, d_bqv, d_bff = run_layers(
        lengths, ends.reshape(2, ROWS, 1024), full, gains, shifts, b_qv, b_ff.reshape(1, 4096)
    )
    extra = pack_extra(d_gains, d_shifts, d_bqv, d_bff.reshape(4096)).astype(jnp.bfloat16)
    return (ends_out.reshape(1, 2, 1, ROWS, 1024),) + unpack_shard(scatter_grads(main, extra))


def solution(mesh):
    in_specs = (
        P("section", None, "dp", None, None),
        P(None, "dp"),
        P("section", "dp", None, "tensor"),
        P("section", "tensor", "dp"),
        P("section", "dp", "tensor"),
        P("section", "tensor", "dp"),
        P("section", None, "dp"),
        P("section", None, "dp"),
        P("section", None, "tensor", "dp"),
        P("section", "tensor", "dp"),
    )
    out_specs = (
        P("section", None, "dp", None, None),
        P("section", "dp", None, "tensor"),
        P("section", "tensor", "dp"),
        P("section", "dp", "tensor"),
        P("section", "tensor", "dp"),
        P("section", None, "dp"),
        P("section", None, "dp"),
        P("section", None, "tensor", "dp"),
        P("section", "tensor", "dp"),
    )
    return jax.shard_map(body, mesh=mesh, in_specs=in_specs, out_specs=out_specs, check_vma=False)
```

```python
import jax
import jax.numpy as jnp
from jax import lax
from jax.experimental import pallas as pl
from jax.experimental.pallas import tpu as pltpu
from jax.sharding import PartitionSpec as P

HD = 64
epsilon = 1e-05

COLS = 6272
ROWS = 192
BLOCK = 512
EXTRA, UP, DOWN = 2048, 2176, 4224
CHUNKS = ((0, 1536), (1536, 512), (UP, 2048), (DOWN, 2048))
PASSES = ((DOWN, 2048, 1024), (UP, 2048, 1024), (0, 2176, 1152))


HALF_A = 3200
OFFSETS = (0, 3, 1, 2)
MESH = pl.DeviceIdType.MESH


def place():
    d = lax.axis_index("dp")
    return lax.div(d, 8), lax.rem(lax.div(d, 2), 4), lax.rem(d, 2), lax.axis_index("tensor")


def dp_at(x, y, c):
    return (x * 4 + y) * 2 + c


def beside(h, phase, step, x, y, c):
    if (h == 0) == (phase == 1):
        return {"dp": dp_at(lax.rem(x + step, 4), y, c)}
    return {"dp": dp_at(x, lax.rem(y + step, 4), c)}


def meet(x, y, c, t):
    barrier = pltpu.get_barrier_semaphore()
    partners = [
        {"dp": dp_at(lax.rem(x + 1, 4), y, c)},
        {"dp": dp_at(lax.rem(x + 3, 4), y, c)},
        {"dp": dp_at(x, lax.rem(y + 1, 4), c)},
        {"dp": dp_at(x, lax.rem(y + 3, 4), c)},
        {"dp": dp_at(x, y, 1 - c)},
        {"tensor": 1 - t},
        {"section": 1 - lax.axis_index("section")},
    ]
    for partner in partners:
        pl.semaphore_signal(barrier, inc=1, device_id=partner, device_id_type=MESH)
    pl.semaphore_wait(barrier, len(partners))


class Sender:
    def __init__(self, send_sems, recv_sems):
        self.send_sems, self.recv_sems, self.copies = send_sems, recv_sems, []

    def __call__(self, src, dst, where):
        i = len(self.copies)
        copy = pltpu.make_async_remote_copy(
            src_ref=src,
            dst_ref=dst,
            send_sem=self.send_sems.at[i],
            recv_sem=self.recv_sems.at[i],
            device_id=where,
            device_id_type=MESH,
        )
        copy.start()
        self.copies.append(copy)
        return copy

    def finish(self):
        for copy in self.copies:
            copy.wait_send()


N_GATHER = 143


def gather_kernel(shard, out, local_sem, send_sems, recv_sems):
    x, y, c, t = place()
    cols = shard.shape[-1]
    part_a, part_b = pl.ds(0, HALF_A), pl.ds(HALF_A, cols - HALF_A)
    meet(x, y, c, t)
    send = Sender(send_sems, recv_sems)
    sibling = {"dp": dp_at(x, y, 1 - c)}
    own = out.at[t, x, y, c]
    local = pltpu.make_async_copy(shard, own, local_sem)
    local.start()
    from_partner = send(shard, own, {"tensor": 1 - t})
    to_sibling = [send(shard, own, sibling)]

    def block(k, h, ja, jb):
        a, b = OFFSETS[ja], OFFSETS[jb]
        dx, dy = (a, b) if h == 0 else (b, a)
        return out.at[t if k == 0 else 1 - t, lax.rem(x + dx, 4), lax.rem(y + dy, 4), c, h]

    def both(k, h, phase, ja):
        dst = block(k, h, ja, 0)
        src = shard.at[h] if (k == 0 and ja == 0) else dst
        return (
            send(src, dst, beside(h, phase, 1, x, y, c)),
            send(src, dst, beside(h, phase, 3, x, y, c)),
        )

    def take(k, h, phase, ja, pair):
        onward = []
        for copy, j, part, step in ((pair[0], 1, part_a, 1), (pair[1], 2, part_b, 3)):
            copy.wait_recv()
            here = block(k, h, *((j, 0) if phase == 1 else (ja, j)))
            onward.append(send(here.at[:, part], here.at[:, part], beside(h, phase, step, x, y, c)))
            to_sibling.append(send(here, here, sibling))
        return onward

    first, second = {}, {}

    def begin(k):
        for h in (0, 1):
            first[k, h] = both(k, h, 1, 0)
        for h in (0, 1):
            second[k, h, 0] = both(k, h, 2, 0)

    mate = out.at[1 - t, x, y, c]
    onward, last = {}, {}

    def first_in(k):
        for h in (0, 1):
            onward[k, h] = take(k, h, 1, 0, first[k, h])
        for h in (0, 1):
            for ja in (1, 2):
                second[k, h, ja] = both(k, h, 2, ja)

    def far_in(k):
        for h in (0, 1):
            for copy in onward[k, h]:
                copy.wait_recv()
            second[k, h, 3] = both(k, h, 2, 3)
            here = block(k, h, 3, 0)
            to_sibling.append(send(here, here, sibling))

    def second_in(k, *places):
        for ja in places:
            for h in (0, 1):
                last[k, h, ja] = take(k, h, 2, ja, second[k, h, ja])

    def last_in(k):
        for ja in (0, 1, 2, 3):
            for h in (0, 1):
                for copy in last[k, h, ja]:
                    copy.wait_recv()
                here = block(k, h, ja, 3)
                to_sibling.append(send(here, here, sibling))

    begin(0)
    first_in(0)
    from_partner.wait_recv()
    begin(1)
    to_sibling.append(send(mate, mate, sibling))
    far_in(0)
    second_in(0, 0)
    first_in(1)
    second_in(0, 1, 2)
    far_in(1)
    second_in(1, 0)
    second_in(0, 3)
    second_in(1, 1, 2)
    last_in(0)
    second_in(1, 3)
    last_in(1)
    local.wait()
    for copy in to_sibling:
        copy.wait_recv()
    send.finish()


def gather_weights(shard):
    rows, cols = shard.shape
    out = pl.pallas_call(
        gather_kernel,
        out_shape=jax.ShapeDtypeStruct((2, 4, 4, 2, 2, 16, cols), jnp.bfloat16),
        in_specs=[pl.BlockSpec(memory_space=pl.ANY)],
        out_specs=pl.BlockSpec(memory_space=pl.ANY),
        scratch_shapes=[
            pltpu.SemaphoreType.DMA,
            pltpu.SemaphoreType.DMA((N_GATHER,)),
            pltpu.SemaphoreType.DMA((N_GATHER,)),
        ],
        compiler_params=pltpu.CompilerParams(collective_id=0, has_side_effects=True),
        name="gather_weights",
    )(shard.reshape(2, 16, cols))
    return out.reshape(2, 32 * rows, cols)


N_EACH = 60


def dot(a, b):
    return lax.dot_general(a, b, (((1,), (0,)), ((), ())), preferred_element_type=jnp.float32)


def dot_nt(a, b):
    return lax.dot_general(a, b, (((1,), (1,)), ((), ())), preferred_element_type=jnp.float32)


def dot_tn(a, b):
    return lax.dot_general(a, b, (((0,), (0,)), ((), ())), preferred_element_type=jnp.float32)


def low(v):
    return v.astype(jnp.bfloat16)


def high(v):
    return v.astype(jnp.float32)


def columns(start, size):
    return pl.ds(pl.multiple_of(start, 128), size)


def each(count, work):
    lax.fori_loop(0, count, lambda i, z: (work(i), z)[1], 0)


def total(v):
    return jnp.sum(v, axis=0, keepdims=True)


def normalize(values):
    centred = values - jnp.mean(values, -1, keepdims=True)
    inverse_std = lax.rsqrt(jnp.mean(centred * centred, -1, keepdims=True) + epsilon)
    return centred * inverse_std, inverse_std


def norm_backward(grad_norm, normed, inverse_std):
    return inverse_std * (
        grad_norm
        - jnp.mean(grad_norm, -1, keepdims=True)
        - normed * jnp.mean(grad_norm * normed, -1, keepdims=True)
    )


def layers_kernel(
    lengths, ends, full, gains, shifts, b_qv, b_ff,
    ends_out, out,
    d_gains, d_shifts, d_bqv, d_bff,
    w, x_own, x_in, relay, q, k, v, o, probs, n1, n2, i1, i2, res, hid, act, slope, d_act, d_qkv,
    acc, d_low, a_low, kept, small,
    s_x, s_hid, s_d_low, s_a_low, s_act, s_d_act, s_o, s_d_qkv, s_small,
    passing, near_p, near_m, q_passing, q_p, q_m, mate, to_mate,
    load_sems, io_sems, send_sems, recv_sems,
):
    x, y, c, t = place()
    s = lax.axis_index("section")
    loads = {}
    own_load = pltpu.make_async_copy(ends.at[t], x_own, io_sems.at[0])
    own_load.start()
    for n, (start, size) in enumerate(CHUNKS):
        for half in (0, 1):
            part = pl.ds(start, size)
            load = pltpu.make_async_copy(
                full.at[half, :, part], w.at[half, :, part], load_sems.at[2 * n + half]
            )
            load.start()
            loads[n, half] = load

    meet(x, y, c, t)
    send = Sender(send_sems, recv_sems)
    sibling = {"dp": dp_at(x, y, 1 - c)}
    given = {}

    def ready(n):
        for half in (0, 1):
            if (n, half) in loads:
                loads.pop((n, half)).wait()

    length = lengths[t, 0]
    first_half = lax.broadcasted_iota(jnp.int32, (ROWS, 128), 1) < HD
    valid = lax.broadcasted_iota(jnp.int32, (ROWS, ROWS), 1) < length
    scale = HD**-0.5

    def pick(e, value):
        return jnp.where(first_half == (e == 0), value, jnp.zeros_like(value))

    def forward(x):
        ready(0)

        def project(i):
            half, j = lax.div(i, 3), lax.rem(i, 3)
            p = dot(x[...], w[half, :, columns(j * BLOCK, BLOCK)])
            at = columns(half * BLOCK, BLOCK)

            @pl.when(j == 0)
            def _():
                q[:, at] = low(p + b_qv[0:1, at])

            @pl.when(j == 1)
            def _():
                k[:, at] = low(p)

            @pl.when(j == 2)
            def _():
                v[:, at] = low(p + b_qv[1:2, at])

        each(6, project)

        def heads(i):
            at = columns(i * 128, 128)
            kp, vp, qp = k[:, at], v[:, at], q[:, at]
            outs = []
            for e in (0, 1):
                scores = dot_nt(pick(e, qp), kp) * scale
                scores = jnp.where(valid, scores, -1e9)
                powers = jnp.exp(scores - jnp.max(scores, -1, keepdims=True))
                p = powers / jnp.sum(powers, -1, keepdims=True)
                probs[2 * i + e] = p
                outs.append(dot(low(p), vp))
            o[:, at] = low(jnp.where(first_half, outs[0], outs[1]))

        each(8, heads)
        ready(1)
        attended = dot_nt(o[:, 0:512], w[0, :, 1536:2048]) + dot_nt(o[:, 512:1024], w[1, :, 1536:2048])
        normed, inverse = normalize(high(x[...]) + attended + shifts[0:1])
        n1[...], i1[...] = normed, inverse
        hidden = normed * gains[0:1] + shifts[1:2]
        res[...] = hidden
        hid[...] = low(hidden)
        ready(2)

        def widen(i):
            half, j = lax.div(i, 4), lax.rem(i, 4)
            at = columns(i * BLOCK, BLOCK)
            u = dot(hid[...], w[half, :, columns(UP + j * BLOCK, BLOCK)]) + b_ff[:, at]
            phi = 0.5 + 0.5 * lax.erf(u * 0.7071067811865476)
            act[:, at] = low(u * phi)
            slope[:, at] = low(phi + u * (jnp.exp(u * u * -0.5) * 0.3989422804014327))

        each(8, widen)
        ready(3)

        def narrow(i):
            at = columns(i * 256, 256)
            rows = pl.ds(pl.multiple_of(i * 256, 256), 256)
            acc[:, at] = dot_nt(act[:, 0:2048], w[0, rows, DOWN:COLS]) + dot_nt(
                act[:, 2048:4096], w[1, rows, DOWN:COLS]
            )

        each(4, narrow)
        normed, inverse = normalize(res[...] + acc[...] + shifts[2:3])
        n2[...], i2[...] = normed, inverse
        return low(normed * gains[1:2] + shifts[3:4])

    def backward(grad_out, after=lambda stage: None):
        normed = n2[...]
        d_gains[1:2] = total(grad_out * normed)
        d_shifts[3:4] = total(grad_out)
        d_sum = norm_backward(grad_out * gains[1:2], normed, i2[...])
        d_shifts[2:3] = total(d_sum)
        res[...] = d_sum
        d_low[...] = low(d_sum)
        after("d_low")

        def widen(i):
            half, j = lax.div(i, 4), lax.rem(i, 4)
            at = columns(i * BLOCK, BLOCK)
            d = low(dot(d_low[...], w[half, :, columns(DOWN + j * BLOCK, BLOCK)]) * high(slope[:, at]))
            d_act[:, at] = d
            d_bff[:, at] = total(high(d))

        each(8, widen)
        after("d_act")

        def narrow(i):
            at = columns(i * 256, 256)
            rows = pl.ds(pl.multiple_of(i * 256, 256), 256)
            acc[:, at] = dot_nt(d_act[:, 0:2048], w[0, rows, UP:DOWN]) + dot_nt(
                d_act[:, 2048:4096], w[1, rows, UP:DOWN]
            )

        each(4, narrow)
        d_hidden = res[...] + acc[...]
        normed = n1[...]
        d_gains[0:1] = total(d_hidden * normed)
        d_shifts[1:2] = total(d_hidden)
        d_sum = norm_backward(d_hidden * gains[0:1], normed, i1[...])
        d_shifts[0:1] = total(d_sum)
        res[...] = d_sum
        a_low[...] = low(d_sum)
        after("a_low")

        def heads(i):
            at = columns(i * 128, 128)
            half = lax.div(i, 4)
            d_o = low(dot(a_low[...], w[half, :, columns(1536 + lax.rem(i, 4) * 128, 128)]))
            kp, vp, qp = k[:, at], v[:, at], q[:, at]
            parts = []
            for e in (0, 1):
                p = probs[2 * i + e]
                d_p = dot_nt(pick(e, d_o), vp)
                d_s = low(p * (d_p - jnp.sum(p * d_p, -1, keepdims=True)))
                parts.append((dot(d_s, kp) * scale, dot_tn(d_s, qp) * scale, dot_tn(low(p), d_o)))
            d_q, d_k, d_v = (low(jnp.where(first_half, a, b)) for a, b in zip(*parts))
            d_qkv[0, :, at] = d_q
            d_qkv[1, :, at] = d_k
            d_qkv[2, :, at] = d_v
            d_bqv[0:1, at] = total(high(d_q))
            d_bqv[1:2, at] = total(high(d_v))

        each(8, heads)
        after("d_qkv")

        def narrow_in(i):
            at = columns(i * 256, 256)
            rows = pl.ds(pl.multiple_of(i * 256, 256), 256)
            acc[:, at] = sum(
                dot_nt(d_qkv[j, :, 512 * half : 512 * half + 512], w[half, rows, 512 * j : 512 * j + 512])
                for half in (0, 1)
                for j in (0, 1, 2)
            )

        each(4, narrow_in)
        return low(res[...] + acc[...])

    other_half = columns((1 - c) * 2048, 2048)
    other_heads = columns((1 - c) * 512, 512)

    def swap(name, src, dst):
        given[name] = send(src, dst, sibling)

    def have(*names):
        for name in names:
            given[name].wait_recv()

    def block(start, left, right, s_left, s_right):
        whole = low(dot_tn(left, right) + dot_tn(s_left, s_right))
        for chip in range(16):
            for h in (0, 1):
                f, g = (chip // 4, chip % 4) if h == 0 else (chip % 4, chip // 4)
                to, of = h * 512 + f * 128 + g * 32, chip * 64 + h * 32
                w[0, to : to + 32, columns(start, right.shape[1])] = whole[of : of + 32]

    def grads_down():
        have("act", "d_low")

        def one(i):
            at = columns(i * BLOCK, BLOCK)
            block(DOWN + i * BLOCK, d_low[...], act[:, columns(c * 2048 + i * BLOCK, BLOCK)], s_d_low[...], s_act[:, at])

        each(4, one)

    def grads_up():
        have("hid", "d_act")

        def one(i):
            at = columns(i * BLOCK, BLOCK)
            block(UP + i * BLOCK, hid[...], d_act[:, columns(c * 2048 + i * BLOCK, BLOCK)], s_hid[...], s_d_act[:, at])

        each(4, one)

    def spread(row, size, offset):
        lanes = row.shape[1]
        wide = (32, lanes)
        owner = lax.broadcasted_iota(jnp.int32, wide, 0) == lax.div(
            lax.broadcasted_iota(jnp.int32, wide, 1), size
        )
        fold = lax.rem(lax.broadcasted_iota(jnp.int32, (lanes, 128), 0), size) == lax.broadcasted_iota(
            jnp.int32, (lanes, 128), 1
        )
        table = dot(low(jnp.where(owner, row, 0.0)), low(jnp.where(fold, 1.0, 0.0)))
        back = (128, 1024)
        lane = lax.broadcasted_iota(jnp.int32, back, 1)
        source = lax.broadcasted_iota(jnp.int32, back, 0)
        span = min(size, 32)
        place_in = lax.rem(lane, 32)
        if size == 16:
            open_ = (place_in == source + offset) & (source < span)
        else:
            open_ = (place_in + offset == source) & (source < size)
        rows = dot(low(table), low(jnp.where(open_, 1.0, 0.0)))
        mine = lax.broadcasted_iota(jnp.int32, (32, 1024), 0) == lax.div(
            lax.broadcasted_iota(jnp.int32, (32, 1024), 1), 32
        )
        return total(jnp.where(mine, rows, 0.0))

    def small_rows(half, dst):
        heads_at, units_at = columns(half * 512, 512), columns(half * 2048, 2048)
        dst[...] = jnp.zeros_like(dst)
        dst[0:2] = d_gains[...]
        dst[2:6] = d_shifts[...]
        dst[6:7] = spread(d_bqv[0:1, heads_at], 16, 0) + spread(d_bqv[1:2, heads_at], 16, 16)
        dst[7:8] = spread(d_bff[:, units_at], 64, 0)
        dst[8:9] = spread(d_bff[:, units_at], 64, 32)

    def grads_rest():
        have("o", "a_low", "x", "d_qkv", "small")
        block(1536, a_low[...], o[:, columns(c * 512, 512)], s_a_low[...], s_o[...])
        for j in (0, 1, 2):
            block(j * 512, x_in[...], d_qkv[j, :, columns(c * 512, 512)], s_x[...], s_d_qkv[j])
        summed = small[0] + s_small[...]
        column = low(jnp.concatenate([summed, jnp.zeros((112, 1024), jnp.float32)], axis=0).T)
        for chip in range(16):
            for h in (0, 1):
                f, g = (chip // 4, chip % 4) if h == 0 else (chip % 4, chip // 4)
                to, of = h * 512 + f * 128 + g * 32, chip * 64 + h * 32
                w[0, to : to + 32, EXTRA:UP] = column[of : of + 32]

    sent = {}

    def side(h, phase):
        return x if (h == 0) == (phase == 1) else y

    def rows_at(h, step):
        return pl.ds(pl.multiple_of(h * 512 + lax.rem(side(h, 1) + step, 4) * 128, 128), 128)

    def line_at(h, step):
        start = h * 512 + side(h, 1) * 128 + lax.rem(side(h, 2) + step, 4) * 32
        return pl.ds(pl.multiple_of(start, 32), 32)

    def parts(n):
        start, size, half = PASSES[n]
        return pl.ds(start, size), pl.ds(start, half), pl.ds(start + half, size - half)

    def add(dst, *others):
        def one(i):
            at = pl.ds(pl.multiple_of(i * 16, 16), 16)
            dst[at] = low(sum((high(o[at]) for o in others), high(dst[at])))

        each(dst.shape[0] // 16, one)

    def far(n):
        whole, part_a, part_b = parts(n)
        for h in (0, 1):
            rows = rows_at(h, 2)
            sent[n, h, "far"] = (
                send(w.at[0, rows, part_a], passing.at[h, :, part_a], beside(h, 1, 1, x, y, c)),
                send(w.at[0, rows, part_b], passing.at[h, :, part_b], beside(h, 1, 3, x, y, c)),
            )

    def near(n):
        whole, part_a, part_b = parts(n)
        for h in (0, 1):
            up, down = sent[n, h, "far"]
            up.wait_recv()
            add(w.at[0, rows_at(h, 1), part_a], passing.at[h, :, part_a])
            one = send(w.at[0, rows_at(h, 1), whole], near_p.at[h, :, whole], beside(h, 1, 1, x, y, c))
            down.wait_recv()
            add(w.at[0, rows_at(h, 3), part_b], passing.at[h, :, part_b])
            two = send(w.at[0, rows_at(h, 3), whole], near_m.at[h, :, whole], beside(h, 1, 3, x, y, c))
            sent[n, h, "near"] = (one, two)

    def q_far(n):
        whole, part_a, part_b = parts(n)
        for h in (0, 1):
            for copy in sent[n, h, "near"]:
                copy.wait_recv()
            add(w.at[0, rows_at(h, 0), whole], near_p.at[h, :, whole], near_m.at[h, :, whole])
            rows = line_at(h, 2)
            sent[n, h, "q_far"] = (
                send(w.at[0, rows, part_a], q_passing.at[h, :, part_a], beside(h, 2, 1, x, y, c)),
                send(w.at[0, rows, part_b], q_passing.at[h, :, part_b], beside(h, 2, 3, x, y, c)),
            )

    def q_near(n):
        whole, part_a, part_b = parts(n)
        for h in (0, 1):
            up, down = sent[n, h, "q_far"]
            up.wait_recv()
            add(w.at[0, line_at(h, 1), part_a], q_passing.at[h, :, part_a])
            one = send(w.at[0, line_at(h, 1), whole], q_p.at[h, :, whole], beside(h, 2, 1, x, y, c))
            down.wait_recv()
            add(w.at[0, line_at(h, 3), part_b], q_passing.at[h, :, part_b])
            two = send(w.at[0, line_at(h, 3), whole], q_m.at[h, :, whole], beside(h, 2, 3, x, y, c))
            sent[n, h, "q_near"] = (one, two)

    crossing, handing = {}, {}
    owner, sender = c == t, c != t

    def remote(i, src, dst, where):
        return pltpu.make_async_remote_copy(
            src_ref=src,
            dst_ref=dst,
            send_sem=send_sems.at[N_EACH + i],
            recv_sem=recv_sems.at[N_EACH + i],
            device_id=where,
            device_id_type=MESH,
        )

    def cross(n):
        whole, _, _ = parts(n)
        for h in (0, 1):
            for copy in sent[n, h, "q_near"]:
                copy.wait_recv()
            add(w.at[0, line_at(h, 0), whole], q_p.at[h, :, whole], q_m.at[h, :, whole])
            crossing[n, h] = remote(
                2 * n + h, w.at[0, line_at(h, 0), whole], mate.at[h, :, whole], {"tensor": 1 - t}
            )

            @pl.when(sender)
            def _():
                crossing[n, h].start()

    def hand(n):
        whole, _, _ = parts(n)
        handing[n] = remote(6 + n, to_mate.at[:, whole], out.at[:, whole], sibling)

        @pl.when(owner)
        def _():
            for h in (0, 1):
                crossing[n, h].wait_recv()
                value = high(w[0, line_at(h, 0), whole]) + high(mate[h, :, whole])

                @pl.when(c == h)
                def _():
                    out[:, whole] = value

                @pl.when(c != h)
                def _():
                    to_mate[:, whole] = value

            handing[n].start()

    def exchange(n):
        copy = send(kept.at[n], relay.at[n], {"section": 1 - s})
        copy.wait_recv()
        return relay[n]

    def last_stage(stage):
        if stage == "d_low":
            swap("d_low", d_low, s_d_low)
        if stage == "d_act":
            swap("d_act", d_act.at[:, other_half], s_d_act)
            grads_down()
            far(0)
        if stage == "a_low":
            swap("a_low", a_low, s_a_low)
            grads_up()
            far(1)
            near(0)
        if stage == "d_qkv":
            swap("d_qkv", d_qkv.at[:, :, other_heads], s_d_qkv)
            small_rows(1 - c, small.at[1])
            swap("small", small.at[1], s_small)
            near(1)

    own_load.wait()
    kept[0] = forward(x_own)
    x_in[...] = jnp.where(s == 0, x_own[...], exchange(0))
    swap("x", x_in, s_x)
    result = forward(x_in)
    swap("hid", hid, s_hid)
    swap("act", act.at[:, other_half], s_act)
    swap("o", o.at[:, other_heads], s_o)
    kept[2] = result
    kept[1] = backward(high(x_own[...]))
    grad_out = jnp.where(s == 1, x_own[...], exchange(1))
    d_x = backward(high(grad_out), last_stage)
    kept[2] = jnp.where(s == 0, d_x, kept[2])
    across = send(kept.at[2], ends_out.at[t], {"tensor": 1 - t})
    here = pltpu.make_async_copy(kept.at[2], ends_out.at[t], io_sems.at[1])
    here.start()
    small_rows(c, small.at[0])
    grads_rest()
    far(2)
    q_far(0)
    near(2)
    q_far(1)
    q_near(0)
    q_near(1)
    cross(0)
    q_far(2)
    cross(1)
    hand(0)
    q_near(2)
    hand(1)
    cross(2)
    hand(2)
    for n in (0, 1, 2):

        @pl.when(sender)
        def _():
            handing[n].wait_recv()
            for h in (0, 1):
                crossing[n, h].wait_send()

        @pl.when(owner)
        def _():
            handing[n].wait_send()

    here.wait()
    across.wait_recv()
    send.finish()


def run_layers(lengths, ends, full, gains, shifts, b_qv, b_ff):
    vmem = pltpu.VMEM
    bf, f32 = jnp.bfloat16, jnp.float32
    hbm = pl.BlockSpec(memory_space=pl.ANY)
    near = pl.BlockSpec(memory_space=vmem)
    sem = pltpu.SemaphoreType.DMA
    shape = jax.ShapeDtypeStruct
    return pl.pallas_call(
        layers_kernel,
        out_shape=(
            shape((2, ROWS, 1024), bf),
            shape((32, COLS), f32),
        ),
        in_specs=[pl.BlockSpec(memory_space=pltpu.SMEM), hbm, hbm, near, near, near, near],
        out_specs=(hbm, near),
        scratch_shapes=[
            vmem((2, 1024), f32),
            vmem((4, 1024), f32),
            vmem((2, 1024), f32),
            vmem((1, 4096), f32),
            vmem((2, 1024, COLS), bf),
            vmem((ROWS, 1024), bf),
            vmem((ROWS, 1024), bf),
            vmem((2, ROWS, 1024), bf),
            vmem((ROWS, 1024), bf),
            vmem((ROWS, 1024), bf),
            vmem((ROWS, 1024), bf),
            vmem((ROWS, 1024), bf),
            vmem((16, ROWS, ROWS), f32),
            vmem((ROWS, 1024), f32),
            vmem((ROWS, 1024), f32),
            vmem((ROWS, 1), f32),
            vmem((ROWS, 1), f32),
            vmem((ROWS, 1024), f32),
            vmem((ROWS, 1024), bf),
            vmem((ROWS, 4096), bf),
            vmem((ROWS, 4096), bf),
            vmem((ROWS, 4096), bf),
            vmem((3, ROWS, 1024), bf),
            vmem((ROWS, 1024), f32),
            vmem((ROWS, 1024), bf),
            vmem((ROWS, 1024), bf),
            vmem((3, ROWS, 1024), bf),
            vmem((2, 16, 1024), f32),
            vmem((ROWS, 1024), bf),
            vmem((ROWS, 1024), bf),
            vmem((ROWS, 1024), bf),
            vmem((ROWS, 1024), bf),
            vmem((ROWS, 2048), bf),
            vmem((ROWS, 2048), bf),
            vmem((ROWS, 512), bf),
            vmem((3, ROWS, 512), bf),
            vmem((16, 1024), f32),
            vmem((2, 128, COLS), bf),
            vmem((2, 128, COLS), bf),
            vmem((2, 128, COLS), bf),
            vmem((2, 32, COLS), bf),
            vmem((2, 32, COLS), bf),
            vmem((2, 32, COLS), bf),
            vmem((2, 32, COLS), bf),
            vmem((32, COLS), f32),
            sem((8,)),
            sem((2,)),
            sem((N_EACH + 9,)),
            sem((N_EACH + 9,)),
        ],
        compiler_params=pltpu.CompilerParams(
            collective_id=2, has_side_effects=True, vmem_limit_bytes=62 * 2**20
        ),
        name="run_layers",
    )(lengths, ends, full, gains, shifts, b_qv, b_ff)


def pack_shard(w_qkv, w_out, w_up, w_down, gains, shifts, b_qv, b_ff):
    extra = jnp.concatenate(
        [gains[0].T, shifts[0].T, b_qv[0, :, 0].reshape(32, 1), b_ff[0, 0].reshape(2, 32).T], axis=1
    )
    return jnp.concatenate(
        [
            w_qkv[0].reshape(32, 1536),
            w_out[0].T,
            jnp.pad(extra, ((0, 0), (0, 119))),
            w_up[0],
            w_down[0].T,
        ],
        axis=1,
    )


def unpack_extra(extra):
    extra = extra.astype(jnp.float32)
    gains = extra[0, :, 0:2].T
    shifts = extra[0, :, 2:6].T
    b_qv = extra[:, :, 6].reshape(2, 32, 2, 16).transpose(2, 0, 1, 3).reshape(2, 1024)
    b_ff = extra[:, :, 7:9].reshape(2, 32, 32, 2).transpose(0, 1, 3, 2).reshape(4096)
    return gains, shifts, b_qv, b_ff


def unpack_shard(got):
    extra = got[:, EXTRA:UP]
    return (
        got[:, :1536].reshape(1, 32, 3, 512),
        got[:, 1536:2048].T[None],
        got[:, UP:DOWN][None],
        got[:, DOWN:].T[None],
        extra[:, 0:2].T[None],
        extra[:, 2:6].T[None],
        extra[:, 6].reshape(1, 2, 1, 16),
        extra[:, 7:9].T.reshape(1, 1, 64),
    )


def body(ends, lengths, w_qkv, w_out, w_up, w_down, gains, shifts, b_qv, b_ff):
    full = gather_weights(pack_shard(w_qkv, w_out, w_up, w_down, gains, shifts, b_qv, b_ff))
    gains, shifts, b_qv, b_ff = unpack_extra(full[:, :, EXTRA:UP])
    ends_out, got = run_layers(
        lengths, ends.reshape(2, ROWS, 1024), full, gains, shifts, b_qv, b_ff.reshape(1, 4096)
    )
    return (ends_out.reshape(1, 2, 1, ROWS, 1024),) + unpack_shard(got)


def solution(mesh):
    in_specs = (
        P("section", None, "dp", None, None),
        P(None, "dp"),
        P("section", "dp", None, "tensor"),
        P("section", "tensor", "dp"),
        P("section", "dp", "tensor"),
        P("section", "tensor", "dp"),
        P("section", None, "dp"),
        P("section", None, "dp"),
        P("section", None, "tensor", "dp"),
        P("section", "tensor", "dp"),
    )
    out_specs = (
        P("section", None, "dp", None, None),
        P("section", "dp", None, "tensor"),
        P("section", "tensor", "dp"),
        P("section", "dp", "tensor"),
        P("section", "tensor", "dp"),
        P("section", None, "dp"),
        P("section", None, "dp"),
        P("section", None, "tensor", "dp"),
        P("section", "tensor", "dp"),
    )
    return jax.shard_map(body, mesh=mesh, in_specs=in_specs, out_specs=out_specs, check_vma=False)
```

```python
import jax
import jax.numpy as jnp
from jax import lax
from jax.experimental import pallas as pl
from jax.experimental.pallas import tpu as pltpu
from jax.sharding import PartitionSpec as P

HD = 64
epsilon = 1e-05

COLS = 6272
ROWS = 192
BLOCK = 512
EXTRA, UP, DOWN = 2048, 2176, 4224
GATHERS = ((0, 2176, 1152), (UP, 2048, 1024), (DOWN, 2048, 1024))
PASSES = ((DOWN, 2048, 1024), (UP, 2048, 1024), (0, 2176, 1152))


OFFSETS = (0, 3, 1, 2)
MESH = pl.DeviceIdType.MESH


def place():
    d = lax.axis_index("dp")
    return lax.div(d, 8), lax.rem(lax.div(d, 2), 4), lax.rem(d, 2), lax.axis_index("tensor")


def dp_at(x, y, c):
    return (x * 4 + y) * 2 + c


def beside(h, phase, step, x, y, c):
    if (h == 0) == (phase == 1):
        return {"dp": dp_at(lax.rem(x + step, 4), y, c)}
    return {"dp": dp_at(x, lax.rem(y + step, 4), c)}


def meet(x, y, c, t):
    barrier = pltpu.get_barrier_semaphore()
    partners = [
        {"dp": dp_at(lax.rem(x + 1, 4), y, c)},
        {"dp": dp_at(lax.rem(x + 3, 4), y, c)},
        {"dp": dp_at(x, lax.rem(y + 1, 4), c)},
        {"dp": dp_at(x, lax.rem(y + 3, 4), c)},
        {"dp": dp_at(x, y, 1 - c)},
        {"tensor": 1 - t},
        {"section": 1 - lax.axis_index("section")},
    ]
    for partner in partners:
        pl.semaphore_signal(barrier, inc=1, device_id=partner, device_id_type=MESH)
    pl.semaphore_wait(barrier, len(partners))


class Sender:
    def __init__(self, send_sems, recv_sems):
        self.send_sems, self.recv_sems, self.copies = send_sems, recv_sems, []

    def __call__(self, src, dst, where):
        i = len(self.copies)
        copy = pltpu.make_async_remote_copy(
            src_ref=src,
            dst_ref=dst,
            send_sem=self.send_sems.at[i],
            recv_sem=self.recv_sems.at[i],
            device_id=where,
            device_id_type=MESH,
        )
        copy.start()
        self.copies.append(copy)
        return copy

    def finish(self):
        for copy in self.copies:
            copy.wait_send()


N_EACH = 60
N_GATHER = 147


def dot(a, b):
    return lax.dot_general(a, b, (((1,), (0,)), ((), ())), preferred_element_type=jnp.float32)


def dot_nt(a, b):
    return lax.dot_general(a, b, (((1,), (1,)), ((), ())), preferred_element_type=jnp.float32)


def dot_tn(a, b):
    return lax.dot_general(a, b, (((0,), (0,)), ((), ())), preferred_element_type=jnp.float32)


def low(v):
    return v.astype(jnp.bfloat16)


def high(v):
    return v.astype(jnp.float32)


def columns(start, size):
    return pl.ds(pl.multiple_of(start, 128), size)


def each(count, work):
    lax.fori_loop(0, count, lambda i, z: (work(i), z)[1], 0)


def total(v):
    return jnp.sum(v, axis=0, keepdims=True)


def normalize(values):
    centred = values - jnp.mean(values, -1, keepdims=True)
    inverse_std = lax.rsqrt(jnp.mean(centred * centred, -1, keepdims=True) + epsilon)
    return centred * inverse_std, inverse_std


def norm_backward(grad_norm, normed, inverse_std):
    return inverse_std * (
        grad_norm
        - jnp.mean(grad_norm, -1, keepdims=True)
        - normed * jnp.mean(grad_norm * normed, -1, keepdims=True)
    )


def layers_kernel(
    lengths, ends, my_qkv, my_out, my_up, my_down, my_small,
    ends_out, out,
    gains, shifts, b_qv, b_ff,
    d_gains, d_shifts, d_bqv, d_bff,
    blocks, x_own, x_in, relay, q, k, v, o, probs, n1, n2, i1, i2, res, hid, act, slope, d_act, d_qkv,
    acc, d_low, a_low, kept, small,
    s_x, s_hid, s_d_low, s_a_low, s_act, s_d_act, s_o, s_d_qkv, s_small,
    passing, near_p, near_m, q_passing, q_p, q_m, mate, to_mate,
    io_sems, send_sems, recv_sems, gather_send_sems, gather_recv_sems,
):
    x, y, c, t = place()
    s = lax.axis_index("section")
    w = blocks.reshape(2, 1024, COLS)
    own_load = pltpu.make_async_copy(ends.at[t], x_own, io_sems.at[0])
    own_load.start()
    own = blocks.at[t, x, y, c]
    own[:, :, 0:1536] = my_qkv[...].reshape(2, 16, 1536)
    own[:, :, 1536:EXTRA] = my_out[...].reshape(2, 16, 512)
    own[:, :, EXTRA:UP] = low(my_small[...].T)[0:32].reshape(2, 16, 128)
    own[:, :, UP:DOWN] = my_up[...].reshape(2, 16, 2048)
    own[:, :, DOWN:COLS] = my_down[...].reshape(2, 16, 2048)
    meet(x, y, c, t)
    send = Sender(send_sems, recv_sems)
    share = Sender(gather_send_sems, gather_recv_sems)
    sibling = {"dp": dp_at(x, y, 1 - c)}
    given, shared, to_sibling = {}, {}, {0: [], 1: [], 2: []}

    def half_block(n, kk, h, step):
        start, size, _ = GATHERS[n]
        tt = t if kk == 0 else 1 - t
        xx, yy = (lax.rem(x + step, 4), y) if h == 0 else (x, lax.rem(y + step, 4))
        return blocks.at[tt, xx, yy, c, h, :, pl.ds(start, size)]

    def lane_of(n, kk, h, step):
        start, size, _ = GATHERS[n]
        tt = t if kk == 0 else 1 - t
        if h == 0:
            return blocks.at[tt, :, lax.rem(y + step, 4), c, 0, :, pl.ds(start, size)]
        return blocks.at[tt, lax.rem(x + step, 4), :, c, 1, :, pl.ds(start, size)]

    def part_of(n, ref, first):
        _, size, half = GATHERS[n]
        part = pl.ds(0, half) if first else pl.ds(half, size - half)
        return ref.at[:, part] if len(ref.shape) == 2 else ref.at[:, :, part]

    def first_send(n, kk):
        for h in (0, 1):
            src = half_block(n, kk, h, 0)
            shared[n, kk, h, 1] = [share(src, src, beside(h, 1, step, x, y, c)) for step in (1, 3)]

    def pass_on(n, kk, h, phase, find):
        onward = []
        for copy, step in zip(shared[n, kk, h, phase], (1, 3)):
            copy.wait_recv()
            here = find(n, kk, h, 4 - step)
            part = part_of(n, here, step == 1)
            onward.append(share(part, part, beside(h, phase, step, x, y, c)))
            if phase == 2:
                to_sibling[n].append(share(here, here, sibling))
        shared[n, kk, h, phase] = onward

    def first_on(n, kk):
        for h in (0, 1):
            pass_on(n, kk, h, 1, half_block)

    def second_send(n, kk):
        for h in (0, 1):
            for copy in shared[n, kk, h, 1]:
                copy.wait_recv()
            src = lane_of(n, kk, h, 0)
            shared[n, kk, h, 2] = [share(src, src, beside(h, 2, step, x, y, c)) for step in (1, 3)]
            to_sibling[n].append(share(src, src, sibling))

    def second_on(n, kk):
        for h in (0, 1):
            pass_on(n, kk, h, 2, lane_of)

    def second_end(n, kk):
        for h in (0, 1):
            for copy in shared[n, kk, h, 2]:
                copy.wait_recv()
            here = lane_of(n, kk, h, 2)
            to_sibling[n].append(share(here, here, sibling))

    def complete(n):
        for copy in to_sibling[n]:
            copy.wait_recv()

    def collect(half, rows):
        wide = (32, 1024)
        owner_of = lax.broadcasted_iota(jnp.int32, wide, 0) == lax.div(
            lax.broadcasted_iota(jnp.int32, wide, 1), 32
        )
        fold = lax.rem(lax.broadcasted_iota(jnp.int32, (1024, 128), 0), 32) == lax.broadcasted_iota(
            jnp.int32, (1024, 128), 1
        )
        fold = low(jnp.where(fold, 1.0, 0.0))
        tables = [low(dot(low(jnp.where(owner_of, row, 0.0)), fold)) for row in rows]

        def open_up(size, *terms):
            lanes = size * 32
            lane = lax.broadcasted_iota(jnp.int32, (128, lanes), 1)
            source = lax.broadcasted_iota(jnp.int32, (128, lanes), 0)
            found = jnp.zeros((32, lanes), jnp.float32)
            for table, offset in terms:
                pick_at = (lax.rem(lane, size) + offset == source) & (source < 32)
                found = found + dot(table, low(jnp.where(pick_at, 1.0, 0.0)))
            mine = lax.broadcasted_iota(jnp.int32, (32, lanes), 0) == lax.div(
                lax.broadcasted_iota(jnp.int32, (32, lanes), 1), size
            )
            return total(jnp.where(mine, found, 0.0))

        at = pl.ds(half * 512, 512)
        b_qv[0:1, at] = open_up(16, (tables[0], 0))
        b_qv[1:2, at] = open_up(16, (tables[0], 16))
        b_ff[:, pl.ds(half * 2048, 2048)] = open_up(64, (tables[1], 0), (tables[2], -32))

    def take_parameters():
        for half in (0, 1):
            rows = high(w[half, :, EXTRA:UP]).T
            if half == 0:
                gains[...] = rows[0:2]
                shifts[...] = rows[2:6]
            collect(half, (rows[6:7], rows[7:8], rows[8:9]))

    length = lengths[t, 0]
    first_half = lax.broadcasted_iota(jnp.int32, (ROWS, 128), 1) < HD
    valid = lax.broadcasted_iota(jnp.int32, (ROWS, ROWS), 1) < length
    scale = HD**-0.5

    def pick(e, value):
        return jnp.where(first_half == (e == 0), value, jnp.zeros_like(value))

    def forward(x, after=lambda stage: None):

        def project(i):
            half, j = lax.div(i, 3), lax.rem(i, 3)
            p = dot(x[...], w[half, :, columns(j * BLOCK, BLOCK)])
            at = columns(half * BLOCK, BLOCK)

            @pl.when(j == 0)
            def _():
                q[:, at] = low(p + b_qv[0:1, at])

            @pl.when(j == 1)
            def _():
                k[:, at] = low(p)

            @pl.when(j == 2)
            def _():
                v[:, at] = low(p + b_qv[1:2, at])

        each(6, project)
        after("qkv")

        def heads(i):
            at = columns(i * 128, 128)
            kp, vp, qp = k[:, at], v[:, at], q[:, at]
            outs = []
            for e in (0, 1):
                scores = dot_nt(pick(e, qp), kp) * scale
                scores = jnp.where(valid, scores, -1e9)
                powers = jnp.exp(scores - jnp.max(scores, -1, keepdims=True))
                p = low(powers / jnp.sum(powers, -1, keepdims=True))
                probs[2 * i + e] = p
                outs.append(dot(p, vp))
            o[:, at] = low(jnp.where(first_half, outs[0], outs[1]))

        each(8, heads)
        after("heads")
        attended = dot_nt(o[:, 0:512], w[0, :, 1536:2048]) + dot_nt(o[:, 512:1024], w[1, :, 1536:2048])
        normed, inverse = normalize(high(x[...]) + attended + shifts[0:1])
        n1[...], i1[...] = normed, inverse
        hidden = normed * gains[0:1] + shifts[1:2]
        res[...] = hidden
        hid[...] = low(hidden)
        after("hid")

        def widen(i):
            half, j = lax.div(i, 4), lax.rem(i, 4)
            at = columns(i * BLOCK, BLOCK)
            u = dot(hid[...], w[half, :, columns(UP + j * BLOCK, BLOCK)]) + b_ff[:, at]
            phi = 0.5 + 0.5 * lax.erf(u * 0.7071067811865476)
            act[:, at] = low(u * phi)
            slope[:, at] = low(phi + u * (jnp.exp(u * u * -0.5) * 0.3989422804014327))

        each(8, widen)
        after("act")

        def narrow(i):
            at = columns(i * 256, 256)
            rows = pl.ds(pl.multiple_of(i * 256, 256), 256)
            acc[:, at] = dot_nt(act[:, 0:2048], w[0, rows, DOWN:COLS]) + dot_nt(
                act[:, 2048:4096], w[1, rows, DOWN:COLS]
            )

        each(4, narrow)
        normed, inverse = normalize(res[...] + acc[...] + shifts[2:3])
        n2[...], i2[...] = normed, inverse
        return low(normed * gains[1:2] + shifts[3:4])

    def backward(grad_out, after=lambda stage: None):
        normed = n2[...]
        d_gains[1:2] = total(grad_out * normed)
        d_shifts[3:4] = total(grad_out)
        d_sum = norm_backward(grad_out * gains[1:2], normed, i2[...])
        d_shifts[2:3] = total(d_sum)
        res[...] = d_sum
        d_low[...] = low(d_sum)
        after("d_low")

        def widen(i):
            half, j = lax.div(i, 4), lax.rem(i, 4)
            at = columns(i * BLOCK, BLOCK)
            d = low(dot(d_low[...], w[half, :, columns(DOWN + j * BLOCK, BLOCK)]) * high(slope[:, at]))
            d_act[:, at] = d
            d_bff[:, at] = total(high(d))

        each(8, widen)
        after("d_act")

        def narrow(i):
            at = columns(i * 256, 256)
            rows = pl.ds(pl.multiple_of(i * 256, 256), 256)
            acc[:, at] = dot_nt(d_act[:, 0:2048], w[0, rows, UP:DOWN]) + dot_nt(
                d_act[:, 2048:4096], w[1, rows, UP:DOWN]
            )

        each(4, narrow)
        d_hidden = res[...] + acc[...]
        normed = n1[...]
        d_gains[0:1] = total(d_hidden * normed)
        d_shifts[1:2] = total(d_hidden)
        d_sum = norm_backward(d_hidden * gains[0:1], normed, i1[...])
        d_shifts[0:1] = total(d_sum)
        res[...] = d_sum
        a_low[...] = low(d_sum)
        after("a_low")

        def heads(i):
            at = columns(i * 128, 128)
            half = lax.div(i, 4)
            d_o = low(dot(a_low[...], w[half, :, columns(1536 + lax.rem(i, 4) * 128, 128)]))
            kp, vp, qp = k[:, at], v[:, at], q[:, at]
            parts = []
            for e in (0, 1):
                p_low = probs[2 * i + e]
                p = high(p_low)
                d_p = dot_nt(pick(e, d_o), vp)
                d_s = low(p * (d_p - jnp.sum(p * d_p, -1, keepdims=True)))
                parts.append((dot(d_s, kp) * scale, dot_tn(d_s, qp) * scale, dot_tn(p_low, d_o)))
            d_q, d_k, d_v = (low(jnp.where(first_half, a, b)) for a, b in zip(*parts))
            d_qkv[0, :, at] = d_q
            d_qkv[1, :, at] = d_k
            d_qkv[2, :, at] = d_v
            d_bqv[0:1, at] = total(high(d_q))
            d_bqv[1:2, at] = total(high(d_v))

        each(8, heads)
        after("d_qkv")

        def narrow_in(i):
            at = columns(i * 256, 256)
            rows = pl.ds(pl.multiple_of(i * 256, 256), 256)
            acc[:, at] = sum(
                dot_nt(d_qkv[j, :, 512 * half : 512 * half + 512], w[half, rows, 512 * j : 512 * j + 512])
                for half in (0, 1)
                for j in (0, 1, 2)
            )

        each(4, narrow_in)
        return low(res[...] + acc[...])

    other_half = columns((1 - c) * 2048, 2048)
    other_heads = columns((1 - c) * 512, 512)

    def swap(name, src, dst):
        given[name] = send(src, dst, sibling)

    def have(*names):
        for name in names:
            given[name].wait_recv()

    def block(start, left, right, s_left, s_right):
        whole = low(dot_tn(left, right) + dot_tn(s_left, s_right))
        for chip in range(16):
            for h in (0, 1):
                f, g = (chip // 4, chip % 4) if h == 0 else (chip % 4, chip // 4)
                to, of = h * 512 + f * 128 + g * 32, chip * 64 + h * 32
                w[0, to : to + 32, columns(start, right.shape[1])] = whole[of : of + 32]

    def grads_down():
        have("act", "d_low")

        def one(i):
            at = columns(i * BLOCK, BLOCK)
            block(DOWN + i * BLOCK, d_low[...], act[:, columns(c * 2048 + i * BLOCK, BLOCK)], s_d_low[...], s_act[:, at])

        each(4, one)

    def grads_up():
        have("hid", "d_act")

        def one(i):
            at = columns(i * BLOCK, BLOCK)
            block(UP + i * BLOCK, hid[...], d_act[:, columns(c * 2048 + i * BLOCK, BLOCK)], s_hid[...], s_d_act[:, at])

        each(4, one)

    def spread(row, size, offset):
        lanes = row.shape[1]
        wide = (32, lanes)
        owner = lax.broadcasted_iota(jnp.int32, wide, 0) == lax.div(
            lax.broadcasted_iota(jnp.int32, wide, 1), size
        )
        fold = lax.rem(lax.broadcasted_iota(jnp.int32, (lanes, 128), 0), size) == lax.broadcasted_iota(
            jnp.int32, (lanes, 128), 1
        )
        table = dot(low(jnp.where(owner, row, 0.0)), low(jnp.where(fold, 1.0, 0.0)))
        back = (128, 1024)
        lane = lax.broadcasted_iota(jnp.int32, back, 1)
        source = lax.broadcasted_iota(jnp.int32, back, 0)
        span = min(size, 32)
        place_in = lax.rem(lane, 32)
        if size == 16:
            open_ = (place_in == source + offset) & (source < span)
        else:
            open_ = (place_in + offset == source) & (source < size)
        rows = dot(low(table), low(jnp.where(open_, 1.0, 0.0)))
        mine = lax.broadcasted_iota(jnp.int32, (32, 1024), 0) == lax.div(
            lax.broadcasted_iota(jnp.int32, (32, 1024), 1), 32
        )
        return total(jnp.where(mine, rows, 0.0))

    def small_rows(half, dst):
        heads_at, units_at = columns(half * 512, 512), columns(half * 2048, 2048)
        dst[...] = jnp.zeros_like(dst)
        dst[0:2] = d_gains[...]
        dst[2:6] = d_shifts[...]
        dst[6:7] = spread(d_bqv[0:1, heads_at], 16, 0) + spread(d_bqv[1:2, heads_at], 16, 16)
        dst[7:8] = spread(d_bff[:, units_at], 64, 0)
        dst[8:9] = spread(d_bff[:, units_at], 64, 32)

    def grads_rest():
        have("o", "a_low", "x", "d_qkv", "small")
        block(1536, a_low[...], o[:, columns(c * 512, 512)], s_a_low[...], s_o[...])
        for j in (0, 1, 2):
            block(j * 512, x_in[...], d_qkv[j, :, columns(c * 512, 512)], s_x[...], s_d_qkv[j])
        summed = small[0] + s_small[...]
        column = low(jnp.concatenate([summed, jnp.zeros((112, 1024), jnp.float32)], axis=0).T)
        for chip in range(16):
            for h in (0, 1):
                f, g = (chip // 4, chip % 4) if h == 0 else (chip % 4, chip // 4)
                to, of = h * 512 + f * 128 + g * 32, chip * 64 + h * 32
                w[0, to : to + 32, EXTRA:UP] = column[of : of + 32]

    sent = {}

    def side(h, phase):
        return x if (h == 0) == (phase == 1) else y

    def rows_at(h, step):
        return pl.ds(pl.multiple_of(h * 512 + lax.rem(side(h, 1) + step, 4) * 128, 128), 128)

    def line_at(h, step):
        start = h * 512 + side(h, 1) * 128 + lax.rem(side(h, 2) + step, 4) * 32
        return pl.ds(pl.multiple_of(start, 32), 32)

    def parts(n):
        start, size, half = PASSES[n]
        return pl.ds(start, size), pl.ds(start, half), pl.ds(start + half, size - half)

    def add(dst, *others):
        def one(i):
            at = pl.ds(pl.multiple_of(i * 16, 16), 16)
            dst[at] = low(sum((high(o[at]) for o in others), high(dst[at])))

        each(dst.shape[0] // 16, one)

    def far(n):
        whole, part_a, part_b = parts(n)
        for h in (0, 1):
            rows = rows_at(h, 2)
            sent[n, h, "far"] = (
                send(w.at[0, rows, part_a], passing.at[h, :, part_a], beside(h, 1, 1, x, y, c)),
                send(w.at[0, rows, part_b], passing.at[h, :, part_b], beside(h, 1, 3, x, y, c)),
            )

    def near(n):
        whole, part_a, part_b = parts(n)
        for h in (0, 1):
            up, down = sent[n, h, "far"]
            up.wait_recv()
            add(w.at[0, rows_at(h, 1), part_a], passing.at[h, :, part_a])
            one = send(w.at[0, rows_at(h, 1), whole], near_p.at[h, :, whole], beside(h, 1, 1, x, y, c))
            down.wait_recv()
            add(w.at[0, rows_at(h, 3), part_b], passing.at[h, :, part_b])
            two = send(w.at[0, rows_at(h, 3), whole], near_m.at[h, :, whole], beside(h, 1, 3, x, y, c))
            sent[n, h, "near"] = (one, two)

    def q_far(n):
        whole, part_a, part_b = parts(n)
        for h in (0, 1):
            for copy in sent[n, h, "near"]:
                copy.wait_recv()
            add(w.at[0, rows_at(h, 0), whole], near_p.at[h, :, whole], near_m.at[h, :, whole])
            rows = line_at(h, 2)
            sent[n, h, "q_far"] = (
                send(w.at[0, rows, part_a], q_passing.at[h, :, part_a], beside(h, 2, 1, x, y, c)),
                send(w.at[0, rows, part_b], q_passing.at[h, :, part_b], beside(h, 2, 3, x, y, c)),
            )

    def q_near(n):
        whole, part_a, part_b = parts(n)
        for h in (0, 1):
            up, down = sent[n, h, "q_far"]
            up.wait_recv()
            add(w.at[0, line_at(h, 1), part_a], q_passing.at[h, :, part_a])
            one = send(w.at[0, line_at(h, 1), whole], q_p.at[h, :, whole], beside(h, 2, 1, x, y, c))
            down.wait_recv()
            add(w.at[0, line_at(h, 3), part_b], q_passing.at[h, :, part_b])
            two = send(w.at[0, line_at(h, 3), whole], q_m.at[h, :, whole], beside(h, 2, 3, x, y, c))
            sent[n, h, "q_near"] = (one, two)

    crossing, handing = {}, {}
    owner, sender = c == t, c != t

    def remote(i, src, dst, where):
        return pltpu.make_async_remote_copy(
            src_ref=src,
            dst_ref=dst,
            send_sem=send_sems.at[N_EACH + i],
            recv_sem=recv_sems.at[N_EACH + i],
            device_id=where,
            device_id_type=MESH,
        )

    def cross(n):
        whole, _, _ = parts(n)
        for h in (0, 1):
            for copy in sent[n, h, "q_near"]:
                copy.wait_recv()
            add(w.at[0, line_at(h, 0), whole], q_p.at[h, :, whole], q_m.at[h, :, whole])
            crossing[n, h] = remote(
                2 * n + h, w.at[0, line_at(h, 0), whole], mate.at[h, :, whole], {"tensor": 1 - t}
            )

            @pl.when(sender)
            def _():
                crossing[n, h].start()

    def hand(n):
        whole, _, _ = parts(n)
        handing[n] = remote(6 + n, to_mate.at[:, whole], out.at[:, whole], sibling)

        @pl.when(owner)
        def _():
            for h in (0, 1):
                crossing[n, h].wait_recv()
                value = high(w[0, line_at(h, 0), whole]) + high(mate[h, :, whole])

                @pl.when(c == h)
                def _():
                    out[:, whole] = value

                @pl.when(c != h)
                def _():
                    to_mate[:, whole] = value

            handing[n].start()

    def exchange(n):
        copy = send(kept.at[n], relay.at[n], {"section": 1 - s})
        copy.wait_recv()
        return relay[n]

    def last_stage(stage):
        if stage == "d_low":
            swap("d_low", d_low, s_d_low)
        if stage == "d_act":
            swap("d_act", d_act.at[:, other_half], s_d_act)
            grads_down()
            far(0)
        if stage == "a_low":
            swap("a_low", a_low, s_a_low)
            grads_up()
            far(1)
            near(0)
        if stage == "d_qkv":
            swap("d_qkv", d_qkv.at[:, :, other_heads], s_d_qkv)
            small_rows(1 - c, small.at[1])
            swap("small", small.at[1], s_small)
            near(1)

    def first_stage(stage):
        if stage == "qkv":
            second_on(1, 0)
            second_send(2, 0)
            first_on(2, 1)
        if stage == "heads":
            second_on(1, 1)
            second_send(2, 1)
        if stage == "hid":
            second_end(1, 0)
            second_end(1, 1)
            second_on(2, 0)
            complete(1)
        if stage == "act":
            second_on(2, 1)
            second_end(2, 0)
            second_end(2, 1)
            complete(2)

    z_sends = []
    for n, (start, size, _) in enumerate(GATHERS):
        part = own.at[:, :, pl.ds(start, size)]
        z_sends.append(share(part, part, {"tensor": 1 - t}))
        first_send(n, 0)
    first_on(0, 0)
    z_sends[0].wait_recv()
    first_send(0, 1)
    second_send(0, 0)
    first_on(0, 1)
    first_on(1, 0)
    second_send(0, 1)
    z_sends[1].wait_recv()
    first_send(1, 1)
    second_on(0, 0)
    second_send(1, 0)
    first_on(1, 1)
    second_on(0, 1)
    z_sends[2].wait_recv()
    first_on(2, 0)
    first_send(2, 1)
    second_send(1, 1)
    second_end(0, 0)
    second_end(0, 1)
    complete(0)
    take_parameters()
    own_load.wait()
    kept[0] = forward(x_own, first_stage)
    share.finish()
    x_in[...] = jnp.where(s == 0, x_own[...], exchange(0))
    swap("x", x_in, s_x)
    result = forward(x_in)
    swap("hid", hid, s_hid)
    swap("act", act.at[:, other_half], s_act)
    swap("o", o.at[:, other_heads], s_o)
    kept[2] = result
    kept[1] = backward(high(x_own[...]))
    grad_out = jnp.where(s == 1, x_own[...], exchange(1))
    d_x = backward(high(grad_out), last_stage)
    kept[2] = jnp.where(s == 0, d_x, kept[2])
    across = send(kept.at[2], ends_out.at[t], {"tensor": 1 - t})
    here = pltpu.make_async_copy(kept.at[2], ends_out.at[t], io_sems.at[1])
    here.start()
    small_rows(c, small.at[0])
    grads_rest()
    far(2)
    q_far(0)
    near(2)
    q_far(1)
    q_near(0)
    q_near(1)
    cross(0)
    q_far(2)
    cross(1)
    hand(0)
    q_near(2)
    hand(1)
    cross(2)
    hand(2)
    for n in (0, 1, 2):

        @pl.when(sender)
        def _():
            handing[n].wait_recv()
            for h in (0, 1):
                crossing[n, h].wait_send()

        @pl.when(owner)
        def _():
            handing[n].wait_send()

    here.wait()
    across.wait_recv()
    send.finish()


def run_layers(lengths, ends, *shards):
    vmem = pltpu.VMEM
    bf, f32 = jnp.bfloat16, jnp.float32
    hbm = pl.BlockSpec(memory_space=pl.ANY)
    near = pl.BlockSpec(memory_space=vmem)
    sem = pltpu.SemaphoreType.DMA
    shape = jax.ShapeDtypeStruct
    return pl.pallas_call(
        layers_kernel,
        out_shape=(
            shape((2, ROWS, 1024), bf),
            shape((32, COLS), f32),
        ),
        in_specs=[pl.BlockSpec(memory_space=pltpu.SMEM), hbm, near, near, near, near, near],
        out_specs=(hbm, near),
        scratch_shapes=[
            vmem((2, 1024), f32),
            vmem((4, 1024), f32),
            vmem((2, 1024), f32),
            vmem((1, 4096), f32),
            vmem((2, 1024), f32),
            vmem((4, 1024), f32),
            vmem((2, 1024), f32),
            vmem((1, 4096), f32),
            vmem((2, 4, 4, 2, 2, 16, COLS), bf),
            vmem((ROWS, 1024), bf),
            vmem((ROWS, 1024), bf),
            vmem((2, ROWS, 1024), bf),
            vmem((ROWS, 1024), bf),
            vmem((ROWS, 1024), bf),
            vmem((ROWS, 1024), bf),
            vmem((ROWS, 1024), bf),
            vmem((16, ROWS, ROWS), bf),
            vmem((ROWS, 1024), f32),
            vmem((ROWS, 1024), f32),
            vmem((ROWS, 1), f32),
            vmem((ROWS, 1), f32),
            vmem((ROWS, 1024), f32),
            vmem((ROWS, 1024), bf),
            vmem((ROWS, 4096), bf),
            vmem((ROWS, 4096), bf),
            vmem((ROWS, 4096), bf),
            vmem((3, ROWS, 1024), bf),
            vmem((ROWS, 1024), f32),
            vmem((ROWS, 1024), bf),
            vmem((ROWS, 1024), bf),
            vmem((3, ROWS, 1024), bf),
            vmem((2, 16, 1024), f32),
            vmem((ROWS, 1024), bf),
            vmem((ROWS, 1024), bf),
            vmem((ROWS, 1024), bf),
            vmem((ROWS, 1024), bf),
            vmem((ROWS, 2048), bf),
            vmem((ROWS, 2048), bf),
            vmem((ROWS, 512), bf),
            vmem((3, ROWS, 512), bf),
            vmem((16, 1024), f32),
            vmem((2, 128, COLS), bf),
            vmem((2, 128, COLS), bf),
            vmem((2, 128, COLS), bf),
            vmem((2, 32, COLS), bf),
            vmem((2, 32, COLS), bf),
            vmem((2, 32, COLS), bf),
            vmem((2, 32, COLS), bf),
            vmem((32, COLS), f32),
            sem((2,)),
            sem((N_EACH + 9,)),
            sem((N_EACH + 9,)),
            sem((N_GATHER,)),
            sem((N_GATHER,)),
        ],
        compiler_params=pltpu.CompilerParams(
            collective_id=0, has_side_effects=True, vmem_limit_bytes=62 * 2**20
        ),
        name="run_layers",
    )(lengths, ends, *shards)


def pack_shard(w_qkv, w_out, w_up, w_down, gains, shifts, b_qv, b_ff):
    small = jnp.concatenate([gains[0], shifts[0], b_qv.reshape(1, 32), b_ff.reshape(2, 32)], axis=0)
    return (
        w_qkv[0].reshape(32, 1536),
        w_out[0].T,
        w_up[0],
        w_down[0].T,
        jnp.pad(small.astype(jnp.float32), ((0, 119), (0, 96))),
    )


def unpack_shard(got):
    extra = got[:, EXTRA:UP]
    return (
        got[:, :1536].reshape(1, 32, 3, 512),
        got[:, 1536:2048].T[None],
        got[:, UP:DOWN][None],
        got[:, DOWN:].T[None],
        extra[:, 0:2].T[None],
        extra[:, 2:6].T[None],
        extra[:, 6].reshape(1, 2, 1, 16),
        extra[:, 7:9].T.reshape(1, 1, 64),
    )


def body(ends, lengths, w_qkv, w_out, w_up, w_down, gains, shifts, b_qv, b_ff):
    shards = pack_shard(w_qkv, w_out, w_up, w_down, gains, shifts, b_qv, b_ff)
    ends_out, got = run_layers(lengths, ends.reshape(2, ROWS, 1024), *shards)
    return (ends_out.reshape(1, 2, 1, ROWS, 1024),) + unpack_shard(got)


def solution(mesh):
    in_specs = (
        P("section", None, "dp", None, None),
        P(None, "dp"),
        P("section", "dp", None, "tensor"),
        P("section", "tensor", "dp"),
        P("section", "dp", "tensor"),
        P("section", "tensor", "dp"),
        P("section", None, "dp"),
        P("section", None, "dp"),
        P("section", None, "tensor", "dp"),
        P("section", "tensor", "dp"),
    )
    out_specs = (
        P("section", None, "dp", None, None),
        P("section", "dp", None, "tensor"),
        P("section", "tensor", "dp"),
        P("section", "dp", "tensor"),
        P("section", "tensor", "dp"),
        P("section", None, "dp"),
        P("section", None, "dp"),
        P("section", None, "tensor", "dp"),
        P("section", "tensor", "dp"),
    )
    return jax.shard_map(body, mesh=mesh, in_specs=in_specs, out_specs=out_specs, check_vma=False)
```

```python
import jax
import jax.numpy as jnp
from jax import lax
from jax.experimental import pallas as pl
from jax.experimental.pallas import tpu as pltpu
from jax.sharding import PartitionSpec as P

HD = 64
epsilon = 1e-05

COLS = 6272
ROWS = 192
BLOCK = 512
EXTRA, UP, DOWN = 2048, 2176, 4224
GATHERS = ((0, 2176, 1152), (UP, 2048, 1024), (DOWN, 2048, 1024))
PASSES = (
    (DOWN, 1024, 512),
    (DOWN + 1024, 1024, 512),
    (UP, 1024, 512),
    (UP + 1024, 1024, 512),
    (0, 1536, 768),
    (1536, 640, 384),
)


OFFSETS = (0, 3, 1, 2)
MESH = pl.DeviceIdType.MESH


def place():
    d = lax.axis_index("dp")
    return lax.div(d, 8), lax.rem(lax.div(d, 2), 4), lax.rem(d, 2), lax.axis_index("tensor")


def dp_at(x, y, c):
    return (x * 4 + y) * 2 + c


def beside(h, phase, step, x, y, c):
    if (h == 0) == (phase == 1):
        return {"dp": dp_at(lax.rem(x + step, 4), y, c)}
    return {"dp": dp_at(x, lax.rem(y + step, 4), c)}


def meet(x, y, c, t):
    barrier = pltpu.get_barrier_semaphore()
    partners = [
        {"dp": dp_at(lax.rem(x + 1, 4), y, c)},
        {"dp": dp_at(lax.rem(x + 3, 4), y, c)},
        {"dp": dp_at(x, lax.rem(y + 1, 4), c)},
        {"dp": dp_at(x, lax.rem(y + 3, 4), c)},
        {"dp": dp_at(x, y, 1 - c)},
        {"tensor": 1 - t},
        {"section": 1 - lax.axis_index("section")},
    ]
    for partner in partners:
        pl.semaphore_signal(barrier, inc=1, device_id=partner, device_id_type=MESH)
    pl.semaphore_wait(barrier, len(partners))


class Sender:
    def __init__(self, send_sems, recv_sems):
        self.send_sems, self.recv_sems, self.copies = send_sems, recv_sems, []

    def __call__(self, src, dst, where):
        i = len(self.copies)
        copy = pltpu.make_async_remote_copy(
            src_ref=src,
            dst_ref=dst,
            send_sem=self.send_sems.at[i],
            recv_sem=self.recv_sems.at[i],
            device_id=where,
            device_id_type=MESH,
        )
        copy.start()
        self.copies.append(copy)
        return copy

    def finish(self):
        for copy in self.copies:
            copy.wait_send()


N_EACH = 108
N_GATHER = 147


def dot(a, b):
    return lax.dot_general(a, b, (((1,), (0,)), ((), ())), preferred_element_type=jnp.float32)


def dot_nt(a, b):
    return lax.dot_general(a, b, (((1,), (1,)), ((), ())), preferred_element_type=jnp.float32)


def dot_tn(a, b):
    return lax.dot_general(a, b, (((0,), (0,)), ((), ())), preferred_element_type=jnp.float32)


def low(v):
    return v.astype(jnp.bfloat16)


def high(v):
    return v.astype(jnp.float32)


def columns(start, size):
    return pl.ds(pl.multiple_of(start, 128), size)


def each(count, work):
    lax.fori_loop(0, count, lambda i, z: (work(i), z)[1], 0)


def total(v):
    return jnp.sum(v, axis=0, keepdims=True)


def normalize(values):
    centred = values - jnp.mean(values, -1, keepdims=True)
    inverse_std = lax.rsqrt(jnp.mean(centred * centred, -1, keepdims=True) + epsilon)
    return centred * inverse_std, inverse_std


def norm_backward(grad_norm, normed, inverse_std):
    return inverse_std * (
        grad_norm
        - jnp.mean(grad_norm, -1, keepdims=True)
        - normed * jnp.mean(grad_norm * normed, -1, keepdims=True)
    )


def layers_kernel(
    lengths, ends, shard,
    ends_out, out,
    gains, shifts, b_qv, b_ff,
    d_gains, d_shifts, d_bqv, d_bff,
    blocks, x_own, x_in, relay, q, k, v, o, probs, n1, n2, i1, i2, res, hid, act, slope, d_act, d_qkv,
    acc, d_low, a_low, kept, small,
    s_x, s_hid, s_d_low, s_a_low, s_act, s_d_act, s_o, s_d_qkv, s_small,
    passing, near_p, near_m, q_passing, q_p, q_m, mate, to_mate,
    io_sems, send_sems, recv_sems, gather_send_sems, gather_recv_sems,
):
    x, y, c, t = place()
    s = lax.axis_index("section")
    w = blocks.reshape(2, 1024, COLS)
    own_load = pltpu.make_async_copy(ends.at[t], x_own, io_sems.at[0])
    own_load.start()
    own = blocks.at[t, x, y, c]
    shard_load = pltpu.make_async_copy(shard, own, io_sems.at[1])
    shard_load.start()
    meet(x, y, c, t)
    send = Sender(send_sems, recv_sems)
    share = Sender(gather_send_sems, gather_recv_sems)
    sibling = {"dp": dp_at(x, y, 1 - c)}
    given, shared, to_sibling = {}, {}, {0: [], 1: [], 2: []}

    def half_block(n, kk, h, step):
        start, size, _ = GATHERS[n]
        tt = t if kk == 0 else 1 - t
        xx, yy = (lax.rem(x + step, 4), y) if h == 0 else (x, lax.rem(y + step, 4))
        return blocks.at[tt, xx, yy, c, h, :, pl.ds(start, size)]

    def lane_of(n, kk, h, step):
        start, size, _ = GATHERS[n]
        tt = t if kk == 0 else 1 - t
        if h == 0:
            return blocks.at[tt, :, lax.rem(y + step, 4), c, 0, :, pl.ds(start, size)]
        return blocks.at[tt, lax.rem(x + step, 4), :, c, 1, :, pl.ds(start, size)]

    def part_of(n, ref, first):
        _, size, half = GATHERS[n]
        part = pl.ds(0, half) if first else pl.ds(half, size - half)
        return ref.at[:, part] if len(ref.shape) == 2 else ref.at[:, :, part]

    def first_send(n, kk):
        for h in (0, 1):
            src = half_block(n, kk, h, 0)
            shared[n, kk, h, 1] = [share(src, src, beside(h, 1, step, x, y, c)) for step in (1, 3)]

    def pass_on(n, kk, h, phase, find):
        onward = []
        for copy, step in zip(shared[n, kk, h, phase], (1, 3)):
            copy.wait_recv()
            here = find(n, kk, h, 4 - step)
            part = part_of(n, here, step == 1)
            onward.append(share(part, part, beside(h, phase, step, x, y, c)))
            if phase == 2:
                to_sibling[n].append(share(here, here, sibling))
        shared[n, kk, h, phase] = onward

    def first_on(n, kk):
        for h in (0, 1):
            pass_on(n, kk, h, 1, half_block)

    def second_send(n, kk):
        for h in (0, 1):
            for copy in shared[n, kk, h, 1]:
                copy.wait_recv()
            src = lane_of(n, kk, h, 0)
            shared[n, kk, h, 2] = [share(src, src, beside(h, 2, step, x, y, c)) for step in (1, 3)]
            to_sibling[n].append(share(src, src, sibling))

    def second_on(n, kk):
        for h in (0, 1):
            pass_on(n, kk, h, 2, lane_of)

    def second_end(n, kk):
        for h in (0, 1):
            for copy in shared[n, kk, h, 2]:
                copy.wait_recv()
            here = lane_of(n, kk, h, 2)
            to_sibling[n].append(share(here, here, sibling))

    def complete(n):
        for copy in to_sibling[n]:
            copy.wait_recv()

    def collect(half, rows):
        wide = (32, 1024)
        owner_of = lax.broadcasted_iota(jnp.int32, wide, 0) == lax.div(
            lax.broadcasted_iota(jnp.int32, wide, 1), 32
        )
        fold = lax.rem(lax.broadcasted_iota(jnp.int32, (1024, 128), 0), 32) == lax.broadcasted_iota(
            jnp.int32, (1024, 128), 1
        )
        fold = low(jnp.where(fold, 1.0, 0.0))
        tables = [low(dot(low(jnp.where(owner_of, row, 0.0)), fold)) for row in rows]

        def open_up(size, *terms):
            lanes = size * 32
            lane = lax.broadcasted_iota(jnp.int32, (128, lanes), 1)
            source = lax.broadcasted_iota(jnp.int32, (128, lanes), 0)
            found = jnp.zeros((32, lanes), jnp.float32)
            for table, offset in terms:
                pick_at = (lax.rem(lane, size) + offset == source) & (source < 32)
                found = found + dot(table, low(jnp.where(pick_at, 1.0, 0.0)))
            mine = lax.broadcasted_iota(jnp.int32, (32, lanes), 0) == lax.div(
                lax.broadcasted_iota(jnp.int32, (32, lanes), 1), size
            )
            return total(jnp.where(mine, found, 0.0))

        at = pl.ds(half * 512, 512)
        b_qv[0:1, at] = open_up(16, (tables[0], 0))
        b_qv[1:2, at] = open_up(16, (tables[0], 16))
        b_ff[:, pl.ds(half * 2048, 2048)] = open_up(64, (tables[1], 0), (tables[2], -32))

    def take_parameters():
        for half in (0, 1):
            rows = high(w[half, :, EXTRA:UP]).T
            if half == 0:
                gains[...] = rows[0:2]
                shifts[...] = rows[2:6]
            collect(half, (rows[6:7], rows[7:8], rows[8:9]))

    length = lengths[t, 0]
    first_half = lax.broadcasted_iota(jnp.int32, (ROWS, 128), 1) < HD
    valid = lax.broadcasted_iota(jnp.int32, (ROWS, ROWS), 0) < length
    scale = HD**-0.5

    def pick(e, value):
        return jnp.where(first_half == (e == 0), value, jnp.zeros_like(value))

    def forward(x, after=lambda stage: None):

        def project(i):
            half, j = lax.div(i, 3), lax.rem(i, 3)
            p = dot(x[...], w[half, :, columns(j * BLOCK, BLOCK)])
            at = columns(half * BLOCK, BLOCK)

            @pl.when(j == 0)
            def _():
                q[:, at] = low(p + b_qv[0:1, at])

            @pl.when(j == 1)
            def _():
                k[:, at] = low(p)

            @pl.when(j == 2)
            def _():
                v[:, at] = low(p + b_qv[1:2, at])

        each(6, project)
        after("qkv")

        def heads(i):
            at = columns(i * 128, 128)
            kp, vp, qp = k[:, at], v[:, at], q[:, at] * scale
            vt, outs = vp.T, []
            for e in (0, 1):
                scores = jnp.where(valid, dot_nt(kp, pick(e, qp)), -1e9)
                powers = jnp.exp(scores - jnp.max(scores, 0, keepdims=True))
                p = low(powers * (1.0 / total(powers)))
                probs[2 * i + e] = p
                outs.append(dot(vt[64 * e : 64 * e + 64], p))
            o[:, at] = low(jnp.concatenate(outs)).T

        each(4, lambda i: (heads(2 * i), heads(2 * i + 1)))
        after("heads")
        attended = dot_nt(o[:, 0:512], w[0, :, 1536:2048]) + dot_nt(o[:, 512:1024], w[1, :, 1536:2048])
        normed, inverse = normalize(high(x[...]) + attended + shifts[0:1])
        n1[...], i1[...] = normed, inverse
        hidden = normed * gains[0:1] + shifts[1:2]
        res[...] = hidden
        hid[...] = low(hidden)
        after("hid")

        def widen(i):
            half, j = lax.div(i, 4), lax.rem(i, 4)
            at = columns(i * BLOCK, BLOCK)
            u = dot(hid[...], w[half, :, columns(UP + j * BLOCK, BLOCK)]) + b_ff[:, at]
            phi = 0.5 + 0.5 * lax.erf(u * 0.7071067811865476)
            act[:, at] = low(u * phi)
            slope[:, at] = low(phi + u * (jnp.exp(u * u * -0.5) * 0.3989422804014327))

        each(8, widen)
        after("act")

        def narrow(i):
            at = columns(i * 256, 256)
            rows = pl.ds(pl.multiple_of(i * 256, 256), 256)
            acc[:, at] = dot_nt(act[:, 0:2048], w[0, rows, DOWN:COLS]) + dot_nt(
                act[:, 2048:4096], w[1, rows, DOWN:COLS]
            )

        each(4, narrow)
        normed, inverse = normalize(res[...] + acc[...] + shifts[2:3])
        n2[...], i2[...] = normed, inverse
        return low(normed * gains[1:2] + shifts[3:4])

    def backward(grad_out, after=lambda stage: None):
        normed = n2[...]
        d_gains[1:2] = total(grad_out * normed)
        d_shifts[3:4] = total(grad_out)
        d_sum = norm_backward(grad_out * gains[1:2], normed, i2[...])
        d_shifts[2:3] = total(d_sum)
        res[...] = d_sum
        d_low[...] = low(d_sum)
        after("d_low")

        def widen(i):
            half, j = lax.div(i, 4), lax.rem(i, 4)
            at = columns(i * BLOCK, BLOCK)
            d = low(dot(d_low[...], w[half, :, columns(DOWN + j * BLOCK, BLOCK)]) * high(slope[:, at]))
            d_act[:, at] = d
            d_bff[:, at] = total(high(d))

        each(8, widen)
        after("d_act")

        def narrow(i):
            at = columns(i * 256, 256)
            rows = pl.ds(pl.multiple_of(i * 256, 256), 256)
            acc[:, at] = dot_nt(d_act[:, 0:2048], w[0, rows, UP:DOWN]) + dot_nt(
                d_act[:, 2048:4096], w[1, rows, UP:DOWN]
            )

        each(4, narrow)
        d_hidden = res[...] + acc[...]
        normed = n1[...]
        d_gains[0:1] = total(d_hidden * normed)
        d_shifts[1:2] = total(d_hidden)
        d_sum = norm_backward(d_hidden * gains[0:1], normed, i1[...])
        d_shifts[0:1] = total(d_sum)
        res[...] = d_sum
        a_low[...] = low(d_sum)
        after("a_low")
        for half in (0, 1):
            d_qkv[2, :, half * 512 : half * 512 + 512] = low(dot(a_low[...], w[half, :, 1536:EXTRA]))

        def heads(i):
            at = columns(i * 128, 128)
            kp, vp, qp, d_o = k[:, at], v[:, at], q[:, at], d_qkv[2, :, at]
            kt, parts = kp.T, []
            for e in (0, 1):
                p_low = probs[2 * i + e]
                p = high(p_low)
                product = p * dot_nt(vp, pick(e, d_o))
                d_s = low(product - p * total(product))
                parts.append(
                    (dot(kt[64 * e : 64 * e + 64], d_s) * scale, dot(d_s, qp) * scale, dot(p_low, d_o))
                )
            d_q = low(jnp.concatenate([parts[0][0], parts[1][0]])).T
            d_k, d_v = (low(jnp.where(first_half, a, b)) for a, b in zip(parts[0][1:], parts[1][1:]))
            d_qkv[0, :, at] = d_q
            d_qkv[1, :, at] = d_k
            d_qkv[2, :, at] = d_v
            d_bqv[0:1, at] = total(high(d_q))
            d_bqv[1:2, at] = total(high(d_v))

        each(4, lambda i: (heads(2 * i), heads(2 * i + 1)))
        after("d_qkv")

        def narrow_in(i):
            at = columns(i * 256, 256)
            rows = pl.ds(pl.multiple_of(i * 256, 256), 256)
            acc[:, at] = sum(
                dot_nt(d_qkv[j, :, 512 * half : 512 * half + 512], w[half, rows, 512 * j : 512 * j + 512])
                for half in (0, 1)
                for j in (0, 1, 2)
            )

        each(4, narrow_in)
        return low(res[...] + acc[...])

    other_half = columns((1 - c) * 2048, 2048)
    other_heads = columns((1 - c) * 512, 512)

    def swap(name, src, dst):
        given[name] = send(src, dst, sibling)

    def have(*names):
        for name in names:
            given[name].wait_recv()

    def block(start, left, right, s_left, s_right):
        whole = low(dot_tn(jnp.concatenate([left, s_left]), jnp.concatenate([right, s_right])))
        for chip in range(16):
            for h in (0, 1):
                f, g = (chip // 4, chip % 4) if h == 0 else (chip % 4, chip // 4)
                to, of = h * 512 + f * 128 + g * 32, chip * 64 + h * 32
                w[0, to : to + 32, columns(start, right.shape[1])] = whole[of : of + 32]

    def grads_down(first):
        def one(i):
            i = i + first
            at = columns(i * BLOCK, BLOCK)
            block(DOWN + i * BLOCK, d_low[...], act[:, columns(c * 2048 + i * BLOCK, BLOCK)], s_d_low[...], s_act[:, at])

        each(2, one)

    def grads_up(first):
        def one(i):
            i = i + first
            at = columns(i * BLOCK, BLOCK)
            block(UP + i * BLOCK, hid[...], d_act[:, columns(c * 2048 + i * BLOCK, BLOCK)], s_hid[...], s_d_act[:, at])

        each(2, one)

    def spread(row, size, offset):
        lanes = row.shape[1]
        wide = (32, lanes)
        owner = lax.broadcasted_iota(jnp.int32, wide, 0) == lax.div(
            lax.broadcasted_iota(jnp.int32, wide, 1), size
        )
        fold = lax.rem(lax.broadcasted_iota(jnp.int32, (lanes, 128), 0), size) == lax.broadcasted_iota(
            jnp.int32, (lanes, 128), 1
        )
        table = dot(low(jnp.where(owner, row, 0.0)), low(jnp.where(fold, 1.0, 0.0)))
        back = (128, 1024)
        lane = lax.broadcasted_iota(jnp.int32, back, 1)
        source = lax.broadcasted_iota(jnp.int32, back, 0)
        span = min(size, 32)
        place_in = lax.rem(lane, 32)
        if size == 16:
            open_ = (place_in == source + offset) & (source < span)
        else:
            open_ = (place_in + offset == source) & (source < size)
        rows = dot(low(table), low(jnp.where(open_, 1.0, 0.0)))
        mine = lax.broadcasted_iota(jnp.int32, (32, 1024), 0) == lax.div(
            lax.broadcasted_iota(jnp.int32, (32, 1024), 1), 32
        )
        return total(jnp.where(mine, rows, 0.0))

    def small_rows(half, dst):
        heads_at, units_at = columns(half * 512, 512), columns(half * 2048, 2048)
        dst[...] = jnp.zeros_like(dst)
        dst[0:2] = d_gains[...]
        dst[2:6] = d_shifts[...]
        dst[6:7] = spread(d_bqv[0:1, heads_at], 16, 0) + spread(d_bqv[1:2, heads_at], 16, 16)
        dst[7:8] = spread(d_bff[:, units_at], 64, 0)
        dst[8:9] = spread(d_bff[:, units_at], 64, 32)

    def grads_qkv():
        for j in (0, 1, 2):
            block(j * 512, x_in[...], d_qkv[j, :, columns(c * 512, 512)], s_x[...], s_d_qkv[j])

    def grads_rest():
        block(1536, a_low[...], o[:, columns(c * 512, 512)], s_a_low[...], s_o[...])
        summed = small[0] + s_small[...]
        column = low(jnp.concatenate([summed, jnp.zeros((112, 1024), jnp.float32)], axis=0).T)
        for chip in range(16):
            for h in (0, 1):
                f, g = (chip // 4, chip % 4) if h == 0 else (chip % 4, chip // 4)
                to, of = h * 512 + f * 128 + g * 32, chip * 64 + h * 32
                w[0, to : to + 32, EXTRA:UP] = column[of : of + 32]

    sent = {}

    def side(h, phase):
        return x if (h == 0) == (phase == 1) else y

    def rows_at(h, step):
        return pl.ds(pl.multiple_of(h * 512 + lax.rem(side(h, 1) + step, 4) * 128, 128), 128)

    def line_at(h, step):
        start = h * 512 + side(h, 1) * 128 + lax.rem(side(h, 2) + step, 4) * 32
        return pl.ds(pl.multiple_of(start, 32), 32)

    def parts(n):
        start, size, half = PASSES[n]
        return pl.ds(start, size), pl.ds(start, half), pl.ds(start + half, size - half)

    def add(dst, *others):
        def one(i):
            at = pl.ds(pl.multiple_of(i * 16, 16), 16)
            dst[at] = low(sum((high(o[at]) for o in others), high(dst[at])))

        each(dst.shape[0] // 16, one)

    def far(n):
        whole, part_a, part_b = parts(n)
        for h in (0, 1):
            rows = rows_at(h, 2)
            sent[n, h, "far"] = (
                send(w.at[0, rows, part_a], passing.at[h, :, part_a], beside(h, 1, 1, x, y, c)),
                send(w.at[0, rows, part_b], passing.at[h, :, part_b], beside(h, 1, 3, x, y, c)),
            )

    def near(n):
        whole, part_a, part_b = parts(n)
        for h in (0, 1):
            up, down = sent[n, h, "far"]
            up.wait_recv()
            add(w.at[0, rows_at(h, 1), part_a], passing.at[h, :, part_a])
            one = send(w.at[0, rows_at(h, 1), whole], near_p.at[h, :, whole], beside(h, 1, 1, x, y, c))
            down.wait_recv()
            add(w.at[0, rows_at(h, 3), part_b], passing.at[h, :, part_b])
            two = send(w.at[0, rows_at(h, 3), whole], near_m.at[h, :, whole], beside(h, 1, 3, x, y, c))
            sent[n, h, "near"] = (one, two)

    def q_far(n):
        whole, part_a, part_b = parts(n)
        for h in (0, 1):
            for copy in sent[n, h, "near"]:
                copy.wait_recv()
            add(w.at[0, rows_at(h, 0), whole], near_p.at[h, :, whole], near_m.at[h, :, whole])
            rows = line_at(h, 2)
            sent[n, h, "q_far"] = (
                send(w.at[0, rows, part_a], q_passing.at[h, :, part_a], beside(h, 2, 1, x, y, c)),
                send(w.at[0, rows, part_b], q_passing.at[h, :, part_b], beside(h, 2, 3, x, y, c)),
            )

    def q_near(n):
        whole, part_a, part_b = parts(n)
        for h in (0, 1):
            up, down = sent[n, h, "q_far"]
            up.wait_recv()
            add(w.at[0, line_at(h, 1), part_a], q_passing.at[h, :, part_a])
            one = send(w.at[0, line_at(h, 1), whole], q_p.at[h, :, whole], beside(h, 2, 1, x, y, c))
            down.wait_recv()
            add(w.at[0, line_at(h, 3), part_b], q_passing.at[h, :, part_b])
            two = send(w.at[0, line_at(h, 3), whole], q_m.at[h, :, whole], beside(h, 2, 3, x, y, c))
            sent[n, h, "q_near"] = (one, two)

    crossing, handing = {}, {}
    owner, sender = c == t, c != t

    def remote(i, src, dst, where):
        return pltpu.make_async_remote_copy(
            src_ref=src,
            dst_ref=dst,
            send_sem=send_sems.at[N_EACH + i],
            recv_sem=recv_sems.at[N_EACH + i],
            device_id=where,
            device_id_type=MESH,
        )

    def cross(n):
        whole, _, _ = parts(n)
        for h in (0, 1):
            for copy in sent[n, h, "q_near"]:
                copy.wait_recv()
            add(w.at[0, line_at(h, 0), whole], q_p.at[h, :, whole], q_m.at[h, :, whole])
            crossing[n, h] = remote(
                2 * n + h, w.at[0, line_at(h, 0), whole], mate.at[h, :, whole], {"tensor": 1 - t}
            )

            @pl.when(sender)
            def _():
                crossing[n, h].start()

    def hand(n):
        whole, _, _ = parts(n)
        handing[n] = remote(12 + n, to_mate.at[:, whole], out.at[:, whole], sibling)

        @pl.when(owner)
        def _():
            for h in (0, 1):
                crossing[n, h].wait_recv()
                value = high(w[0, line_at(h, 0), whole]) + high(mate[h, :, whole])

                @pl.when(c == h)
                def _():
                    out[:, whole] = value

                @pl.when(c != h)
                def _():
                    to_mate[:, whole] = value

            handing[n].start()

    def exchange(n):
        copy = send(kept.at[n], relay.at[n], {"section": 1 - s})
        copy.wait_recv()
        return relay[n]

    def last_stage(stage):
        if stage == "d_low":
            swap("d_low", d_low, s_d_low)
        if stage == "d_act":
            swap("d_act", d_act.at[:, other_half], s_d_act)
            have("act", "d_low")
            grads_down(0)
            far(0)
            grads_down(2)
            far(1)
        if stage == "a_low":
            swap("a_low", a_low, s_a_low)
            near(0)
            have("hid", "d_act")
            grads_up(0)
            far(2)
            near(1)
            grads_up(2)
            far(3)
            near(2)
        if stage == "d_qkv":
            swap("d_qkv", d_qkv.at[:, :, other_heads], s_d_qkv)
            small_rows(1 - c, small.at[1])
            swap("small", small.at[1], s_small)
            small_rows(c, small.at[0])
            q_far(0)
            near(3)
            q_far(1)

    def first_stage(stage):
        if stage == "qkv":
            second_on(1, 0)
            second_send(2, 0)
            first_on(2, 1)
        if stage == "heads":
            second_on(1, 1)
            second_send(2, 1)
        if stage == "hid":
            second_end(1, 0)
            second_end(1, 1)
            second_on(2, 0)
            complete(1)
        if stage == "act":
            second_on(2, 1)
            second_end(2, 0)
            second_end(2, 1)
            complete(2)

    shard_load.wait()
    z_sends = []
    for n, (start, size, _) in enumerate(GATHERS):
        part = own.at[:, :, pl.ds(start, size)]
        z_sends.append(share(part, part, {"tensor": 1 - t}))
        first_send(n, 0)
    first_on(0, 0)
    z_sends[0].wait_recv()
    first_send(0, 1)
    second_send(0, 0)
    first_on(0, 1)
    first_on(1, 0)
    second_send(0, 1)
    z_sends[1].wait_recv()
    first_send(1, 1)
    second_on(0, 0)
    second_send(1, 0)
    first_on(1, 1)
    second_on(0, 1)
    z_sends[2].wait_recv()
    first_on(2, 0)
    first_send(2, 1)
    second_send(1, 1)
    second_end(0, 0)
    second_end(0, 1)
    complete(0)
    take_parameters()
    own_load.wait()
    kept[0] = forward(x_own, first_stage)
    share.finish()
    x_in[...] = jnp.where(s == 0, x_own[...], exchange(0))
    swap("x", x_in, s_x)
    result = forward(x_in)
    swap("hid", hid, s_hid)
    swap("act", act.at[:, other_half], s_act)
    swap("o", o.at[:, other_heads], s_o)
    kept[2] = result
    kept[1] = backward(high(x_own[...]))
    grad_out = jnp.where(s == 1, x_own[...], exchange(1))
    d_x = backward(high(grad_out), last_stage)
    kept[2] = jnp.where(s == 0, d_x, kept[2])
    across = send(kept.at[2], ends_out.at[t], {"tensor": 1 - t})
    here = pltpu.make_async_copy(kept.at[2], ends_out.at[t], io_sems.at[1])
    here.start()
    have("o", "a_low", "x", "d_qkv", "small")
    grads_qkv()
    far(4)
    q_far(2)
    q_near(0)
    grads_rest()
    far(5)
    near(4)
    q_near(1)
    q_far(3)
    cross(0)
    q_near(2)
    cross(1)
    near(5)
    q_near(3)
    hand(0)
    cross(2)
    hand(1)
    q_far(4)
    cross(3)
    q_far(5)
    hand(2)
    q_near(4)
    q_near(5)
    hand(3)
    cross(4)
    cross(5)
    hand(4)
    hand(5)
    for n in range(6):

        @pl.when(sender)
        def _():
            handing[n].wait_recv()
            for h in (0, 1):
                crossing[n, h].wait_send()

        @pl.when(owner)
        def _():
            handing[n].wait_send()

    here.wait()
    across.wait_recv()
    send.finish()


def run_layers(lengths, ends, shard):
    vmem = pltpu.VMEM
    bf, f32 = jnp.bfloat16, jnp.float32
    hbm = pl.BlockSpec(memory_space=pl.ANY)
    near = pl.BlockSpec(memory_space=vmem)
    sem = pltpu.SemaphoreType.DMA
    shape = jax.ShapeDtypeStruct
    return pl.pallas_call(
        layers_kernel,
        out_shape=(
            shape((2, ROWS, 1024), bf),
            shape((32, COLS), f32),
        ),
        in_specs=[pl.BlockSpec(memory_space=pltpu.SMEM), hbm, hbm],
        out_specs=(hbm, near),
        scratch_shapes=[
            vmem((2, 1024), f32),
            vmem((4, 1024), f32),
            vmem((2, 1024), f32),
            vmem((1, 4096), f32),
            vmem((2, 1024), f32),
            vmem((4, 1024), f32),
            vmem((2, 1024), f32),
            vmem((1, 4096), f32),
            vmem((2, 4, 4, 2, 2, 16, COLS), bf),
            vmem((ROWS, 1024), bf),
            vmem((ROWS, 1024), bf),
            vmem((2, ROWS, 1024), bf),
            vmem((ROWS, 1024), bf),
            vmem((ROWS, 1024), bf),
            vmem((ROWS, 1024), bf),
            vmem((ROWS, 1024), bf),
            vmem((16, ROWS, ROWS), bf),
            vmem((ROWS, 1024), f32),
            vmem((ROWS, 1024), f32),
            vmem((ROWS, 1), f32),
            vmem((ROWS, 1), f32),
            vmem((ROWS, 1024), f32),
            vmem((ROWS, 1024), bf),
            vmem((ROWS, 4096), bf),
            vmem((ROWS, 4096), bf),
            vmem((ROWS, 4096), bf),
            vmem((3, ROWS, 1024), bf),
            vmem((ROWS, 1024), f32),
            vmem((ROWS, 1024), bf),
            vmem((ROWS, 1024), bf),
            vmem((3, ROWS, 1024), bf),
            vmem((2, 16, 1024), f32),
            vmem((ROWS, 1024), bf),
            vmem((ROWS, 1024), bf),
            vmem((ROWS, 1024), bf),
            vmem((ROWS, 1024), bf),
            vmem((ROWS, 2048), bf),
            vmem((ROWS, 2048), bf),
            vmem((ROWS, 512), bf),
            vmem((3, ROWS, 512), bf),
            vmem((16, 1024), f32),
            vmem((2, 128, COLS), bf),
            vmem((2, 128, COLS), bf),
            vmem((2, 128, COLS), bf),
            vmem((2, 32, COLS), bf),
            vmem((2, 32, COLS), bf),
            vmem((2, 32, COLS), bf),
            vmem((2, 32, COLS), bf),
            vmem((32, COLS), f32),
            sem((2,)),
            sem((N_EACH + 18,)),
            sem((N_EACH + 18,)),
            sem((N_GATHER,)),
            sem((N_GATHER,)),
        ],
        compiler_params=pltpu.CompilerParams(
            collective_id=0, has_side_effects=True, vmem_limit_bytes=62 * 2**20
        ),
        name="run_layers",
    )(lengths, ends, shard)


def pack_kernel(w_qkv, w_out, w_up, w_down, gains, shifts, b_qv, b_ff, shard, small):
    for j in (0, 1, 2):
        shard[:, j * 512 : j * 512 + 512] = w_qkv[0, j]
    shard[:, 1536:EXTRA] = w_out[0]
    shard[:, UP:DOWN] = w_up[0]
    shard[:, DOWN:COLS] = w_down[0]
    small[...] = jnp.zeros_like(small)
    small[0:2, 0:32] = high(gains[0])
    small[2:6, 0:32] = high(shifts[0])
    small[6:7, 0:32] = jnp.concatenate([high(b_qv[0, 0, 0:1]), high(b_qv[0, 0, 1:2])], axis=1)
    small[7:8, 0:32] = high(b_ff[0, :, 0:32])
    small[8:9, 0:32] = high(b_ff[0, :, 32:64])
    shard[:, EXTRA:UP] = low(small[...].T[0:32])


def pack_shard(w_qkv, w_out, w_up, w_down, gains, shifts, b_qv, b_ff):
    return pl.pallas_call(
        pack_kernel,
        out_shape=jax.ShapeDtypeStruct((32, COLS), jnp.bfloat16),
        scratch_shapes=[pltpu.VMEM((128, 128), jnp.float32)],
        name="pack_shard",
    )(
        w_qkv.transpose(0, 2, 1, 3),
        w_out.transpose(0, 2, 1),
        w_up,
        w_down.transpose(0, 2, 1),
        gains,
        shifts,
        b_qv.transpose(0, 2, 1, 3),
        b_ff,
    )


def unpack_kernel(got, w_qkv, w_out, w_up, w_down, gains, shifts, b_qv, b_ff):
    for j in (0, 1, 2):
        w_qkv[0, j] = got[:, j * 512 : j * 512 + 512]
    w_out[0] = got[:, 1536:EXTRA]
    w_up[0] = got[:, UP:DOWN]
    w_down[0] = got[:, DOWN:COLS]
    rows = got[:, EXTRA:UP].T
    gains[0] = rows[0:2]
    shifts[0] = rows[2:6]
    b_qv[0, 0, 0:1] = rows[6:7, 0:16]
    b_qv[0, 0, 1:2] = rows[6:7, 16:32]
    b_ff[0] = jnp.concatenate([rows[7:8], rows[8:9]], axis=1)


def unpack_shard(got):
    shapes = ((1, 3, 32, 512), (1, 32, 512), (1, 32, 2048), (1, 32, 2048), (1, 2, 32), (1, 4, 32))
    shapes = shapes + ((1, 1, 2, 16), (1, 1, 64))
    w_qkv, w_out, w_up, w_down, gains, shifts, b_qv, b_ff = pl.pallas_call(
        unpack_kernel,
        out_shape=tuple(jax.ShapeDtypeStruct(shape, jnp.float32) for shape in shapes),
        name="unpack_shard",
    )(got)
    return (
        w_qkv.transpose(0, 2, 1, 3),
        w_out.transpose(0, 2, 1),
        w_up,
        w_down.transpose(0, 2, 1),
        gains,
        shifts,
        b_qv.transpose(0, 2, 1, 3),
        b_ff,
    )


def body(ends, lengths, *weights):
    shard = pack_shard(*weights)
    ends_out, got = run_layers(lengths, ends.reshape(2, ROWS, 1024), shard.reshape(2, 16, COLS))
    return (ends_out.reshape(1, 2, 1, ROWS, 1024),) + unpack_shard(got)


def solution(mesh):
    in_specs = (
        P("section", None, "dp", None, None),
        P(None, "dp"),
        P("section", "dp", None, "tensor"),
        P("section", "tensor", "dp"),
        P("section", "dp", "tensor"),
        P("section", "tensor", "dp"),
        P("section", None, "dp"),
        P("section", None, "dp"),
        P("section", None, "tensor", "dp"),
        P("section", "tensor", "dp"),
    )
    out_specs = (
        P("section", None, "dp", None, None),
        P("section", "dp", None, "tensor"),
        P("section", "tensor", "dp"),
        P("section", "dp", "tensor"),
        P("section", "tensor", "dp"),
        P("section", None, "dp"),
        P("section", None, "dp"),
        P("section", None, "tensor", "dp"),
        P("section", "tensor", "dp"),
    )
    return jax.shard_map(body, mesh=mesh, in_specs=in_specs, out_specs=out_specs, check_vma=False)
```

```python
import jax
import jax.numpy as jnp
from jax import lax
from jax.experimental import pallas as pl
from jax.experimental.pallas import tpu as pltpu
from jax.sharding import PartitionSpec as P

HD = 64
epsilon = 1e-05

COLS = 6272
ROWS = 192
BLOCK = 512
EXTRA, UP, DOWN = 2048, 2176, 4224
GATHERS = ((0, 2176, 1152), (UP, 2048, 1024), (DOWN, 2048, 1024))
PASSES = (
    (DOWN, 1024, 512),
    (DOWN + 1024, 1024, 512),
    (UP, 1024, 512),
    (UP + 1024, 1024, 512),
    (0, 1536, 768),
    (1536, 640, 384),
)


OFFSETS = (0, 3, 1, 2)
MESH = pl.DeviceIdType.MESH


def place():
    d = lax.axis_index("dp")
    return lax.div(d, 8), lax.rem(lax.div(d, 2), 4), lax.rem(d, 2), lax.axis_index("tensor")


def dp_at(x, y, c):
    return (x * 4 + y) * 2 + c


def beside(h, phase, step, x, y, c):
    if (h == 0) == (phase == 1):
        return {"dp": dp_at(lax.rem(x + step, 4), y, c)}
    return {"dp": dp_at(x, lax.rem(y + step, 4), c)}


def meet(x, y, c, t):
    barrier = pltpu.get_barrier_semaphore()
    partners = [
        {"dp": dp_at(lax.rem(x + 1, 4), y, c)},
        {"dp": dp_at(lax.rem(x + 3, 4), y, c)},
        {"dp": dp_at(x, lax.rem(y + 1, 4), c)},
        {"dp": dp_at(x, lax.rem(y + 3, 4), c)},
        {"dp": dp_at(x, y, 1 - c)},
        {"tensor": 1 - t},
        {"dp": dp_at(x, y, 1 - c), "tensor": 1 - t},
        {"section": 1 - lax.axis_index("section"), "dp": dp_at(x, y, t), "tensor": c},
    ]
    for partner in partners:
        pl.semaphore_signal(barrier, inc=1, device_id=partner, device_id_type=MESH)
    pl.semaphore_wait(barrier, len(partners))


class Sender:
    def __init__(self, send_sems, recv_sems):
        self.send_sems, self.recv_sems, self.copies = send_sems, recv_sems, []

    def __call__(self, src, dst, where):
        i = len(self.copies)
        copy = pltpu.make_async_remote_copy(
            src_ref=src,
            dst_ref=dst,
            send_sem=self.send_sems.at[i],
            recv_sem=self.recv_sems.at[i],
            device_id=where,
            device_id_type=MESH,
        )
        copy.start()
        self.copies.append(copy)
        return copy

    def finish(self):
        for copy in self.copies:
            copy.wait_send()


N_EACH = 107
N_GATHER = 147


def dot(a, b):
    return lax.dot_general(a, b, (((1,), (0,)), ((), ())), preferred_element_type=jnp.float32)


def dot_nt(a, b):
    return lax.dot_general(a, b, (((1,), (1,)), ((), ())), preferred_element_type=jnp.float32)


def dot_tn(a, b):
    return lax.dot_general(a, b, (((0,), (0,)), ((), ())), preferred_element_type=jnp.float32)


def low(v):
    return v.astype(jnp.bfloat16)


def high(v):
    return v.astype(jnp.float32)


def columns(start, size):
    return pl.ds(pl.multiple_of(start, 128), size)


def each(count, work):
    lax.fori_loop(0, count, lambda i, z: (work(i), z)[1], 0)


def total(v):
    return jnp.sum(v, axis=0, keepdims=True)


def normalize(values):
    centred = values - jnp.mean(values, -1, keepdims=True)
    inverse_std = lax.rsqrt(jnp.mean(centred * centred, -1, keepdims=True) + epsilon)
    return centred * inverse_std, inverse_std


def norm_backward(grad_norm, normed, inverse_std):
    return inverse_std * (
        grad_norm
        - jnp.mean(grad_norm, -1, keepdims=True)
        - normed * jnp.mean(grad_norm * normed, -1, keepdims=True)
    )


def layers_kernel(
    spans, ends, shard,
    ends_out, out,
    gains, shifts, b_qv, b_ff,
    d_gains, d_shifts, d_bqv, d_bff,
    blocks, x_own, x_in, relay, q, k, v, o, probs, n1, n2, i1, i2, res, hid, act, slope, d_act, d_qkv,
    acc, d_low, a_low, kept, small,
    s_x, s_hid, s_d_low, s_a_low, s_act, s_d_act, s_o, s_d_qkv, s_small,
    passing, near_p, near_m, q_passing, q_p, q_m, mate, to_mate, span, span_in,
    io_sems, send_sems, recv_sems, gather_send_sems, gather_recv_sems,
):
    x, y, c, t = place()
    s = lax.axis_index("section")
    w = blocks.reshape(2, 1024, COLS)
    own_load = pltpu.make_async_copy(ends.at[t], x_own, io_sems.at[0])
    own_load.start()
    own = blocks.at[t, x, y, c]
    shard_load = pltpu.make_async_copy(shard, own, io_sems.at[1])
    shard_load.start()
    meet(x, y, c, t)
    send = Sender(send_sems, recv_sems)
    share = Sender(gather_send_sems, gather_recv_sems)
    sibling = {"dp": dp_at(x, y, 1 - c)}
    given, shared, to_sibling = {}, {}, {0: [], 1: [], 2: []}

    def half_block(n, kk, h, step):
        start, size, _ = GATHERS[n]
        tt = t if kk == 0 else 1 - t
        xx, yy = (lax.rem(x + step, 4), y) if h == 0 else (x, lax.rem(y + step, 4))
        return blocks.at[tt, xx, yy, c, h, :, pl.ds(start, size)]

    def lane_of(n, kk, h, step):
        start, size, _ = GATHERS[n]
        tt = t if kk == 0 else 1 - t
        if h == 0:
            return blocks.at[tt, :, lax.rem(y + step, 4), c, 0, :, pl.ds(start, size)]
        return blocks.at[tt, lax.rem(x + step, 4), :, c, 1, :, pl.ds(start, size)]

    def part_of(n, ref, first):
        _, size, half = GATHERS[n]
        part = pl.ds(0, half) if first else pl.ds(half, size - half)
        return ref.at[:, part] if len(ref.shape) == 2 else ref.at[:, :, part]

    def first_send(n, kk):
        for h in (0, 1):
            src = half_block(n, kk, h, 0)
            shared[n, kk, h, 1] = [share(src, src, beside(h, 1, step, x, y, c)) for step in (1, 3)]

    def pass_on(n, kk, h, phase, find):
        onward = []
        for copy, step in zip(shared[n, kk, h, phase], (1, 3)):
            copy.wait_recv()
            here = find(n, kk, h, 4 - step)
            part = part_of(n, here, step == 1)
            onward.append(share(part, part, beside(h, phase, step, x, y, c)))
            if phase == 2:
                to_sibling[n].append(share(here, here, sibling))
        shared[n, kk, h, phase] = onward

    def first_on(n, kk):
        for h in (0, 1):
            pass_on(n, kk, h, 1, half_block)

    def second_send(n, kk):
        for h in (0, 1):
            for copy in shared[n, kk, h, 1]:
                copy.wait_recv()
            src = lane_of(n, kk, h, 0)
            shared[n, kk, h, 2] = [share(src, src, beside(h, 2, step, x, y, c)) for step in (1, 3)]
            to_sibling[n].append(share(src, src, sibling))

    def second_on(n, kk):
        for h in (0, 1):
            pass_on(n, kk, h, 2, lane_of)

    def second_end(n, kk):
        for h in (0, 1):
            for copy in shared[n, kk, h, 2]:
                copy.wait_recv()
            here = lane_of(n, kk, h, 2)
            to_sibling[n].append(share(here, here, sibling))

    def complete(n):
        for copy in to_sibling[n]:
            copy.wait_recv()

    def collect(half, rows):
        wide = (32, 1024)
        owner_of = lax.broadcasted_iota(jnp.int32, wide, 0) == lax.div(
            lax.broadcasted_iota(jnp.int32, wide, 1), 32
        )
        fold = lax.rem(lax.broadcasted_iota(jnp.int32, (1024, 128), 0), 32) == lax.broadcasted_iota(
            jnp.int32, (1024, 128), 1
        )
        fold = low(jnp.where(fold, 1.0, 0.0))
        tables = [low(dot(low(jnp.where(owner_of, row, 0.0)), fold)) for row in rows]

        def open_up(size, *terms):
            lanes = size * 32
            lane = lax.broadcasted_iota(jnp.int32, (128, lanes), 1)
            source = lax.broadcasted_iota(jnp.int32, (128, lanes), 0)
            found = jnp.zeros((32, lanes), jnp.float32)
            for table, offset in terms:
                pick_at = (lax.rem(lane, size) + offset == source) & (source < 32)
                found = found + dot(table, low(jnp.where(pick_at, 1.0, 0.0)))
            mine = lax.broadcasted_iota(jnp.int32, (32, lanes), 0) == lax.div(
                lax.broadcasted_iota(jnp.int32, (32, lanes), 1), size
            )
            return total(jnp.where(mine, found, 0.0))

        at = pl.ds(half * 512, 512)
        b_qv[0:1, at] = open_up(16, (tables[0], 0))
        b_qv[1:2, at] = open_up(16, (tables[0], 16))
        b_ff[:, pl.ds(half * 2048, 2048)] = open_up(64, (tables[1], 0), (tables[2], -32))

    def take_parameters():
        for half in (0, 1):
            rows = high(w[half, :, EXTRA:UP]).T
            if half == 0:
                gains[...] = rows[0:2]
                shifts[...] = rows[2:6]
            collect(half, (rows[6:7], rows[7:8], rows[8:9]))

    first_half = lax.broadcasted_iota(jnp.int32, (ROWS, 128), 1) < HD
    position = lax.broadcasted_iota(jnp.int32, (ROWS, ROWS), 0).astype(jnp.float32)
    scale = HD**-0.5

    def pick(e, value):
        return jnp.where(first_half == (e == 0), value, jnp.zeros_like(value))

    def forward(x, after=lambda stage: None):

        def project(i):
            half, j = lax.div(i, 3), lax.rem(i, 3)
            p = dot(x[...], w[half, :, columns(j * BLOCK, BLOCK)])
            at = columns(half * BLOCK, BLOCK)

            @pl.when(j == 0)
            def _():
                q[:, at] = low(p + b_qv[0:1, at])

            @pl.when(j == 1)
            def _():
                k[:, at] = low(p)

            @pl.when(j == 2)
            def _():
                v[:, at] = low(p + b_qv[1:2, at])

        each(6, project)
        after("qkv")

        def heads(i):
            at = columns(i * 128, 128)
            kp, vp, qp = k[:, at], v[:, at], q[:, at] * scale
            vt, outs = vp.T, []
            for e in (0, 1):
                scores = jnp.where(position < span[0:1, 0:1], dot_nt(kp, pick(e, qp)), -1e9)
                powers = jnp.exp(scores - jnp.max(scores, 0, keepdims=True))
                p = low(powers * (1.0 / total(powers)))
                probs[2 * i + e] = p
                outs.append(dot(vt[64 * e : 64 * e + 64], p))
            o[:, at] = low(jnp.concatenate(outs)).T

        each(4, lambda i: (heads(2 * i), heads(2 * i + 1)))
        after("heads")
        attended = dot_nt(o[:, 0:512], w[0, :, 1536:2048]) + dot_nt(o[:, 512:1024], w[1, :, 1536:2048])
        normed, inverse = normalize(high(x[...]) + attended + shifts[0:1])
        n1[...], i1[...] = normed, inverse
        hidden = normed * gains[0:1] + shifts[1:2]
        res[...] = hidden
        hid[...] = low(hidden)
        after("hid")

        def widen(i):
            half, j = lax.div(i, 4), lax.rem(i, 4)
            at = columns(i * BLOCK, BLOCK)
            u = dot(hid[...], w[half, :, columns(UP + j * BLOCK, BLOCK)]) + b_ff[:, at]
            phi = 0.5 + 0.5 * lax.erf(u * 0.7071067811865476)
            act[:, at] = low(u * phi)
            slope[:, at] = low(phi + u * (jnp.exp(u * u * -0.5) * 0.3989422804014327))

        each(8, widen)
        after("act")

        def narrow(i):
            at = columns(i * 256, 256)
            rows = pl.ds(pl.multiple_of(i * 256, 256), 256)
            acc[:, at] = dot_nt(act[:, 0:2048], w[0, rows, DOWN:COLS]) + dot_nt(
                act[:, 2048:4096], w[1, rows, DOWN:COLS]
            )

        each(4, narrow)
        normed, inverse = normalize(res[...] + acc[...] + shifts[2:3])
        n2[...], i2[...] = normed, inverse
        return low(normed * gains[1:2] + shifts[3:4])

    def backward(grad_out, after=lambda stage: None):
        normed = n2[...]
        d_gains[1:2] = total(grad_out * normed)
        d_shifts[3:4] = total(grad_out)
        d_sum = norm_backward(grad_out * gains[1:2], normed, i2[...])
        d_shifts[2:3] = total(d_sum)
        res[...] = d_sum
        d_low[...] = low(d_sum)
        after("d_low")

        def widen(i):
            half, j = lax.div(i, 4), lax.rem(i, 4)
            at = columns(i * BLOCK, BLOCK)
            d = low(dot(d_low[...], w[half, :, columns(DOWN + j * BLOCK, BLOCK)]) * high(slope[:, at]))
            d_act[:, at] = d
            d_bff[:, at] = total(high(d))

        each(8, widen)
        after("d_act")

        def narrow(i):
            at = columns(i * 256, 256)
            rows = pl.ds(pl.multiple_of(i * 256, 256), 256)
            acc[:, at] = dot_nt(d_act[:, 0:2048], w[0, rows, UP:DOWN]) + dot_nt(
                d_act[:, 2048:4096], w[1, rows, UP:DOWN]
            )

        each(4, narrow)
        d_hidden = res[...] + acc[...]
        normed = n1[...]
        d_gains[0:1] = total(d_hidden * normed)
        d_shifts[1:2] = total(d_hidden)
        d_sum = norm_backward(d_hidden * gains[0:1], normed, i1[...])
        d_shifts[0:1] = total(d_sum)
        res[...] = d_sum
        a_low[...] = low(d_sum)
        after("a_low")
        for half in (0, 1):
            d_qkv[2, :, half * 512 : half * 512 + 512] = low(dot(a_low[...], w[half, :, 1536:EXTRA]))

        def heads(i):
            at = columns(i * 128, 128)
            kp, vp, qp, d_o = k[:, at], v[:, at], q[:, at], d_qkv[2, :, at]
            kt, parts = kp.T, []
            for e in (0, 1):
                p_low = probs[2 * i + e]
                p = high(p_low)
                product = p * dot_nt(vp, pick(e, d_o))
                d_s = low(product - p * total(product))
                parts.append(
                    (dot(kt[64 * e : 64 * e + 64], d_s) * scale, dot(d_s, qp) * scale, dot(p_low, d_o))
                )
            d_q = low(jnp.concatenate([parts[0][0], parts[1][0]])).T
            d_k, d_v = (low(jnp.where(first_half, a, b)) for a, b in zip(parts[0][1:], parts[1][1:]))
            d_qkv[0, :, at] = d_q
            d_qkv[1, :, at] = d_k
            d_qkv[2, :, at] = d_v
            d_bqv[0:1, at] = total(high(d_q))
            d_bqv[1:2, at] = total(high(d_v))

        each(4, lambda i: (heads(2 * i), heads(2 * i + 1)))
        after("d_qkv")

        def narrow_in(i):
            at = columns(i * 256, 256)
            rows = pl.ds(pl.multiple_of(i * 256, 256), 256)
            acc[:, at] = sum(
                dot_nt(d_qkv[j, :, 512 * half : 512 * half + 512], w[half, rows, 512 * j : 512 * j + 512])
                for half in (0, 1)
                for j in (0, 1, 2)
            )

        each(4, narrow_in)
        return low(res[...] + acc[...])

    other_half = columns((1 - c) * 2048, 2048)
    other_heads = columns((1 - c) * 512, 512)

    def swap(name, src, dst):
        given[name] = send(src, dst, sibling)

    def have(*names):
        for name in names:
            given[name].wait_recv()

    def block(start, left, right, s_left, s_right):
        whole = low(dot_tn(jnp.concatenate([left, s_left]), jnp.concatenate([right, s_right])))
        for chip in range(16):
            for h in (0, 1):
                f, g = (chip // 4, chip % 4) if h == 0 else (chip % 4, chip // 4)
                to, of = h * 512 + f * 128 + g * 32, chip * 64 + h * 32
                w[0, to : to + 32, columns(start, right.shape[1])] = whole[of : of + 32]

    def grads_down(first):
        def one(i):
            i = i + first
            at = columns(i * BLOCK, BLOCK)
            block(DOWN + i * BLOCK, d_low[...], act[:, columns(c * 2048 + i * BLOCK, BLOCK)], s_d_low[...], s_act[:, at])

        each(2, one)

    def grads_up(first):
        def one(i):
            i = i + first
            at = columns(i * BLOCK, BLOCK)
            block(UP + i * BLOCK, hid[...], d_act[:, columns(c * 2048 + i * BLOCK, BLOCK)], s_hid[...], s_d_act[:, at])

        each(2, one)

    def spread(row, size, offset):
        lanes = row.shape[1]
        wide = (32, lanes)
        owner = lax.broadcasted_iota(jnp.int32, wide, 0) == lax.div(
            lax.broadcasted_iota(jnp.int32, wide, 1), size
        )
        fold = lax.rem(lax.broadcasted_iota(jnp.int32, (lanes, 128), 0), size) == lax.broadcasted_iota(
            jnp.int32, (lanes, 128), 1
        )
        table = dot(low(jnp.where(owner, row, 0.0)), low(jnp.where(fold, 1.0, 0.0)))
        back = (128, 1024)
        lane = lax.broadcasted_iota(jnp.int32, back, 1)
        source = lax.broadcasted_iota(jnp.int32, back, 0)
        span = min(size, 32)
        place_in = lax.rem(lane, 32)
        if size == 16:
            open_ = (place_in == source + offset) & (source < span)
        else:
            open_ = (place_in + offset == source) & (source < size)
        rows = dot(low(table), low(jnp.where(open_, 1.0, 0.0)))
        mine = lax.broadcasted_iota(jnp.int32, (32, 1024), 0) == lax.div(
            lax.broadcasted_iota(jnp.int32, (32, 1024), 1), 32
        )
        return total(jnp.where(mine, rows, 0.0))

    def small_rows(half, dst):
        heads_at, units_at = columns(half * 512, 512), columns(half * 2048, 2048)
        dst[...] = jnp.zeros_like(dst)
        dst[0:2] = d_gains[...]
        dst[2:6] = d_shifts[...]
        dst[6:7] = spread(d_bqv[0:1, heads_at], 16, 0) + spread(d_bqv[1:2, heads_at], 16, 16)
        dst[7:8] = spread(d_bff[:, units_at], 64, 0)
        dst[8:9] = spread(d_bff[:, units_at], 64, 32)

    def grads_qkv():
        for j in (0, 1, 2):
            block(j * 512, x_in[...], d_qkv[j, :, columns(c * 512, 512)], s_x[...], s_d_qkv[j])

    def grads_rest():
        block(1536, a_low[...], o[:, columns(c * 512, 512)], s_a_low[...], s_o[...])
        summed = small[0] + s_small[...]
        column = low(jnp.concatenate([summed, jnp.zeros((112, 1024), jnp.float32)], axis=0).T)
        for chip in range(16):
            for h in (0, 1):
                f, g = (chip // 4, chip % 4) if h == 0 else (chip % 4, chip // 4)
                to, of = h * 512 + f * 128 + g * 32, chip * 64 + h * 32
                w[0, to : to + 32, EXTRA:UP] = column[of : of + 32]

    sent = {}

    def side(h, phase):
        return x if (h == 0) == (phase == 1) else y

    def rows_at(h, step):
        return pl.ds(pl.multiple_of(h * 512 + lax.rem(side(h, 1) + step, 4) * 128, 128), 128)

    def line_at(h, step):
        start = h * 512 + side(h, 1) * 128 + lax.rem(side(h, 2) + step, 4) * 32
        return pl.ds(pl.multiple_of(start, 32), 32)

    def parts(n):
        start, size, half = PASSES[n]
        return pl.ds(start, size), pl.ds(start, half), pl.ds(start + half, size - half)

    def add(dst, *others):
        def one(i):
            at = pl.ds(pl.multiple_of(i * 16, 16), 16)
            dst[at] = low(sum((high(o[at]) for o in others), high(dst[at])))

        each(dst.shape[0] // 16, one)

    def far(n):
        whole, part_a, part_b = parts(n)
        for h in (0, 1):
            rows = rows_at(h, 2)
            sent[n, h, "far"] = (
                send(w.at[0, rows, part_a], passing.at[h, :, part_a], beside(h, 1, 1, x, y, c)),
                send(w.at[0, rows, part_b], passing.at[h, :, part_b], beside(h, 1, 3, x, y, c)),
            )

    def near(n):
        whole, part_a, part_b = parts(n)
        for h in (0, 1):
            up, down = sent[n, h, "far"]
            up.wait_recv()
            add(w.at[0, rows_at(h, 1), part_a], passing.at[h, :, part_a])
            one = send(w.at[0, rows_at(h, 1), whole], near_p.at[h, :, whole], beside(h, 1, 1, x, y, c))
            down.wait_recv()
            add(w.at[0, rows_at(h, 3), part_b], passing.at[h, :, part_b])
            two = send(w.at[0, rows_at(h, 3), whole], near_m.at[h, :, whole], beside(h, 1, 3, x, y, c))
            sent[n, h, "near"] = (one, two)

    def q_far(n):
        whole, part_a, part_b = parts(n)
        for h in (0, 1):
            for copy in sent[n, h, "near"]:
                copy.wait_recv()
            add(w.at[0, rows_at(h, 0), whole], near_p.at[h, :, whole], near_m.at[h, :, whole])
            rows = line_at(h, 2)
            sent[n, h, "q_far"] = (
                send(w.at[0, rows, part_a], q_passing.at[h, :, part_a], beside(h, 2, 1, x, y, c)),
                send(w.at[0, rows, part_b], q_passing.at[h, :, part_b], beside(h, 2, 3, x, y, c)),
            )

    def q_near(n):
        whole, part_a, part_b = parts(n)
        for h in (0, 1):
            up, down = sent[n, h, "q_far"]
            up.wait_recv()
            add(w.at[0, line_at(h, 1), part_a], q_passing.at[h, :, part_a])
            one = send(w.at[0, line_at(h, 1), whole], q_p.at[h, :, whole], beside(h, 2, 1, x, y, c))
            down.wait_recv()
            add(w.at[0, line_at(h, 3), part_b], q_passing.at[h, :, part_b])
            two = send(w.at[0, line_at(h, 3), whole], q_m.at[h, :, whole], beside(h, 2, 3, x, y, c))
            sent[n, h, "q_near"] = (one, two)

    crossing, handing = {}, {}
    owner, sender = c == t, c != t

    def remote(i, src, dst, where):
        return pltpu.make_async_remote_copy(
            src_ref=src,
            dst_ref=dst,
            send_sem=send_sems.at[N_EACH + i],
            recv_sem=recv_sems.at[N_EACH + i],
            device_id=where,
            device_id_type=MESH,
        )

    def cross(n):
        whole, _, _ = parts(n)
        for h in (0, 1):
            for copy in sent[n, h, "q_near"]:
                copy.wait_recv()
            add(w.at[0, line_at(h, 0), whole], q_p.at[h, :, whole], q_m.at[h, :, whole])
            crossing[n, h] = remote(
                2 * n + h, w.at[0, line_at(h, 0), whole], mate.at[h, :, whole], {"tensor": 1 - t}
            )

            @pl.when(sender)
            def _():
                crossing[n, h].start()

    def hand(n):
        whole, _, _ = parts(n)
        handing[n] = remote(12 + n, to_mate.at[:, whole], out.at[:, whole], sibling)

        @pl.when(owner)
        def _():
            for h in (0, 1):
                crossing[n, h].wait_recv()
                value = high(w[0, line_at(h, 0), whole]) + high(mate[h, :, whole])

                @pl.when(c == h)
                def _():
                    out[:, whole] = value

                @pl.when(c != h)
                def _():
                    to_mate[:, whole] = value

            handing[n].start()

    def exchange(n):
        copy = send(
            kept.at[n], relay.at[n], {"section": 1 - s, "dp": dp_at(x, y, t), "tensor": c}
        )
        copy.wait_recv()
        return relay[n]

    def last_stage(stage):
        if stage == "d_low":
            swap("d_low", d_low, s_d_low)
        if stage == "d_act":
            swap("d_act", d_act.at[:, other_half], s_d_act)
            have("act", "d_low")
            grads_down(0)
            far(0)
            grads_down(2)
            far(1)
        if stage == "a_low":
            swap("a_low", a_low, s_a_low)
            near(0)
            have("hid", "d_act")
            grads_up(0)
            far(2)
            near(1)
            grads_up(2)
            far(3)
            near(2)
        if stage == "d_qkv":
            swap("d_qkv", d_qkv.at[:, :, other_heads], s_d_qkv)
            small_rows(1 - c, small.at[1])
            swap("small", small.at[1], s_small)
            small_rows(c, small.at[0])
            q_far(0)
            near(3)
            q_far(1)

    def first_stage(stage):
        if stage == "qkv":
            second_on(1, 0)
            second_send(2, 0)
            first_on(2, 1)
        if stage == "heads":
            second_on(1, 1)
            second_send(2, 1)
        if stage == "hid":
            second_end(1, 0)
            second_end(1, 1)
            second_on(2, 0)
            complete(1)
        if stage == "act":
            second_on(2, 1)
            second_end(2, 0)
            second_end(2, 1)
            complete(2)

    lent = (
        remote(18, ends.at[1 - t], x_in, sibling),
        remote(19, spans.at[1 - t], span_in, sibling),
    )

    @pl.when(owner)
    def _():
        for copy in lent:
            copy.start()

    shard_load.wait()
    z_sends = []
    for n, (start, size, _) in enumerate(GATHERS):
        part = own.at[:, :, pl.ds(start, size)]
        z_sends.append(share(part, part, {"tensor": 1 - t}))
        first_send(n, 0)
    first_on(0, 0)
    z_sends[0].wait_recv()
    first_send(0, 1)
    second_send(0, 0)
    first_on(0, 1)
    first_on(1, 0)
    second_send(0, 1)
    z_sends[1].wait_recv()
    first_send(1, 1)
    second_on(0, 0)
    second_send(1, 0)
    first_on(1, 1)
    second_on(0, 1)
    z_sends[2].wait_recv()
    first_on(2, 0)
    first_send(2, 1)
    second_send(1, 1)
    second_end(0, 0)
    second_end(0, 1)
    complete(0)
    take_parameters()
    own_load.wait()
    span[...] = spans[t]

    @pl.when(sender)
    def _():
        for copy in lent:
            copy.wait_recv()
        x_own[...] = jnp.where(s == 1, x_in[...], x_own[...])
        span[...] = jnp.where(s == 1, span_in[...], span[...])

    kept[0] = forward(x_own, first_stage)
    share.finish()
    x_in[...] = jnp.where(s == 0, x_own[...], exchange(0))
    swap("x", x_in, s_x)
    result = forward(x_in)
    swap("hid", hid, s_hid)
    swap("act", act.at[:, other_half], s_act)
    swap("o", o.at[:, other_heads], s_o)
    kept[2] = result
    kept[1] = backward(high(x_own[...]))
    grad_out = jnp.where(s == 1, x_own[...], exchange(1))
    d_x = backward(high(grad_out), last_stage)
    kept[2] = jnp.where(s == 0, d_x, kept[2])
    slot = t + s * (c - t)
    done, moved = kept.at[2], (s == 1) & sender
    here = pltpu.make_async_copy(done, ends_out.at[slot], io_sems.at[1])
    beyond = remote(20, done, ends_out.at[slot], {"tensor": 1 - t})
    to_core = remote(21, done, ends_out.at[slot], sibling)
    to_cross = remote(22, done, ends_out.at[slot], {"dp": dp_at(x, y, 1 - c), "tensor": 1 - t})

    @pl.when(moved)
    def _():
        to_core.start()
        to_cross.start()

    @pl.when(jnp.logical_not(moved))
    def _():
        here.start()
        beyond.start()

    have("o", "a_low", "x", "d_qkv", "small")
    grads_qkv()
    far(4)
    q_far(2)
    q_near(0)
    grads_rest()
    far(5)
    near(4)
    q_near(1)
    q_far(3)
    cross(0)
    q_near(2)
    cross(1)
    near(5)
    q_near(3)
    hand(0)
    cross(2)
    hand(1)
    q_far(4)
    cross(3)
    q_far(5)
    hand(2)
    q_near(4)
    q_near(5)
    hand(3)
    cross(4)
    cross(5)
    hand(4)
    hand(5)
    for n in range(6):

        @pl.when(sender)
        def _():
            handing[n].wait_recv()
            for h in (0, 1):
                crossing[n, h].wait_send()

        @pl.when(owner)
        def _():
            handing[n].wait_send()

    @pl.when(moved)
    def _():
        to_core.wait_send()
        to_cross.wait()
        beyond.wait_recv()

    @pl.when(jnp.logical_not(moved))
    def _():
        here.wait()
        beyond.wait_send()

    @pl.when(s == 0)
    def _():
        beyond.wait_recv()

    @pl.when((s == 1) & owner)
    def _():
        to_core.wait_recv()

    @pl.when(owner)
    def _():
        for copy in lent:
            copy.wait_send()

    send.finish()


def run_layers(spans, ends, shard):
    vmem = pltpu.VMEM
    bf, f32 = jnp.bfloat16, jnp.float32
    hbm = pl.BlockSpec(memory_space=pl.ANY)
    near = pl.BlockSpec(memory_space=vmem)
    sem = pltpu.SemaphoreType.DMA
    shape = jax.ShapeDtypeStruct
    return pl.pallas_call(
        layers_kernel,
        out_shape=(
            shape((2, ROWS, 1024), bf),
            shape((32, COLS), f32),
        ),
        in_specs=[near, hbm, hbm],
        out_specs=(hbm, near),
        scratch_shapes=[
            vmem((2, 1024), f32),
            vmem((4, 1024), f32),
            vmem((2, 1024), f32),
            vmem((1, 4096), f32),
            vmem((2, 1024), f32),
            vmem((4, 1024), f32),
            vmem((2, 1024), f32),
            vmem((1, 4096), f32),
            vmem((2, 4, 4, 2, 2, 16, COLS), bf),
            vmem((ROWS, 1024), bf),
            vmem((ROWS, 1024), bf),
            vmem((2, ROWS, 1024), bf),
            vmem((ROWS, 1024), bf),
            vmem((ROWS, 1024), bf),
            vmem((ROWS, 1024), bf),
            vmem((ROWS, 1024), bf),
            vmem((16, ROWS, ROWS), bf),
            vmem((ROWS, 1024), f32),
            vmem((ROWS, 1024), f32),
            vmem((ROWS, 1), f32),
            vmem((ROWS, 1), f32),
            vmem((ROWS, 1024), f32),
            vmem((ROWS, 1024), bf),
            vmem((ROWS, 4096), bf),
            vmem((ROWS, 4096), bf),
            vmem((ROWS, 4096), bf),
            vmem((3, ROWS, 1024), bf),
            vmem((ROWS, 1024), f32),
            vmem((ROWS, 1024), bf),
            vmem((ROWS, 1024), bf),
            vmem((3, ROWS, 1024), bf),
            vmem((2, 16, 1024), f32),
            vmem((ROWS, 1024), bf),
            vmem((ROWS, 1024), bf),
            vmem((ROWS, 1024), bf),
            vmem((ROWS, 1024), bf),
            vmem((ROWS, 2048), bf),
            vmem((ROWS, 2048), bf),
            vmem((ROWS, 512), bf),
            vmem((3, ROWS, 512), bf),
            vmem((16, 1024), f32),
            vmem((2, 128, COLS), bf),
            vmem((2, 128, COLS), bf),
            vmem((2, 128, COLS), bf),
            vmem((2, 32, COLS), bf),
            vmem((2, 32, COLS), bf),
            vmem((2, 32, COLS), bf),
            vmem((2, 32, COLS), bf),
            vmem((32, COLS), f32),
            vmem((8, 128), f32),
            vmem((8, 128), f32),
            sem((2,)),
            sem((N_EACH + 23,)),
            sem((N_EACH + 23,)),
            sem((N_GATHER,)),
            sem((N_GATHER,)),
        ],
        compiler_params=pltpu.CompilerParams(
            collective_id=0, has_side_effects=True, vmem_limit_bytes=62 * 2**20
        ),
        name="run_layers",
    )(spans, ends, shard)


def pack_kernel(w_qkv, w_out, w_up, w_down, gains, shifts, b_qv, b_ff, shard, small):
    for j in (0, 1, 2):
        shard[:, j * 512 : j * 512 + 512] = w_qkv[0, j]
    shard[:, 1536:EXTRA] = w_out[0]
    shard[:, UP:DOWN] = w_up[0]
    shard[:, DOWN:COLS] = w_down[0]
    small[...] = jnp.zeros_like(small)
    small[0:2, 0:32] = high(gains[0])
    small[2:6, 0:32] = high(shifts[0])
    small[6:7, 0:32] = jnp.concatenate([high(b_qv[0, 0, 0:1]), high(b_qv[0, 0, 1:2])], axis=1)
    small[7:8, 0:32] = high(b_ff[0, :, 0:32])
    small[8:9, 0:32] = high(b_ff[0, :, 32:64])
    shard[:, EXTRA:UP] = low(small[...].T[0:32])


def pack_shard(w_qkv, w_out, w_up, w_down, gains, shifts, b_qv, b_ff):
    return pl.pallas_call(
        pack_kernel,
        out_shape=jax.ShapeDtypeStruct((32, COLS), jnp.bfloat16),
        scratch_shapes=[pltpu.VMEM((128, 128), jnp.float32)],
        name="pack_shard",
    )(
        w_qkv.transpose(0, 2, 1, 3),
        w_out.transpose(0, 2, 1),
        w_up,
        w_down.transpose(0, 2, 1),
        gains,
        shifts,
        b_qv.transpose(0, 2, 1, 3),
        b_ff,
    )


def unpack_kernel(got, w_qkv, w_out, w_up, w_down, gains, shifts, b_qv, b_ff):
    for j in (0, 1, 2):
        w_qkv[0, j] = got[:, j * 512 : j * 512 + 512]
    w_out[0] = got[:, 1536:EXTRA]
    w_up[0] = got[:, UP:DOWN]
    w_down[0] = got[:, DOWN:COLS]
    rows = got[:, EXTRA:UP].T
    gains[0] = rows[0:2]
    shifts[0] = rows[2:6]
    b_qv[0, 0, 0:1] = rows[6:7, 0:16]
    b_qv[0, 0, 1:2] = rows[6:7, 16:32]
    b_ff[0] = jnp.concatenate([rows[7:8], rows[8:9]], axis=1)


def unpack_shard(got):
    shapes = ((1, 3, 32, 512), (1, 32, 512), (1, 32, 2048), (1, 32, 2048), (1, 2, 32), (1, 4, 32))
    shapes = shapes + ((1, 1, 2, 16), (1, 1, 64))
    w_qkv, w_out, w_up, w_down, gains, shifts, b_qv, b_ff = pl.pallas_call(
        unpack_kernel,
        out_shape=tuple(jax.ShapeDtypeStruct(shape, jnp.float32) for shape in shapes),
        name="unpack_shard",
    )(got)
    return (
        w_qkv.transpose(0, 2, 1, 3),
        w_out.transpose(0, 2, 1),
        w_up,
        w_down.transpose(0, 2, 1),
        gains,
        shifts,
        b_qv.transpose(0, 2, 1, 3),
        b_ff,
    )


def body(ends, lengths, *weights):
    shard = pack_shard(*weights)
    spans = jnp.broadcast_to(lengths[:, :, None].astype(jnp.float32), (2, 8, 128))
    ends_out, got = run_layers(spans, ends.reshape(2, ROWS, 1024), shard.reshape(2, 16, COLS))
    return (ends_out.reshape(1, 2, 1, ROWS, 1024),) + unpack_shard(got)


def solution(mesh):
    in_specs = (
        P("section", None, "dp", None, None),
        P(None, "dp"),
        P("section", "dp", None, "tensor"),
        P("section", "tensor", "dp"),
        P("section", "dp", "tensor"),
        P("section", "tensor", "dp"),
        P("section", None, "dp"),
        P("section", None, "dp"),
        P("section", None, "tensor", "dp"),
        P("section", "tensor", "dp"),
    )
    out_specs = (
        P("section", None, "dp", None, None),
        P("section", "dp", None, "tensor"),
        P("section", "tensor", "dp"),
        P("section", "dp", "tensor"),
        P("section", "tensor", "dp"),
        P("section", None, "dp"),
        P("section", None, "dp"),
        P("section", None, "tensor", "dp"),
        P("section", "tensor", "dp"),
    )
    return jax.shard_map(body, mesh=mesh, in_specs=in_specs, out_specs=out_specs, check_vma=False)
```

```python
import jax
import jax.numpy as jnp
from jax import lax
from jax.experimental import pallas as pl
from jax.experimental.pallas import tpu as pltpu
from jax.sharding import PartitionSpec as P

HD = 64
epsilon = 1e-05

COLS = 6272
ROWS = 192
BLOCK = 512
EXTRA, UP, DOWN = 2048, 2176, 4224
GATHERS = ((0, 2176, 1152), (UP, 2048, 1024), (DOWN, 2048, 1024))
PASSES = (
    (DOWN, 1024, 512),
    (DOWN + 1024, 1024, 512),
    (UP, 1024, 512),
    (UP + 1024, 1024, 512),
    (0, 1536, 768),
    (1536, 640, 384),
)


OFFSETS = (0, 3, 1, 2)
MESH = pl.DeviceIdType.MESH


def place():
    d = lax.axis_index("dp")
    return lax.div(d, 8), lax.rem(lax.div(d, 2), 4), lax.rem(d, 2), lax.axis_index("tensor")


def dp_at(x, y, c):
    return (x * 4 + y) * 2 + c


def beside(h, phase, step, x, y, c):
    if (h == 0) == (phase == 1):
        return {"dp": dp_at(lax.rem(x + step, 4), y, c)}
    return {"dp": dp_at(x, lax.rem(y + step, 4), c)}


def meet(x, y, c, t):
    barrier = pltpu.get_barrier_semaphore()
    partners = [
        {"dp": dp_at(lax.rem(x + 1, 4), y, c)},
        {"dp": dp_at(lax.rem(x + 3, 4), y, c)},
        {"dp": dp_at(x, lax.rem(y + 1, 4), c)},
        {"dp": dp_at(x, lax.rem(y + 3, 4), c)},
        {"dp": dp_at(x, y, 1 - c)},
        {"tensor": 1 - t},
        {"dp": dp_at(x, y, 1 - c), "tensor": 1 - t},
        {"section": 1 - lax.axis_index("section"), "dp": dp_at(x, y, t), "tensor": c},
    ]
    for partner in partners:
        pl.semaphore_signal(barrier, inc=1, device_id=partner, device_id_type=MESH)
    pl.semaphore_wait(barrier, len(partners))


class Sender:
    def __init__(self, send_sems, recv_sems):
        self.send_sems, self.recv_sems, self.copies = send_sems, recv_sems, []

    def __call__(self, src, dst, where):
        i = len(self.copies)
        copy = pltpu.make_async_remote_copy(
            src_ref=src,
            dst_ref=dst,
            send_sem=self.send_sems.at[i],
            recv_sem=self.recv_sems.at[i],
            device_id=where,
            device_id_type=MESH,
        )
        copy.start()
        self.copies.append(copy)
        return copy

    def finish(self):
        for copy in self.copies:
            copy.wait_send()


N_EACH = 107
N_GATHER = 147


def dot(a, b):
    return lax.dot_general(a, b, (((1,), (0,)), ((), ())), preferred_element_type=jnp.float32)


def dot_nt(a, b):
    return lax.dot_general(a, b, (((1,), (1,)), ((), ())), preferred_element_type=jnp.float32)


def dot_tn(a, b):
    return lax.dot_general(a, b, (((0,), (0,)), ((), ())), preferred_element_type=jnp.float32)


def low(v):
    return v.astype(jnp.bfloat16)


def high(v):
    return v.astype(jnp.float32)


def columns(start, size):
    return pl.ds(pl.multiple_of(start, 128), size)


def each(count, work):
    lax.fori_loop(0, count, lambda i, z: (work(i), z)[1], 0)


def total(v):
    return jnp.sum(v, axis=0, keepdims=True)


def normalize(values):
    centred = values - jnp.mean(values, -1, keepdims=True)
    inverse_std = lax.rsqrt(jnp.mean(centred * centred, -1, keepdims=True) + epsilon)
    return centred * inverse_std, inverse_std


def norm_backward(grad_norm, normed, inverse_std):
    return inverse_std * (
        grad_norm
        - jnp.mean(grad_norm, -1, keepdims=True)
        - normed * jnp.mean(grad_norm * normed, -1, keepdims=True)
    )


def layers_kernel(
    spans, ends, shard,
    ends_out, out,
    gains, shifts, b_qv, b_ff,
    d_gains, d_shifts, d_bqv, d_bff,
    blocks, x_own, x_in, relay, q, k, v, o, probs, n1, n2, i1, i2, res, hid, act, slope, d_act, d_qkv,
    acc, d_low, a_low, kept, small,
    s_x, s_hid, s_d_low, s_a_low, s_act, s_d_act, s_o, s_d_qkv, s_small,
    passing, near_p, near_m, q_passing, q_p, q_m, mate, to_mate, span, span_in,
    io_sems, send_sems, recv_sems, gather_send_sems, gather_recv_sems,
):
    x, y, c, t = place()
    s = lax.axis_index("section")
    w = blocks.reshape(2, 1024, COLS)
    own_load = pltpu.make_async_copy(ends.at[t], x_own, io_sems.at[0])
    own_load.start()
    own = blocks.at[t, x, y, c]
    shard_load = pltpu.make_async_copy(shard, own, io_sems.at[1])
    shard_load.start()
    meet(x, y, c, t)
    send = Sender(send_sems, recv_sems)
    share = Sender(gather_send_sems, gather_recv_sems)
    sibling = {"dp": dp_at(x, y, 1 - c)}
    given, shared, to_sibling = {}, {}, {0: [], 1: [], 2: []}

    def half_block(n, kk, h, step):
        start, size, _ = GATHERS[n]
        tt = t if kk == 0 else 1 - t
        xx, yy = (lax.rem(x + step, 4), y) if h == 0 else (x, lax.rem(y + step, 4))
        return blocks.at[tt, xx, yy, c, h, :, pl.ds(start, size)]

    def lane_of(n, kk, h, step):
        start, size, _ = GATHERS[n]
        tt = t if kk == 0 else 1 - t
        if h == 0:
            return blocks.at[tt, :, lax.rem(y + step, 4), c, 0, :, pl.ds(start, size)]
        return blocks.at[tt, lax.rem(x + step, 4), :, c, 1, :, pl.ds(start, size)]

    def part_of(n, ref, first):
        _, size, half = GATHERS[n]
        part = pl.ds(0, half) if first else pl.ds(half, size - half)
        return ref.at[:, part] if len(ref.shape) == 2 else ref.at[:, :, part]

    def first_send(n, kk):
        for h in (0, 1):
            src = half_block(n, kk, h, 0)
            shared[n, kk, h, 1] = [share(src, src, beside(h, 1, step, x, y, c)) for step in (1, 3)]

    def pass_on(n, kk, h, phase, find):
        onward = []
        for copy, step in zip(shared[n, kk, h, phase], (1, 3)):
            copy.wait_recv()
            here = find(n, kk, h, 4 - step)
            part = part_of(n, here, step == 1)
            onward.append(share(part, part, beside(h, phase, step, x, y, c)))
            if phase == 2:
                to_sibling[n].append(share(here, here, sibling))
        shared[n, kk, h, phase] = onward

    def first_on(n, kk):
        for h in (0, 1):
            pass_on(n, kk, h, 1, half_block)

    def second_send(n, kk):
        for h in (0, 1):
            for copy in shared[n, kk, h, 1]:
                copy.wait_recv()
            src = lane_of(n, kk, h, 0)
            shared[n, kk, h, 2] = [share(src, src, beside(h, 2, step, x, y, c)) for step in (1, 3)]
            to_sibling[n].append(share(src, src, sibling))

    def second_on(n, kk):
        for h in (0, 1):
            pass_on(n, kk, h, 2, lane_of)

    def second_end(n, kk):
        for h in (0, 1):
            for copy in shared[n, kk, h, 2]:
                copy.wait_recv()
            here = lane_of(n, kk, h, 2)
            to_sibling[n].append(share(here, here, sibling))

    def complete(n):
        for copy in to_sibling[n]:
            copy.wait_recv()

    def collect(half, rows):
        wide = (32, 1024)
        owner_of = lax.broadcasted_iota(jnp.int32, wide, 0) == lax.div(
            lax.broadcasted_iota(jnp.int32, wide, 1), 32
        )
        fold = lax.rem(lax.broadcasted_iota(jnp.int32, (1024, 128), 0), 32) == lax.broadcasted_iota(
            jnp.int32, (1024, 128), 1
        )
        fold = low(jnp.where(fold, 1.0, 0.0))
        tables = [low(dot(low(jnp.where(owner_of, row, 0.0)), fold)) for row in rows]

        def open_up(size, *terms):
            lanes = size * 32
            lane = lax.broadcasted_iota(jnp.int32, (128, lanes), 1)
            source = lax.broadcasted_iota(jnp.int32, (128, lanes), 0)
            found = jnp.zeros((32, lanes), jnp.float32)
            for table, offset in terms:
                pick_at = (lax.rem(lane, size) + offset == source) & (source < 32)
                found = found + dot(table, low(jnp.where(pick_at, 1.0, 0.0)))
            mine = lax.broadcasted_iota(jnp.int32, (32, lanes), 0) == lax.div(
                lax.broadcasted_iota(jnp.int32, (32, lanes), 1), size
            )
            return total(jnp.where(mine, found, 0.0))

        at = pl.ds(half * 512, 512)
        b_qv[0:1, at] = open_up(16, (tables[0], 0))
        b_qv[1:2, at] = open_up(16, (tables[0], 16))
        b_ff[:, pl.ds(half * 2048, 2048)] = open_up(64, (tables[1], 0), (tables[2], -32))

    def take_parameters():
        for half in (0, 1):
            rows = high(w[half, :, EXTRA:UP]).T
            if half == 0:
                gains[...] = rows[0:2]
                shifts[...] = rows[2:6]
            collect(half, (rows[6:7], rows[7:8], rows[8:9]))

    first_half = lax.broadcasted_iota(jnp.int32, (ROWS, 128), 1) < HD
    position = lax.broadcasted_iota(jnp.int32, (ROWS, ROWS), 0).astype(jnp.float32)
    scale = HD**-0.5

    def pick(e, value):
        return jnp.where(first_half == (e == 0), value, jnp.zeros_like(value))

    def forward(x, after=lambda stage: None):

        def project(i):
            half, j = lax.div(i, 3), lax.rem(i, 3)
            p = dot(x[...], w[half, :, columns(j * BLOCK, BLOCK)])
            at = columns(half * BLOCK, BLOCK)

            @pl.when(j == 0)
            def _():
                q[:, at] = low(p + b_qv[0:1, at])

            @pl.when(j == 1)
            def _():
                k[:, at] = low(p)

            @pl.when(j == 2)
            def _():
                v[:, at] = low(p + b_qv[1:2, at])

        each(3, lambda i: (project(2 * i), project(2 * i + 1)))
        after("qkv")

        def heads(i):
            at = columns(i * 128, 128)
            kp, vp, qp = k[:, at], v[:, at], q[:, at] * scale
            vt, outs = vp.T, []
            for e in (0, 1):
                scores = jnp.where(position < span[0:1, 0:1], dot_nt(kp, pick(e, qp)), -1e9)
                powers = jnp.exp(scores - jnp.max(scores, 0, keepdims=True))
                p = low(powers * (1.0 / total(powers)))
                probs[2 * i + e] = p
                outs.append(dot(vt[64 * e : 64 * e + 64], p))
            o[:, at] = low(jnp.concatenate(outs)).T

        each(2, lambda i: [heads(4 * i + u) for u in range(4)])
        after("heads")
        attended = dot_nt(o[:, 0:512], w[0, :, 1536:2048]) + dot_nt(o[:, 512:1024], w[1, :, 1536:2048])
        normed, inverse = normalize(high(x[...]) + attended + shifts[0:1])
        n1[...], i1[...] = normed, inverse
        hidden = normed * gains[0:1] + shifts[1:2]
        res[...] = hidden
        hid[...] = low(hidden)
        after("hid")

        def widen(i):
            half, j = lax.div(i, 4), lax.rem(i, 4)
            at = columns(i * BLOCK, BLOCK)
            u = dot(hid[...], w[half, :, columns(UP + j * BLOCK, BLOCK)]) + b_ff[:, at]
            phi = 0.5 + 0.5 * lax.erf(u * 0.7071067811865476)
            act[:, at] = low(u * phi)
            slope[:, at] = low(phi + u * (jnp.exp(u * u * -0.5) * 0.3989422804014327))

        each(4, lambda i: (widen(2 * i), widen(2 * i + 1)))
        after("act")

        def narrow(i):
            at = columns(i * 256, 256)
            rows = pl.ds(pl.multiple_of(i * 256, 256), 256)
            acc[:, at] = dot_nt(act[:, 0:2048], w[0, rows, DOWN:COLS]) + dot_nt(
                act[:, 2048:4096], w[1, rows, DOWN:COLS]
            )

        each(2, lambda i: (narrow(2 * i), narrow(2 * i + 1)))
        normed, inverse = normalize(res[...] + acc[...] + shifts[2:3])
        n2[...], i2[...] = normed, inverse
        return low(normed * gains[1:2] + shifts[3:4])

    def backward(grad_out, after=lambda stage: None):
        normed = n2[...]
        d_gains[1:2] = total(grad_out * normed)
        d_shifts[3:4] = total(grad_out)
        d_sum = norm_backward(grad_out * gains[1:2], normed, i2[...])
        d_shifts[2:3] = total(d_sum)
        res[...] = d_sum
        d_low[...] = low(d_sum)
        after("d_low")

        def widen(i):
            half, j = lax.div(i, 4), lax.rem(i, 4)
            at = columns(i * BLOCK, BLOCK)
            d = low(dot(d_low[...], w[half, :, columns(DOWN + j * BLOCK, BLOCK)]) * high(slope[:, at]))
            d_act[:, at] = d
            d_bff[:, at] = total(high(d))

        each(4, lambda i: (widen(2 * i), widen(2 * i + 1)))
        after("d_act")

        def narrow(i):
            at = columns(i * 256, 256)
            rows = pl.ds(pl.multiple_of(i * 256, 256), 256)
            acc[:, at] = dot_nt(d_act[:, 0:2048], w[0, rows, UP:DOWN]) + dot_nt(
                d_act[:, 2048:4096], w[1, rows, UP:DOWN]
            )

        each(2, lambda i: (narrow(2 * i), narrow(2 * i + 1)))
        d_hidden = res[...] + acc[...]
        normed = n1[...]
        d_gains[0:1] = total(d_hidden * normed)
        d_shifts[1:2] = total(d_hidden)
        d_sum = norm_backward(d_hidden * gains[0:1], normed, i1[...])
        d_shifts[0:1] = total(d_sum)
        res[...] = d_sum
        a_low[...] = low(d_sum)
        after("a_low")
        for half in (0, 1):
            d_qkv[2, :, half * 512 : half * 512 + 512] = low(dot(a_low[...], w[half, :, 1536:EXTRA]))

        def heads(i):
            at = columns(i * 128, 128)
            kp, vp, qp, d_o = k[:, at], v[:, at], q[:, at], d_qkv[2, :, at]
            kt, parts = kp.T, []
            for e in (0, 1):
                p_low = probs[2 * i + e]
                p = high(p_low)
                product = p * dot_nt(vp, pick(e, d_o))
                d_s = low(product - p * total(product))
                parts.append(
                    (dot(kt[64 * e : 64 * e + 64], d_s) * scale, dot(d_s, qp) * scale, dot(p_low, d_o))
                )
            d_q = low(jnp.concatenate([parts[0][0], parts[1][0]])).T
            d_k, d_v = (low(jnp.where(first_half, a, b)) for a, b in zip(parts[0][1:], parts[1][1:]))
            d_qkv[0, :, at] = d_q
            d_qkv[1, :, at] = d_k
            d_qkv[2, :, at] = d_v
            d_bqv[0:1, at] = total(high(d_q))
            d_bqv[1:2, at] = total(high(d_v))

        each(2, lambda i: [heads(4 * i + u) for u in range(4)])
        after("d_qkv")

        def narrow_in(i):
            at = columns(i * 256, 256)
            rows = pl.ds(pl.multiple_of(i * 256, 256), 256)
            acc[:, at] = sum(
                dot_nt(d_qkv[j, :, 512 * half : 512 * half + 512], w[half, rows, 512 * j : 512 * j + 512])
                for half in (0, 1)
                for j in (0, 1, 2)
            )

        each(2, lambda i: (narrow_in(2 * i), narrow_in(2 * i + 1)))
        return low(res[...] + acc[...])

    other_half = columns((1 - c) * 2048, 2048)
    other_heads = columns((1 - c) * 512, 512)

    def swap(name, src, dst):
        given[name] = send(src, dst, sibling)

    def have(*names):
        for name in names:
            given[name].wait_recv()

    def block(start, left, right, s_left, s_right):
        whole = low(dot_tn(jnp.concatenate([left, s_left]), jnp.concatenate([right, s_right])))
        for chip in range(16):
            for h in (0, 1):
                f, g = (chip // 4, chip % 4) if h == 0 else (chip % 4, chip // 4)
                to, of = h * 512 + f * 128 + g * 32, chip * 64 + h * 32
                w[0, to : to + 32, columns(start, right.shape[1])] = whole[of : of + 32]

    def grads_down(first):
        def one(i):
            i = i + first
            at = columns(i * BLOCK, BLOCK)
            block(DOWN + i * BLOCK, d_low[...], act[:, columns(c * 2048 + i * BLOCK, BLOCK)], s_d_low[...], s_act[:, at])

        one(0)
        one(1)

    def grads_up(first):
        def one(i):
            i = i + first
            at = columns(i * BLOCK, BLOCK)
            block(UP + i * BLOCK, hid[...], d_act[:, columns(c * 2048 + i * BLOCK, BLOCK)], s_hid[...], s_d_act[:, at])

        one(0)
        one(1)

    def spread(row, size, offset):
        lanes = row.shape[1]
        wide = (32, lanes)
        owner = lax.broadcasted_iota(jnp.int32, wide, 0) == lax.div(
            lax.broadcasted_iota(jnp.int32, wide, 1), size
        )
        fold = lax.rem(lax.broadcasted_iota(jnp.int32, (lanes, 128), 0), size) == lax.broadcasted_iota(
            jnp.int32, (lanes, 128), 1
        )
        table = dot(low(jnp.where(owner, row, 0.0)), low(jnp.where(fold, 1.0, 0.0)))
        back = (128, 1024)
        lane = lax.broadcasted_iota(jnp.int32, back, 1)
        source = lax.broadcasted_iota(jnp.int32, back, 0)
        span = min(size, 32)
        place_in = lax.rem(lane, 32)
        if size == 16:
            open_ = (place_in == source + offset) & (source < span)
        else:
            open_ = (place_in + offset == source) & (source < size)
        rows = dot(low(table), low(jnp.where(open_, 1.0, 0.0)))
        mine = lax.broadcasted_iota(jnp.int32, (32, 1024), 0) == lax.div(
            lax.broadcasted_iota(jnp.int32, (32, 1024), 1), 32
        )
        return total(jnp.where(mine, rows, 0.0))

    def small_rows(half, dst):
        heads_at, units_at = columns(half * 512, 512), columns(half * 2048, 2048)
        dst[...] = jnp.zeros_like(dst)
        dst[0:2] = d_gains[...]
        dst[2:6] = d_shifts[...]
        dst[6:7] = spread(d_bqv[0:1, heads_at], 16, 0) + spread(d_bqv[1:2, heads_at], 16, 16)
        dst[7:8] = spread(d_bff[:, units_at], 64, 0)
        dst[8:9] = spread(d_bff[:, units_at], 64, 32)

    def grads_qkv():
        for j in (0, 1, 2):
            block(j * 512, x_in[...], d_qkv[j, :, columns(c * 512, 512)], s_x[...], s_d_qkv[j])

    def grads_rest():
        block(1536, a_low[...], o[:, columns(c * 512, 512)], s_a_low[...], s_o[...])
        summed = small[0] + s_small[...]
        column = low(jnp.concatenate([summed, jnp.zeros((112, 1024), jnp.float32)], axis=0).T)
        for chip in range(16):
            for h in (0, 1):
                f, g = (chip // 4, chip % 4) if h == 0 else (chip % 4, chip // 4)
                to, of = h * 512 + f * 128 + g * 32, chip * 64 + h * 32
                w[0, to : to + 32, EXTRA:UP] = column[of : of + 32]

    sent = {}

    def side(h, phase):
        return x if (h == 0) == (phase == 1) else y

    def rows_at(h, step):
        return pl.ds(pl.multiple_of(h * 512 + lax.rem(side(h, 1) + step, 4) * 128, 128), 128)

    def line_at(h, step):
        start = h * 512 + side(h, 1) * 128 + lax.rem(side(h, 2) + step, 4) * 32
        return pl.ds(pl.multiple_of(start, 32), 32)

    def parts(n):
        start, size, half = PASSES[n]
        return pl.ds(start, size), pl.ds(start, half), pl.ds(start + half, size - half)

    def add(dst, *others):
        def one(i):
            at = pl.ds(pl.multiple_of(i * 16, 16), 16)
            dst[at] = low(sum((high(o[at]) for o in others), high(dst[at])))

        each(dst.shape[0] // 16, one)

    def far(n):
        whole, part_a, part_b = parts(n)
        for h in (0, 1):
            rows = rows_at(h, 2)
            sent[n, h, "far"] = (
                send(w.at[0, rows, part_a], passing.at[h, :, part_a], beside(h, 1, 1, x, y, c)),
                send(w.at[0, rows, part_b], passing.at[h, :, part_b], beside(h, 1, 3, x, y, c)),
            )

    def near(n):
        whole, part_a, part_b = parts(n)
        for h in (0, 1):
            up, down = sent[n, h, "far"]
            up.wait_recv()
            add(w.at[0, rows_at(h, 1), part_a], passing.at[h, :, part_a])
            one = send(w.at[0, rows_at(h, 1), whole], near_p.at[h, :, whole], beside(h, 1, 1, x, y, c))
            down.wait_recv()
            add(w.at[0, rows_at(h, 3), part_b], passing.at[h, :, part_b])
            two = send(w.at[0, rows_at(h, 3), whole], near_m.at[h, :, whole], beside(h, 1, 3, x, y, c))
            sent[n, h, "near"] = (one, two)

    def q_far(n):
        whole, part_a, part_b = parts(n)
        for h in (0, 1):
            for copy in sent[n, h, "near"]:
                copy.wait_recv()
            add(w.at[0, rows_at(h, 0), whole], near_p.at[h, :, whole], near_m.at[h, :, whole])
            rows = line_at(h, 2)
            sent[n, h, "q_far"] = (
                send(w.at[0, rows, part_a], q_passing.at[h, :, part_a], beside(h, 2, 1, x, y, c)),
                send(w.at[0, rows, part_b], q_passing.at[h, :, part_b], beside(h, 2, 3, x, y, c)),
            )

    def q_near(n):
        whole, part_a, part_b = parts(n)
        for h in (0, 1):
            up, down = sent[n, h, "q_far"]
            up.wait_recv()
            add(w.at[0, line_at(h, 1), part_a], q_passing.at[h, :, part_a])
            one = send(w.at[0, line_at(h, 1), whole], q_p.at[h, :, whole], beside(h, 2, 1, x, y, c))
            down.wait_recv()
            add(w.at[0, line_at(h, 3), part_b], q_passing.at[h, :, part_b])
            two = send(w.at[0, line_at(h, 3), whole], q_m.at[h, :, whole], beside(h, 2, 3, x, y, c))
            sent[n, h, "q_near"] = (one, two)

    crossing, handing = {}, {}
    owner, sender = c == t, c != t

    def remote(i, src, dst, where):
        return pltpu.make_async_remote_copy(
            src_ref=src,
            dst_ref=dst,
            send_sem=send_sems.at[N_EACH + i],
            recv_sem=recv_sems.at[N_EACH + i],
            device_id=where,
            device_id_type=MESH,
        )

    def cross(n):
        whole, _, _ = parts(n)
        for h in (0, 1):
            for copy in sent[n, h, "q_near"]:
                copy.wait_recv()
            add(w.at[0, line_at(h, 0), whole], q_p.at[h, :, whole], q_m.at[h, :, whole])
            crossing[n, h] = remote(
                2 * n + h, w.at[0, line_at(h, 0), whole], mate.at[h, :, whole], {"tensor": 1 - t}
            )

            @pl.when(sender)
            def _():
                crossing[n, h].start()

    def hand(n):
        whole, _, _ = parts(n)
        handing[n] = remote(12 + n, to_mate.at[:, whole], out.at[:, whole], sibling)

        @pl.when(owner)
        def _():
            for h in (0, 1):
                crossing[n, h].wait_recv()
                value = high(w[0, line_at(h, 0), whole]) + high(mate[h, :, whole])

                @pl.when(c == h)
                def _():
                    out[:, whole] = value

                @pl.when(c != h)
                def _():
                    to_mate[:, whole] = value

            handing[n].start()

    def exchange(n):
        copy = send(
            kept.at[n], relay.at[n], {"section": 1 - s, "dp": dp_at(x, y, t), "tensor": c}
        )
        copy.wait_recv()
        return relay[n]

    def last_stage(stage):
        if stage == "d_low":
            swap("d_low", d_low, s_d_low)
        if stage == "d_act":
            swap("d_act", d_act.at[:, other_half], s_d_act)
            have("act", "d_low")
            grads_down(0)
            far(0)
            grads_down(2)
            far(1)
        if stage == "a_low":
            swap("a_low", a_low, s_a_low)
            near(0)
            have("hid", "d_act")
            grads_up(0)
            far(2)
            near(1)
            grads_up(2)
            far(3)
            near(2)
        if stage == "d_qkv":
            swap("d_qkv", d_qkv.at[:, :, other_heads], s_d_qkv)
            small_rows(1 - c, small.at[1])
            swap("small", small.at[1], s_small)
            small_rows(c, small.at[0])
            q_far(0)
            near(3)
            q_far(1)

    def first_stage(stage):
        if stage == "qkv":
            second_on(1, 0)
            second_send(2, 0)
            first_on(2, 1)
        if stage == "heads":
            second_on(1, 1)
            second_send(2, 1)
        if stage == "hid":
            second_end(1, 0)
            second_end(1, 1)
            second_on(2, 0)
            complete(1)
        if stage == "act":
            second_on(2, 1)
            second_end(2, 0)
            second_end(2, 1)
            complete(2)

    lent = (
        remote(18, ends.at[1 - t], x_in, sibling),
        remote(19, spans.at[1 - t], span_in, sibling),
    )

    @pl.when(owner)
    def _():
        for copy in lent:
            copy.start()

    shard_load.wait()
    z_sends = []
    for n, (start, size, _) in enumerate(GATHERS):
        part = own.at[:, :, pl.ds(start, size)]
        z_sends.append(share(part, part, {"tensor": 1 - t}))
        first_send(n, 0)
    first_on(0, 0)
    z_sends[0].wait_recv()
    first_send(0, 1)
    second_send(0, 0)
    first_on(0, 1)
    first_on(1, 0)
    second_send(0, 1)
    z_sends[1].wait_recv()
    first_send(1, 1)
    second_on(0, 0)
    second_send(1, 0)
    first_on(1, 1)
    second_on(0, 1)
    z_sends[2].wait_recv()
    first_on(2, 0)
    first_send(2, 1)
    second_send(1, 1)
    second_end(0, 0)
    second_end(0, 1)
    complete(0)
    take_parameters()
    own_load.wait()
    span[...] = spans[t]

    @pl.when(sender)
    def _():
        for copy in lent:
            copy.wait_recv()
        x_own[...] = jnp.where(s == 1, x_in[...], x_own[...])
        span[...] = jnp.where(s == 1, span_in[...], span[...])

    kept[0] = forward(x_own, first_stage)
    share.finish()
    x_in[...] = jnp.where(s == 0, x_own[...], exchange(0))
    swap("x", x_in, s_x)
    result = forward(x_in)
    swap("hid", hid, s_hid)
    swap("act", act.at[:, other_half], s_act)
    swap("o", o.at[:, other_heads], s_o)
    kept[2] = result
    kept[1] = backward(high(x_own[...]))
    grad_out = jnp.where(s == 1, x_own[...], exchange(1))
    d_x = backward(high(grad_out), last_stage)
    kept[2] = jnp.where(s == 0, d_x, kept[2])
    slot = t + s * (c - t)
    done, moved = kept.at[2], (s == 1) & sender
    here = pltpu.make_async_copy(done, ends_out.at[slot], io_sems.at[1])
    beyond = remote(20, done, ends_out.at[slot], {"tensor": 1 - t})
    to_core = remote(21, done, ends_out.at[slot], sibling)
    to_cross = remote(22, done, ends_out.at[slot], {"dp": dp_at(x, y, 1 - c), "tensor": 1 - t})

    @pl.when(moved)
    def _():
        to_core.start()
        to_cross.start()

    @pl.when(jnp.logical_not(moved))
    def _():
        here.start()
        beyond.start()

    have("o", "a_low", "x", "d_qkv", "small")
    grads_qkv()
    far(4)
    q_far(2)
    q_near(0)
    grads_rest()
    far(5)
    near(4)
    q_near(1)
    q_far(3)
    cross(0)
    q_near(2)
    cross(1)
    near(5)
    q_near(3)
    hand(0)
    cross(2)
    hand(1)
    q_far(4)
    cross(3)
    q_far(5)
    hand(2)
    q_near(4)
    q_near(5)
    hand(3)
    cross(4)
    cross(5)
    hand(4)
    hand(5)
    for n in range(6):

        @pl.when(sender)
        def _():
            handing[n].wait_recv()
            for h in (0, 1):
                crossing[n, h].wait_send()

        @pl.when(owner)
        def _():
            handing[n].wait_send()

    @pl.when(moved)
    def _():
        to_core.wait_send()
        to_cross.wait()
        beyond.wait_recv()

    @pl.when(jnp.logical_not(moved))
    def _():
        here.wait()
        beyond.wait_send()

    @pl.when(s == 0)
    def _():
        beyond.wait_recv()

    @pl.when((s == 1) & owner)
    def _():
        to_core.wait_recv()

    @pl.when(owner)
    def _():
        for copy in lent:
            copy.wait_send()

    send.finish()


def run_layers(spans, ends, shard):
    vmem = pltpu.VMEM
    bf, f32 = jnp.bfloat16, jnp.float32
    hbm = pl.BlockSpec(memory_space=pl.ANY)
    near = pl.BlockSpec(memory_space=vmem)
    sem = pltpu.SemaphoreType.DMA
    shape = jax.ShapeDtypeStruct
    return pl.pallas_call(
        layers_kernel,
        out_shape=(
            shape((2, ROWS, 1024), bf),
            shape((32, COLS), f32),
        ),
        in_specs=[near, hbm, hbm],
        out_specs=(hbm, near),
        scratch_shapes=[
            vmem((2, 1024), f32),
            vmem((4, 1024), f32),
            vmem((2, 1024), f32),
            vmem((1, 4096), f32),
            vmem((2, 1024), f32),
            vmem((4, 1024), f32),
            vmem((2, 1024), f32),
            vmem((1, 4096), f32),
            vmem((2, 4, 4, 2, 2, 16, COLS), bf),
            vmem((ROWS, 1024), bf),
            vmem((ROWS, 1024), bf),
            vmem((2, ROWS, 1024), bf),
            vmem((ROWS, 1024), bf),
            vmem((ROWS, 1024), bf),
            vmem((ROWS, 1024), bf),
            vmem((ROWS, 1024), bf),
            vmem((16, ROWS, ROWS), bf),
            vmem((ROWS, 1024), f32),
            vmem((ROWS, 1024), f32),
            vmem((ROWS, 1), f32),
            vmem((ROWS, 1), f32),
            vmem((ROWS, 1024), f32),
            vmem((ROWS, 1024), bf),
            vmem((ROWS, 4096), bf),
            vmem((ROWS, 4096), bf),
            vmem((ROWS, 4096), bf),
            vmem((3, ROWS, 1024), bf),
            vmem((ROWS, 1024), f32),
            vmem((ROWS, 1024), bf),
            vmem((ROWS, 1024), bf),
            vmem((3, ROWS, 1024), bf),
            vmem((2, 16, 1024), f32),
            vmem((ROWS, 1024), bf),
            vmem((ROWS, 1024), bf),
            vmem((ROWS, 1024), bf),
            vmem((ROWS, 1024), bf),
            vmem((ROWS, 2048), bf),
            vmem((ROWS, 2048), bf),
            vmem((ROWS, 512), bf),
            vmem((3, ROWS, 512), bf),
            vmem((16, 1024), f32),
            vmem((2, 128, COLS), bf),
            vmem((2, 128, COLS), bf),
            vmem((2, 128, COLS), bf),
            vmem((2, 32, COLS), bf),
            vmem((2, 32, COLS), bf),
            vmem((2, 32, COLS), bf),
            vmem((2, 32, COLS), bf),
            vmem((32, COLS), f32),
            vmem((8, 128), f32),
            vmem((8, 128), f32),
            sem((2,)),
            sem((N_EACH + 23,)),
            sem((N_EACH + 23,)),
            sem((N_GATHER,)),
            sem((N_GATHER,)),
        ],
        compiler_params=pltpu.CompilerParams(
            collective_id=0, has_side_effects=True, vmem_limit_bytes=62 * 2**20
        ),
        name="run_layers",
    )(spans, ends, shard)


def pack_kernel(w_qkv, w_out, w_up, w_down, gains, shifts, b_qv, b_ff, shard, small):
    for j in (0, 1, 2):
        shard[:, j * 512 : j * 512 + 512] = w_qkv[0, j]
    shard[:, 1536:EXTRA] = w_out[0]
    shard[:, UP:DOWN] = w_up[0]
    shard[:, DOWN:COLS] = w_down[0]
    small[...] = jnp.zeros_like(small)
    small[0:2, 0:32] = high(gains[0])
    small[2:6, 0:32] = high(shifts[0])
    small[6:7, 0:32] = jnp.concatenate([high(b_qv[0, 0, 0:1]), high(b_qv[0, 0, 1:2])], axis=1)
    small[7:8, 0:32] = high(b_ff[0, :, 0:32])
    small[8:9, 0:32] = high(b_ff[0, :, 32:64])
    shard[:, EXTRA:UP] = low(small[...].T[0:32])


def pack_shard(w_qkv, w_out, w_up, w_down, gains, shifts, b_qv, b_ff):
    return pl.pallas_call(
        pack_kernel,
        out_shape=jax.ShapeDtypeStruct((32, COLS), jnp.bfloat16),
        scratch_shapes=[pltpu.VMEM((128, 128), jnp.float32)],
        name="pack_shard",
    )(
        w_qkv.transpose(0, 2, 1, 3),
        w_out.transpose(0, 2, 1),
        w_up,
        w_down.transpose(0, 2, 1),
        gains,
        shifts,
        b_qv.transpose(0, 2, 1, 3),
        b_ff,
    )


def unpack_kernel(got, w_qkv, w_out, w_up, w_down, gains, shifts, b_qv, b_ff):
    for j in (0, 1, 2):
        w_qkv[0, j] = got[:, j * 512 : j * 512 + 512]
    w_out[0] = got[:, 1536:EXTRA]
    w_up[0] = got[:, UP:DOWN]
    w_down[0] = got[:, DOWN:COLS]
    rows = got[:, EXTRA:UP].T
    gains[0] = rows[0:2]
    shifts[0] = rows[2:6]
    b_qv[0, 0, 0:1] = rows[6:7, 0:16]
    b_qv[0, 0, 1:2] = rows[6:7, 16:32]
    b_ff[0] = jnp.concatenate([rows[7:8], rows[8:9]], axis=1)


def unpack_shard(got):
    shapes = ((1, 3, 32, 512), (1, 32, 512), (1, 32, 2048), (1, 32, 2048), (1, 2, 32), (1, 4, 32))
    shapes = shapes + ((1, 1, 2, 16), (1, 1, 64))
    w_qkv, w_out, w_up, w_down, gains, shifts, b_qv, b_ff = pl.pallas_call(
        unpack_kernel,
        out_shape=tuple(jax.ShapeDtypeStruct(shape, jnp.float32) for shape in shapes),
        name="unpack_shard",
    )(got)
    return (
        w_qkv.transpose(0, 2, 1, 3),
        w_out.transpose(0, 2, 1),
        w_up,
        w_down.transpose(0, 2, 1),
        gains,
        shifts,
        b_qv.transpose(0, 2, 1, 3),
        b_ff,
    )


def body(ends, lengths, *weights):
    shard = pack_shard(*weights)
    spans = jnp.broadcast_to(lengths[:, :, None].astype(jnp.float32), (2, 8, 128))
    ends_out, got = run_layers(spans, ends.reshape(2, ROWS, 1024), shard.reshape(2, 16, COLS))
    return (ends_out.reshape(1, 2, 1, ROWS, 1024),) + unpack_shard(got)


def solution(mesh):
    in_specs = (
        P("section", None, "dp", None, None),
        P(None, "dp"),
        P("section", "dp", None, "tensor"),
        P("section", "tensor", "dp"),
        P("section", "dp", "tensor"),
        P("section", "tensor", "dp"),
        P("section", None, "dp"),
        P("section", None, "dp"),
        P("section", None, "tensor", "dp"),
        P("section", "tensor", "dp"),
    )
    out_specs = (
        P("section", None, "dp", None, None),
        P("section", "dp", None, "tensor"),
        P("section", "tensor", "dp"),
        P("section", "dp", "tensor"),
        P("section", "tensor", "dp"),
        P("section", None, "dp"),
        P("section", None, "dp"),
        P("section", None, "tensor", "dp"),
        P("section", "tensor", "dp"),
    )
    return jax.shard_map(body, mesh=mesh, in_specs=in_specs, out_specs=out_specs, check_vma=False)
```
